32 devices in a mesh: img: 4 (over y, core), row: 2 (over x), col: 4 (over z).
Axes of the slice: x: 2, y: 2, z: 4, core: 2. Of those that a mesh axis runs over, the one named last changes fastest.
Arguments:
- image_tokens: bfloat16 [4, 64, 64, 768], P('img', 'row', 'col'), may hold values from -6 to 6
- cotangent: bfloat16 [4, 64, 64, 768], P('img', 'row', 'col'), may hold values from -6 to 6
- content_mask: int32 [4, 64, 64], P('img'), may hold values from 0 to 1, as said below
- norm1_gain: bfloat16 [768], P(('img', 'row', 'col')), may hold values from 0.25 to 1.75
- norm1_bias: bfloat16 [768], P(('img', 'row', 'col')), may hold values from -1.5 to 1.5
- qkv_weight: bfloat16 [768, 2304], P(('img', 'row', 'col')), may hold values from -0.21875 to 0.21875
- query_bias: bfloat16 [768], P(('img', 'row', 'col')), may hold values from -1.5 to 1.5
- value_bias: bfloat16 [768], P(('img', 'row', 'col')), may hold values from -1.5 to 1.5
- rel_rows: bfloat16 [27, 64], replicated, may hold values from -0.8984375 to 0.8984375
- rel_cols: bfloat16 [27, 64], replicated, may hold values from -0.8984375 to 0.8984375
- proj_weight: bfloat16 [768, 768], P(('img', 'row', 'col')), may hold values from -0.875 to 0.875
- proj_bias: bfloat16 [768], P(('img', 'row', 'col')), may hold values from -1.5 to 1.5
- norm2_gain: bfloat16 [768], P(('img', 'row', 'col')), may hold values from 0.25 to 1.75
- norm2_bias: bfloat16 [768], P(('img', 'row', 'col')), may hold values from -1.5 to 1.5
- fc1_weight: bfloat16 [768, 3072], P(('img', 'row', 'col')), may hold values from -0.21875 to 0.21875
- fc1_bias: bfloat16 [3072], P(('img', 'row', 'col')), may hold values from -1.5 to 1.5
- fc2_weight: bfloat16 [3072, 768], P(('img', 'row', 'col')), may hold values from -0.15625 to 0.15625
- fc2_bias: bfloat16 [768], P(('img', 'row', 'col')), may hold values from -1.5 to 1.5
Outputs:
- layer_out: bfloat16 [4, 64, 64, 768], P('img', 'row', 'col')
- grad_tokens: bfloat16 [4, 64, 64, 768], P('img', 'row', 'col')
- grad_norm1_gain: float32 [768], P(('img', 'row', 'col'))
- grad_norm1_bias: float32 [768], P(('img', 'row', 'col'))
- grad_qkv_weight: float32 [768, 2304], P(('img', 'row', 'col'))
- grad_query_bias: float32 [768], P(('img', 'row', 'col'))
- grad_value_bias: float32 [768], P(('img', 'row', 'col'))
- grad_rel_rows: float32 [27, 64], replicated
- grad_rel_cols: float32 [27, 64], replicated
- grad_proj_weight: float32 [768, 768], P(('img', 'row', 'col'))
- grad_proj_bias: float32 [768], P(('img', 'row', 'col'))
- grad_norm2_gain: float32 [768], P(('img', 'row', 'col'))
- grad_norm2_bias: float32 [768], P(('img', 'row', 'col'))
- grad_fc1_weight: float32 [768, 3072], P(('img', 'row', 'col'))
- grad_fc1_bias: float32 [3072], P(('img', 'row', 'col'))
- grad_fc2_weight: float32 [3072, 768], P(('img', 'row', 'col'))
- grad_fc2_bias: float32 [768], P(('img', 'row', 'col'))
The draws below stay inside these ranges and needn't reach their ends.
Inputs may be any that keep to these rules, and one draw needn't show every extreme that they name: `content_mask`: each image's mask is 0 exactly on the cells whose row is at least its own bound tall and whose column is at least its own bound wide, and 1 elsewhere; tall and wide each lie between 57 and 64, so the first row and the first column are 1 throughout and the 0 cells may be none.
All inputs are finite; a program needn't handle non-finite values.
Results may differ from the reference program's by a relative error of at most 0.02.
Values may be sent and summed in bfloat16 or wider, within the bound.
A program may use at most 832 MiB of HBM per device.

```python
import jax
import jax.numpy as jnp
import numpy as np
from jax import lax

D = 768
HEADS = 12
HEAD_DIM = 64
FF = 3072
WIN = 14
GRID = 64
PADDED = 70
IMAGES = 4


def draw_content_mask(key, part):
    extents = jax.random.randint(jax.random.fold_in(key, 11), (IMAGES, 2), PADDED - WIN + 1, GRID + 1)
    positions = jnp.arange(GRID)
    below = positions[None, :, None] >= extents[:, 0][:, None, None]
    beside = positions[None, None, :] >= extents[:, 1][:, None, None]
    return 1 - (below & beside).astype(jnp.int32)


def block_levels(own_key, dims, shards, low, largest):
    gain = 1.0
    for position, blocks in shards:
        draws = jax.random.uniform(jax.random.fold_in(jax.random.fold_in(own_key, 6), position), (blocks,), jnp.float32, low / len(shards), largest / len(shards))
        gain = gain * jnp.repeat(jnp.exp(draws), dims[position] // blocks).reshape((-1,) + (1,) * (len(dims) - 1 - position))
    return gain


def gaussian(stream_key, extent, width, limit, split=(), kind=jnp.bfloat16):
    drawn = width * jax.random.normal(stream_key, extent, jnp.float32)
    if split:
        drawn = drawn * block_levels(stream_key, extent, split, -0.22, 0.18)
    return jnp.clip(drawn, -limit, limit).astype(kind)


def setup_inputs(seed: int = 0) -> dict:
    key_list = jax.random.split(jax.random.key(seed), 19)
    return {
        "image_tokens": gaussian(key_list[0], (IMAGES, GRID, GRID, D), 1.0, 6.0, ((0, 4), (1, 2), (2, 4))),
        "cotangent": gaussian(key_list[1], (IMAGES, GRID, GRID, D), 1.0, 6.0, ((0, 4), (1, 2), (2, 4))),
        "content_mask": draw_content_mask(jax.random.fold_in(key_list[18], 71), 0),
        "norm1_gain": jnp.clip(1.0 + 0.15 * jax.random.normal(key_list[3], (D,), jnp.float32), 0.25, 1.75).astype(jnp.bfloat16),
        "norm1_bias": gaussian(key_list[4], (D,), 0.3, 1.5, ((0, 32),)),
        "qkv_weight": gaussian(key_list[5], (D, 3 * D), D ** -0.5, 0.21875, ((0, 32),)),
        "query_bias": gaussian(key_list[6], (D,), 0.3, 1.5, ((0, 32),)),
        "value_bias": gaussian(key_list[7], (D,), 0.3, 1.5, ((0, 32),)),
        "rel_rows": gaussian(key_list[8], (2 * WIN - 1, HEAD_DIM), 0.15, 0.8984375),
        "rel_cols": gaussian(key_list[9], (2 * WIN - 1, HEAD_DIM), 0.15, 0.8984375),
        "proj_weight": gaussian(key_list[10], (D, D), (D // 16) ** -0.5, 0.875, ((0, 32),)),
        "proj_bias": gaussian(key_list[11], (D,), 0.3, 1.5, ((0, 32),)),
        "norm2_gain": jnp.clip(1.0 + 0.15 * jax.random.normal(key_list[12], (D,), jnp.float32), 0.25, 1.75).astype(jnp.bfloat16),
        "norm2_bias": gaussian(key_list[13], (D,), 0.3, 1.5, ((0, 32),)),
        "fc1_weight": gaussian(key_list[14], (D, FF), D ** -0.5, 0.21875, ((0, 32),)),
        "fc1_bias": gaussian(key_list[15], (FF,), 0.3, 1.5, ((0, 32),)),
        "fc2_weight": gaussian(key_list[16], (FF, D), (FF // 2) ** -0.5, 0.15625, ((0, 32),)),
        "fc2_bias": gaussian(key_list[17], (D,), 0.3, 1.5, ((0, 32),)),
    }


@jax.custom_vjp
def low(v):
    return lax.optimization_barrier(v.astype(jnp.bfloat16)).astype(jnp.float32)

@jax.custom_vjp
def low_back(v):
    return v

def low_keep(v):
    return (low(v), None)

def low_pass(kept, grad):
    return (grad,)

def back_keep(v):
    return (v, None)

def back_low(kept, grad):
    return (low(grad),)
low.defvjp(low_keep, low_pass)
low_back.defvjp(back_keep, back_low)
precise = lax.Precision.HIGHEST

def layer_norm(values, norm_gain, norm_shift):
    center = lax.optimization_barrier(jnp.mean(values, axis=-1, keepdims=True))
    offset = values - center
    spread = lax.optimization_barrier(jnp.mean(offset * offset, axis=-1, keepdims=True))
    return offset * lax.rsqrt(spread + 1e-06) * norm_gain + norm_shift

def to_windows(source):
    across = PADDED // WIN
    grid_cells = source.reshape(GRID, GRID, -1)
    framed = jnp.pad(grid_cells, ((0, PADDED - GRID), (0, PADDED - GRID), (0, 0)))
    window_tiles = framed.reshape(across, WIN, across, WIN, -1).transpose(0, 2, 1, 3, 4)
    return window_tiles.reshape(across * across, WIN * WIN, -1)

def from_windows(window_tiles):
    across = PADDED // WIN
    grid_cells = window_tiles.reshape(across, across, WIN, WIN, -1).transpose(0, 2, 1, 3, 4)
    return grid_cells.reshape(PADDED, PADDED, -1)[:GRID, :GRID].reshape(GRID * GRID, -1)

def window_attention(queries, keys_in, values_in, key_valid, rel_rows_table, rel_cols_table):
    rel_index = np.arange(WIN)[:, None] - np.arange(WIN)[None, :] + WIN - 1
    rows_win = rel_rows_table[rel_index]
    cols_win = rel_cols_table[rel_index]
    q_win = to_windows(queries).reshape(-1, WIN, WIN, HEADS, HEAD_DIM)
    k_win = to_windows(keys_in).reshape(-1, WIN, WIN, HEADS, HEAD_DIM)
    v_win = to_windows(values_in).reshape(-1, WIN * WIN, HEADS, HEAD_DIM)
    windows = q_win.shape[0]
    scores = jnp.einsum('nxyhc,nabhc->nhxyab', q_win, k_win, precision=precise) * HEAD_DIM ** (-0.5)
    along_rows = jnp.einsum('nxyhc,xac->nhxya', q_win, rows_win, precision=precise)
    along_cols = jnp.einsum('nxyhc,ybc->nhxyb', q_win, cols_win, precision=precise)
    scores = scores + along_rows[:, :, :, :, :, None] + along_cols[:, :, :, :, None, :]
    scores = low_back(scores.reshape(windows, HEADS, WIN * WIN, WIN * WIN))
    scores = jnp.where(key_valid[:, None, None, :], scores, -1e+30)
    row_peak = lax.optimization_barrier(jnp.max(scores, axis=-1, keepdims=True))
    exponent = jnp.exp(scores - row_peak)
    soft_weights = low(exponent / lax.optimization_barrier(jnp.sum(exponent, axis=-1, keepdims=True)))
    mixed_out = jnp.einsum('nhqk,nkhc->nqhc', soft_weights, v_win, precision=precise)
    return from_windows(mixed_out.reshape(windows, WIN * WIN, HEADS * HEAD_DIM))

def layer_forward(tokens_in, key_valid, params):
    norm1_gain, norm1_bias, qkv_weight, query_bias, value_bias, rel_rows, rel_cols, proj_weight, proj_bias, norm2_gain, norm2_bias, fc1_weight, fc1_bias, fc2_weight, fc2_bias = params
    normed = low(layer_norm(tokens_in, norm1_gain, norm1_bias))
    mixed_qkv = jnp.dot(normed, qkv_weight, precision=precise)
    queries = low(low_back(mixed_qkv[:, :D] + query_bias))
    keys_in = low(low_back(mixed_qkv[:, D:2 * D]))
    values_in = low(low_back(mixed_qkv[:, 2 * D:] + value_bias))
    attended = low(low_back(window_attention(queries, keys_in, values_in, key_valid, rel_rows, rel_cols)))
    residual = tokens_in + low_back(jnp.dot(attended, proj_weight, precision=precise) + proj_bias)
    normed_two = low(layer_norm(residual, norm2_gain, norm2_bias))
    hidden = low_back(jnp.dot(normed_two, fc1_weight, precision=precise) + fc1_bias)
    activated = low(jax.nn.gelu(hidden, approximate=False))
    return residual + low_back(jnp.dot(activated, fc2_weight, precision=precise) + fc2_bias)

def reference(image_tokens, cotangent, content_mask, norm1_gain, norm1_bias, qkv_weight, query_bias, value_bias, rel_rows, rel_cols, proj_weight, proj_bias, norm2_gain, norm2_bias, fc1_weight, fc1_bias, fc2_weight, fc2_bias):
    params = tuple((member.astype(jnp.float32) for member in (norm1_gain, norm1_bias, qkv_weight, query_bias, value_bias, rel_rows, rel_cols, proj_weight, proj_bias, norm2_gain, norm2_bias, fc1_weight, fc1_bias, fc2_weight, fc2_bias)))

    def per_image(totals, inputs):
        image, image_grad, image_mask = inputs
        framed = to_windows(image_mask.reshape(GRID * GRID, 1))
        key_valid = framed[:, :, 0] == 1

        def run_layer(tokens_in, weights_in):
            return layer_forward(tokens_in, key_valid, weights_in)
        result, pullback = jax.vjp(run_layer, image.astype(jnp.float32).reshape(GRID * GRID, D), params)
        grad_in, grad_params = pullback(image_grad.astype(jnp.float32).reshape(GRID * GRID, D))
        totals = jax.tree.map(jnp.add, totals, grad_params)
        return (totals, (result.astype(jnp.bfloat16).reshape(GRID, GRID, D), grad_in.astype(jnp.bfloat16).reshape(GRID, GRID, D)))
    zeros_init = tuple((jnp.zeros_like(member) for member in params))
    totals, (layer_out, grad_tokens) = lax.scan(per_image, zeros_init, (image_tokens, cotangent, content_mask))
    return (layer_out, grad_tokens, totals[0], totals[1], totals[2], totals[3], totals[4], totals[5], totals[6], totals[7], totals[8], totals[9], totals[10], totals[11], totals[12], totals[13], totals[14])
```

```python
import functools

import jax
import jax.numpy as jnp
import numpy as np
from jax import lax
from jax.experimental import pallas as pl
from jax.experimental.pallas import tpu as pltpu
from jax.sharding import PartitionSpec as P

D = 768
HEADS = 12
HEAD_DIM = 64
PAIRS = HEADS // 2
WIN = 14
CELLS = WIN * WIN
SLOT = 208
MESH = pl.DeviceIdType.MESH
F32 = jnp.float32
BF16 = jnp.bfloat16
VMEM_LIMIT = 60 * 2**20


def round_up(value, unit):
    return -(-value // unit) * unit


def plan_windows(rows, cols, tile_rows, tile_cols):
    devices = rows * cols
    height, width = rows * tile_rows, cols * tile_cols
    windows = []
    for top in range(0, height, WIN):
        for left in range(0, width, WIN):
            windows.append(
                [
                    (r, c, r - top, c - left)
                    for r in range(top, min(top + WIN, height))
                    for c in range(left, min(left + WIN, width))
                ]
            )
    bins = []
    for window in sorted(windows, key=len, reverse=True):
        for held in bins:
            if len(held) < 2 and sum(map(len, held)) + len(window) <= CELLS:
                held.append(window)
                break
        else:
            bins.append([window])
    slots = -(-len(bins) // devices)
    while len(bins) < slots * devices:
        bins.append([])

    def home(cell):
        return cell[0] // tile_rows * cols + cell[1] // tile_cols

    weights = np.zeros((len(bins), devices), np.int64)
    for number, held in enumerate(bins):
        for window in held:
            for cell in window:
                weights[number, home(cell)] += 1
    hops = np.zeros((devices, devices, rows * rows * cols + cols * cols * rows))
    for source in range(devices):
        for target in range(devices):
            r0, c0, r1, c1 = source // cols, source % cols, target // cols, target % cols
            step = 1 if r1 > r0 else -1
            for r in range(r0, r1, step):
                hops[source, target, (r * rows + r + step) * cols + c0] = 1
            step = 1 if c1 > c0 else -1
            for c in range(c0, c1, step):
                hops[source, target, rows * rows * cols + (c * cols + c + step) * rows + r1] = 1
    loads = np.einsum("bs,sdl->bdl", weights, hops)

    def cost(order):
        load = loads[np.arange(len(bins)), np.array(order) // slots].sum(axis=0)
        return load.max() * 100 + load.sum()

    order = [0] * len(bins)
    free = [slots] * devices
    for number in range(len(bins)):
        options = [d for d in range(devices) if free[d]]
        best = min(options, key=lambda d: (loads[number, d].sum(), d))
        order[number] = best * slots + slots - free[best]
        free[best] -= 1
    current = cost(order)
    while True:
        found = None
        for a in range(len(bins)):
            for b in range(a):
                if order[a] // slots != order[b] // slots:
                    order[a], order[b] = order[b], order[a]
                    trial = cost(order)
                    if trial < current:
                        current, found = trial, (a, b)
                    order[a], order[b] = order[b], order[a]
        if found is None:
            break
        a, b = found
        order[a], order[b] = order[b], order[a]
    total = slots * SLOT
    place = [[] for _ in range(devices)]
    for number in sorted(range(len(bins)), key=lambda n: order[n]):
        device, slot = order[number] // slots, order[number] % slots
        position = slot * SLOT
        for group, window in enumerate(bins[number]):
            for cell in window:
                place[device].append((position, cell, group))
                position += 1
    cells = tile_rows * tile_cols
    pairs = []
    sent, got = [0] * devices, [0] * devices
    moved = {}
    for source in range(devices):
        for target in range(devices):
            if source != target:
                listed = [e for e in place[target] if home(e[1]) == source]
                if listed:
                    count = round_up(len(listed), 16)
                    pairs.append((source, target, sent[source], got[target], count))
                    moved[source, target] = (listed, sent[source], got[target])
                    sent[source] += count
                    got[target] += count
    packed, landed = round_up(max(sent), 128), round_up(max(got), 128)
    pack_from = np.full((devices, packed), -1, np.int32)
    slot_from = np.full((devices, total), -1, np.int32)
    back_from = np.full((devices, landed), -1, np.int32)
    tile_from = np.full((devices, cells), -1, np.int32)
    where = np.full((devices, total, 8), -1, np.int32)
    for device in range(devices):
        for position, cell, group in place[device]:
            where[device, position, :5] = (cell[2], cell[3], group, cell[0], cell[1])
            if home(cell) == device:
                local = cell[0] % tile_rows * tile_cols + cell[1] % tile_cols
                slot_from[device, position] = local
                tile_from[device, local] = position
    for (source, target), (listed, out, into) in moved.items():
        for k, (position, cell, group) in enumerate(listed):
            local = cell[0] % tile_rows * tile_cols + cell[1] % tile_cols
            pack_from[source, out + k] = local
            slot_from[target, position] = cells + into + k
            back_from[target, into + k] = position
            tile_from[source, local] = total + out + k
    return dict(
        slots=slots, total=total, pairs=pairs, packed=packed, landed=landed, where=where,
        pack_from=pack_from, slot_from=slot_from, back_from=back_from, tile_from=tile_from,
    )


def matmul(a, b):
    return jnp.dot(a, b, preferred_element_type=F32)


def matmul_nt(a, b):
    return lax.dot_general(a, b, (((1,), (1,)), ((), ())), preferred_element_type=F32)


def matmul_tn(a, b):
    return lax.dot_general(a, b, (((0,), (0,)), ((), ())), preferred_element_type=F32)


def one_hot(index, width):
    return (index == lax.broadcasted_iota(jnp.int32, (index.shape[0], width), 1)).astype(BF16)


def normalized(values):
    offset = values - jnp.mean(values, axis=-1, keepdims=True)
    rate = lax.rsqrt(jnp.mean(offset * offset, axis=-1, keepdims=True) + 1e-06)
    return offset * rate, rate


def norm_back(cotangent, gain, hat, rate):
    e = cotangent * gain
    mean_e = jnp.mean(e, axis=-1, keepdims=True)
    mean_eh = jnp.mean(e * hat, axis=-1, keepdims=True)
    return rate * (e - mean_e - hat * mean_eh)


def column_sum(values):
    return jnp.sum(values, axis=0, keepdims=True)


def whole(shape):
    return pl.BlockSpec(shape, lambda *_: (0,) * len(shape))


def params(**more):
    return pltpu.CompilerParams(vmem_limit_bytes=VMEM_LIMIT, **more)


def qkv_kernel(x_ref, vec_ref, mask_ref, where_ref, w_ref, n1_ref, qkv_ref, key_ref):
    hat, _ = normalized(x_ref[...].astype(F32))
    n1_ref[...] = (hat * vec_ref[0:1, :] + vec_ref[1:2, :]).astype(BF16)
    for part in range(3):
        columns = pl.ds(part * D, D)
        out = matmul(n1_ref[...], w_ref[:, columns])
        if part == 0:
            out = out + vec_ref[2:3, :]
        if part == 2:
            out = out + vec_ref[3:4, :]
        qkv_ref[:, columns] = out.astype(BF16)
    place = where_ref[...]
    rows = matmul(one_hot(place[:, 3:4], mask_ref.shape[0]), mask_ref[...])
    lane = lax.broadcasted_iota(jnp.int32, rows.shape, 1)
    valid = jnp.sum(jnp.where(lane == place[:, 4:5], rows, 0.0), axis=1, keepdims=True)
    lane = lax.broadcasted_iota(jnp.int32, key_ref.shape, 1)
    hot = (lane == place[:, 0:1]) | ((lane == place[:, 1:2] + WIN) & (place[:, 1:2] >= 0))
    group = lane - 2 * WIN
    shut = ((group == 0) | (group == 1)) & ((valid < 0.5) | (place[:, 2:3] != group))
    key_ref[...] = jnp.where(shut, -1e30, jnp.where(hot, 1.0, 0.0)).astype(BF16)


def head_halves(pair):
    low = lax.broadcasted_iota(jnp.int32, pair.shape, 1) < HEAD_DIM
    zero = jnp.zeros_like(pair)
    return jnp.concatenate([jnp.where(low, pair, zero), jnp.where(low, zero, pair)], axis=0)


def join_halves(stacked):
    low = lax.broadcasted_iota(jnp.int32, (SLOT, 2 * HEAD_DIM), 1) < HEAD_DIM
    return jnp.where(low, stacked[:SLOT], stacked[SLOT:])


REL = 512


def own_place(where_ref):
    lane = lax.broadcasted_iota(jnp.int32, (SLOT, REL), 1)
    row, col = where_ref[:, 0:1], where_ref[:, 1:2]
    first, second = row * WIN, REL // 2 + col * WIN
    hot = (lane >= first) & (lane < first + WIN) & (row >= 0)
    hot = hot | ((lane >= second) & (lane < second + WIN) & (col >= 0))
    return jnp.where(hot, 1.0, 0.0).astype(BF16)


def attend_kernel(q_ref, k_ref, v_ref, key_ref, where_ref, rel_ref, fold_ref, o_ref, p_ref, own_ref):
    @pl.when(pl.program_id(1) == 0)
    def _():
        own_ref[...] = own_place(where_ref)

    qs = head_halves(q_ref[...])
    own = own_ref[...]
    own2 = jnp.concatenate([own, own], axis=0)
    spread = matmul(qs, rel_ref[...]).astype(BF16) * own2
    lane = lax.broadcasted_iota(jnp.int32, (SLOT, 128), 1)
    group = lane - 2 * WIN
    second = where_ref[:, 2:3] == 1
    mark = jnp.where(((group == 0) & ~second) | ((group == 1) & second), 1.0, 0.0)
    near = matmul(spread, fold_ref[...]) + jnp.concatenate([mark, mark], axis=0)
    left = jnp.concatenate([qs * BF16(0.125), near.astype(BF16)], axis=1)
    right = jnp.concatenate([k_ref[...], key_ref[...]], axis=1)
    scores = matmul_nt(left, right)
    weight = jnp.exp(scores - jnp.max(scores, axis=-1, keepdims=True))
    soft = (weight / jnp.sum(weight, axis=-1, keepdims=True)).astype(BF16)
    p_ref[...] = soft
    o_ref[...] = join_halves(matmul(soft, v_ref[...])).astype(BF16)


def attend_back_kernel(
    q_ref, k_ref, v_ref, o_ref, do_ref, p_ref, key_ref, where_ref, rel_ref, fold_ref,
    dq_ref, dk_ref, dv_ref, drel_ref, own_ref,
):
    @pl.when(pl.program_id(1) == 0)
    def _():
        own_ref[...] = own_place(where_ref)

    @pl.when((pl.program_id(0) == 0) & (pl.program_id(1) == 0))
    def _():
        drel_ref[...] = jnp.zeros_like(drel_ref)

    qs, dos = head_halves(q_ref[...]), head_halves(do_ref[...])
    o = o_ref[...].astype(F32)
    soft = p_ref[...]
    inner = jnp.sum(dos.astype(F32) * jnp.concatenate([o, o], axis=0), axis=-1, keepdims=True)
    ds = (soft.astype(F32) * (matmul_nt(dos, v_ref[...]) - inner)).astype(BF16)
    right = jnp.concatenate([k_ref[...], key_ref[...]], axis=1)
    back = matmul(ds, right)
    own = own_ref[...]
    own2 = jnp.concatenate([own, own], axis=0)
    spread = matmul_nt(back[:, 128:].astype(BF16), fold_ref[...]).astype(BF16) * own2
    dq = back[:, :128] * 0.125 + matmul_nt(spread, rel_ref[...])
    dq_ref[...] = join_halves(dq).astype(BF16)
    drel_ref[...] += matmul_tn(qs, spread)
    dk_ref[...] = (matmul_tn(ds, qs) * 0.125).astype(BF16)
    dv_ref[...] = matmul_tn(soft, dos).astype(BF16)


def rel_tables(rel_rows, rel_cols):
    index = np.arange(WIN)[:, None] - np.arange(WIN)[None, :] + WIN - 1
    select = np.zeros((2, 2 * WIN - 1, REL // 2), np.float32)
    select[:, index.reshape(-1), np.arange(CELLS)] = 1
    rel = jnp.concatenate(
        [
            jnp.einsum("mc,ml->cl", table, select[0].astype(BF16), preferred_element_type=F32)
            for table in (rel_rows, rel_cols)
        ],
        axis=1,
    ).astype(BF16)
    fold = np.zeros((REL, 128), np.float32)
    for first in range(WIN):
        for second in range(WIN):
            fold[first * WIN + second, second] = 1
            fold[REL // 2 + first * WIN + second, WIN + second] = 1
    return jnp.concatenate([rel, rel], axis=0), jnp.asarray(fold, BF16), select[0]


def proj_kernel(o_ref, x_ref, vec_ref, w_ref, r_ref, n2_ref):
    r = x_ref[...].astype(F32) + matmul(o_ref[...], w_ref[...]) + vec_ref[4:5, :]
    r_ref[...] = r
    hat, _ = normalized(r)
    n2_ref[...] = (hat * vec_ref[5:6, :] + vec_ref[6:7, :]).astype(BF16)


def mlp_kernel(n2_ref, g_ref, r_ref, vec_ref, b1_ref, w1_ref, w2_ref, out_ref, dn2_ref, dw1_ref, dw2_ref, db1_ref, acc_ref):
    step = pl.program_id(0)

    @pl.when(step == 0)
    def _():
        acc_ref[...] = r_ref[...] + vec_ref[7:8, :]
        dn2_ref[...] = jnp.zeros_like(dn2_ref)

    n2, g = n2_ref[...], g_ref[...]
    w1, w2 = w1_ref[...], w2_ref[...]
    u = matmul(n2, w1) + b1_ref[...]
    half = 0.5 + 0.5 * lax.erf(u * 0.7071067811865476)
    slope = half + u * jnp.exp(u * u * -0.5) * 0.3989422804014327
    a = (u * half).astype(BF16)
    acc_ref[...] += matmul(a, w2)
    dw2_ref[...] = matmul_tn(a, g).astype(BF16)
    du = matmul_nt(g, w2) * slope
    du = du.astype(BF16)
    db1_ref[...] = column_sum(du.astype(F32))
    dw1_ref[...] = matmul_tn(n2, du).astype(BF16)
    dn2_ref[...] += matmul_nt(du, w1)

    @pl.when(step == pl.num_programs(0) - 1)
    def _():
        out_ref[...] = acc_ref[...].astype(BF16)


def proj_back_kernel(dn2_ref, r_ref, g_ref, o_ref, vec_ref, w_ref, dr_ref, do_ref, dw_ref, sums_ref):
    hat, rate = normalized(r_ref[...])
    dn2, g = dn2_ref[...], g_ref[...].astype(F32)
    sums_ref[0:1, :] = column_sum(dn2 * hat)
    sums_ref[1:2, :] = column_sum(dn2)
    sums_ref[2:3, :] = column_sum(g)
    dr = g + norm_back(dn2, vec_ref[5:6, :], hat, rate)
    dr_ref[...] = dr
    db = dr.astype(BF16)
    sums_ref[3:4, :] = column_sum(db.astype(F32))
    dw_ref[...] = matmul_tn(o_ref[...], db).astype(BF16)
    do_ref[...] = matmul_nt(db, w_ref[...]).astype(BF16)


def qkv_back_kernel(dq_ref, dk_ref, dv_ref, n1_ref, x_ref, dr_ref, vec_ref, w_ref, gx_ref, dw_ref, sums_ref):
    hat, rate = normalized(x_ref[...].astype(F32))
    dn1 = None
    for part, ref in enumerate((dq_ref, dk_ref, dv_ref)):
        columns = pl.ds(part * D, D)
        term = matmul_nt(ref[...], w_ref[:, columns])
        dn1 = term if dn1 is None else dn1 + term
        dw_ref[:, columns] = matmul_tn(n1_ref[...], ref[...]).astype(BF16)
    sums_ref[0:1, :] = column_sum(dn1 * hat)
    sums_ref[1:2, :] = column_sum(dn1)
    sums_ref[2:3, :] = column_sum(dq_ref[...].astype(F32))
    sums_ref[3:4, :] = column_sum(dv_ref[...].astype(F32))
    gx_ref[...] = (dr_ref[...] + norm_back(dn1, vec_ref[0:1, :], hat, rate)).astype(BF16)


def call(kernel, out_shapes, *operands, **more):
    return pl.pallas_call(
        kernel,
        out_shape=[jax.ShapeDtypeStruct(shape, kind) for shape, kind in out_shapes],
        compiler_params=params(),
        **more,
    )(*operands)


def compute(plan, xs, gs, mask, where, rel_rows, rel_cols, vec, b1, w_qkv, w_proj, w_fc1, w_fc2):
    total, slots = plan["total"], plan["slots"]
    ff = w_fc1.shape[1]
    rel, fold, select = rel_tables(rel_rows, rel_cols)
    n1, qkv, key = call(
        qkv_kernel,
        [((total, D), BF16), ((total, 3 * D), BF16), ((total, 128), BF16)],
        xs, vec, mask, where, w_qkv,
    )

    def slab(offset):
        return pl.BlockSpec((SLOT, 128), lambda s, p: (s, offset + p))

    per_slot = pl.BlockSpec((SLOT, 128), lambda s, p: (s, 0))
    place = pl.BlockSpec((SLOT, 8), lambda s, p: (s, 0))
    soft_spec = pl.BlockSpec((None, None, 2 * SLOT, SLOT), lambda s, p: (s, p, 0, 0))
    o, soft = call(
        attend_kernel,
        [((total, D), BF16), ((slots, PAIRS, 2 * SLOT, SLOT), BF16)],
        qkv, qkv, qkv, key, where, rel, fold,
        grid=(slots, PAIRS),
        in_specs=[slab(0), slab(PAIRS), slab(2 * PAIRS), per_slot, place, whole(rel.shape), whole(fold.shape)],
        out_specs=[slab(0), soft_spec],
        scratch_shapes=[pltpu.VMEM((SLOT, REL), BF16)],
    )
    r, n2 = call(proj_kernel, [((total, D), F32), ((total, D), BF16)], o, xs, vec, w_proj)
    block = 512
    steps = ff // block
    out, dn2, dw_fc1, dw_fc2, db1 = call(
        mlp_kernel,
        [((total, D), BF16), ((total, D), F32), ((D, ff), BF16), ((ff, D), BF16), ((1, ff), F32)],
        n2, gs, r, vec, b1, w_fc1, w_fc2,
        grid=(steps,),
        in_specs=[
            whole((total, D)), whole((total, D)), whole((total, D)), whole(vec.shape),
            pl.BlockSpec((1, block), lambda f: (0, f)),
            pl.BlockSpec((D, block), lambda f: (0, f)),
            pl.BlockSpec((block, D), lambda f: (f, 0)),
        ],
        out_specs=[
            whole((total, D)), whole((total, D)),
            pl.BlockSpec((D, block), lambda f: (0, f)),
            pl.BlockSpec((block, D), lambda f: (f, 0)),
            pl.BlockSpec((1, block), lambda f: (0, f)),
        ],
        scratch_shapes=[pltpu.VMEM((total, D), F32)],
    )
    dr, do, dw_proj, sums2 = call(
        proj_back_kernel,
        [((total, D), F32), ((total, D), BF16), ((D, D), BF16), ((8, D), F32)],
        dn2, r, gs, o, vec, w_proj,
    )
    dq, dk, dv, drel = call(
        attend_back_kernel,
        [((total, D), BF16)] * 3 + [((128, REL), F32)],
        qkv, qkv, qkv, o, do, soft, key, where, rel, fold,
        grid=(slots, PAIRS),
        in_specs=[
            slab(0), slab(PAIRS), slab(2 * PAIRS), slab(0), slab(0), soft_spec,
            per_slot, place, whole(rel.shape), whole(fold.shape),
        ],
        out_specs=[slab(0), slab(0), slab(0), whole((128, REL))],
        scratch_shapes=[pltpu.VMEM((SLOT, REL), BF16)],
    )
    gx, dw_qkv, sums1 = call(
        qkv_back_kernel,
        [((total, D), BF16), ((D, 3 * D), BF16), ((8, D), F32)],
        dq, dk, dv, n1, xs, dr, vec, w_qkv,
    )
    drel = drel[:HEAD_DIM] + drel[HEAD_DIM:]
    half = REL // 2
    drel_rows = jnp.einsum("ml,cl->mc", select, drel[:, :half], precision=lax.Precision.HIGHEST)
    drel_cols = jnp.einsum("ml,cl->mc", select, drel[:, half:], precision=lax.Precision.HIGHEST)
    sums = [sums1[0], sums1[1], sums1[2], sums1[3], sums2[3], sums2[0], sums2[1], sums2[2]]
    return out, gx, dw_qkv, dw_proj, dw_fc1, dw_fc2, jnp.stack(sums), db1, drel_rows, drel_cols


def axis_sizes():
    return lax.axis_size("img"), lax.axis_size("row"), lax.axis_size("col")


class Place:
    def __init__(self):
        images, self.rows, self.cols = axis_sizes()
        self.chips = images // 2
        img = lax.axis_index("img")
        self.chip, self.core = img // 2, img % 2
        self.row, self.col = lax.axis_index("row"), lax.axis_index("col")

    def other(self, axis, k):
        if axis == "row":
            index = (self.row + k) % self.rows
            return index, {"row": index}
        if axis == "col":
            index = (self.col + k) % self.cols
            return index, {"col": index}
        index = (self.chip + k) % self.chips
        return index, {"img": index * 2 + self.core}

    def sibling(self):
        return {"img": self.chip * 2 + 1 - self.core}

    def count(self, axis):
        return {"row": self.rows, "col": self.cols, "chip": self.chips}[axis]


def greet(place, image_wide):
    barrier = pltpu.get_barrier_semaphore()
    heard = 1
    pl.semaphore_signal(barrier, inc=1, device_id=place.sibling(), device_id_type=MESH)
    for k in range(1, place.chips):
        pl.semaphore_signal(barrier, inc=1, device_id=place.other("chip", k)[1], device_id_type=MESH)
        heard += 1
    for r in range(place.rows):
        for c in range(place.cols):
            if (r, c) == (0, 0) or not (image_wide or r == 0 or c == 0):
                continue
            target = {"row": (place.row + r) % place.rows, "col": (place.col + c) % place.cols}
            pl.semaphore_signal(barrier, inc=1, device_id=target, device_id_type=MESH)
            heard += 1
    pl.semaphore_wait(barrier, heard)


class Copies:
    def __init__(self, send_sems, recv_sems):
        self.send_sems, self.recv_sems = send_sems, recv_sems
        self.used = 0
        self.open = []

    def start(self, source, target, device):
        copy = pltpu.make_async_remote_copy(
            src_ref=source,
            dst_ref=target,
            send_sem=self.send_sems.at[self.used],
            recv_sem=self.recv_sems.at[self.used],
            device_id=device,
            device_id_type=MESH,
        )
        self.used += 1
        copy.start()
        self.open.append(copy)
        return copy

    def finish(self):
        for copy in self.open:
            copy.wait_send()
        self.open = []


def gather_copies(rows, cols, chips):
    return (cols - 1) + (rows - 1) + (chips - 1) + rows * (chips - 1) + chips * (rows - 1) + chips


def gather_phase(place, copies, phase, shard, full, local):
    y, c, x, z = place.chip, place.core, place.row, place.col
    half = place.cols // 2
    low, high = pl.ds(0, half), pl.ds(half, place.cols - half)
    started = []
    if phase == 0:
        keep = pltpu.make_async_copy(shard, full.at[y, c, x, z], local)
        keep.start()
        for k in range(1, place.cols):
            started.append(copies.start(shard, full.at[y, c, x, z], place.other("col", k)[1]))
        return started, keep
    if phase == 1:
        for k in range(1, place.rows):
            part = full.at[y, c, x, low]
            started.append(copies.start(part, part, place.other("row", k)[1]))
        for k in range(1, place.chips):
            part = full.at[y, c, x, high]
            started.append(copies.start(part, part, place.other("chip", k)[1]))
    if phase == 2:
        for k in range(1, place.chips):
            for row in range(place.rows):
                part = full.at[y, c, row, low]
                started.append(copies.start(part, part, place.other("chip", k)[1]))
        for k in range(1, place.rows):
            for chip in range(place.chips):
                part = full.at[chip, c, x, high]
                started.append(copies.start(part, part, place.other("row", k)[1]))
    if phase == 3:
        for chip in range(place.chips):
            part = full.at[chip, c]
            started.append(copies.start(part, part, place.sibling()))
    return started, None


def wait_phase(started):
    copies, keep = started
    if keep is not None:
        keep.wait()
    for copy in copies:
        copy.wait_recv()


def gather_kernel(groups, *refs):
    count = sum(map(len, groups))
    shards, fulls = refs[:count], refs[count : 2 * count]
    send_sems, recv_sems, local_sems = refs[2 * count :]
    place = Place()
    greet(place, False)
    copies = Copies(send_sems, recv_sems)
    waiting = {}
    for step in range(len(groups) + 4):
        for number in range(len(groups)):
            phase = step - number
            if 0 <= phase <= 4:
                for item in groups[number]:
                    if phase > 0:
                        wait_phase(waiting.pop(item))
                    if phase < 4:
                        waiting[item] = gather_phase(
                            place, copies, phase, shards[item], fulls[item], local_sems.at[item]
                        )
    copies.finish()


def gather(shards, groups, number):
    images, rows, cols = axis_sizes()
    chips = images // 2
    each = gather_copies(rows, cols, chips)
    anywhere = pl.BlockSpec(memory_space=pl.ANY)
    fulls = pl.pallas_call(
        functools.partial(gather_kernel, groups),
        out_shape=[
            jax.ShapeDtypeStruct((chips, 2, rows, cols) + shard.shape, shard.dtype) for shard in shards
        ],
        in_specs=[anywhere] * len(shards),
        out_specs=[anywhere] * len(shards),
        scratch_shapes=[
            pltpu.SemaphoreType.DMA((each * len(shards),)),
            pltpu.SemaphoreType.DMA((each * len(shards),)),
            pltpu.SemaphoreType.DMA((len(shards),)),
        ],
        compiler_params=params(collective_id=number, has_side_effects=True),
    )(*shards)
    return fulls


def scatter_copies(rows, cols, chips):
    return chips + (chips - 1) + (rows - 1) + (rows - 1) + (chips - 1) + (cols - 1)


def scatter_buffers(shape, rows, cols, chips):
    half = cols // 2
    rest = cols - half
    return [
        pltpu.VMEM((chips, rows, cols) + shape, BF16),
        pltpu.VMEM((chips, rows, cols) + shape, BF16),
        pltpu.VMEM((chips - 1, rows, half) + shape, BF16),
        pltpu.VMEM((rows - 1, chips, rest) + shape, BF16),
        pltpu.VMEM((rows - 1, half) + shape, BF16),
        pltpu.VMEM((chips - 1, rest) + shape, BF16),
        pltpu.VMEM((cols - 1,) + shape, BF16),
    ]


def add_into(target, index, terms):
    total = target[index].astype(F32)
    for ref, at in terms:
        total = total + ref[at].astype(F32)
    target[index] = total.astype(BF16)


def scatter_phase(place, copies, phase, full, out, buffers, local):
    y, c, x, z = place.chip, place.core, place.row, place.col
    mine, twin, low_chip, high_row, low_row, high_chip, along = buffers
    half = place.cols // 2
    rest = place.cols - half
    low, high = pl.ds(0, half), pl.ds(half, rest)
    started, keep = [], None
    if phase == 0:
        keep = pltpu.make_async_copy(full.at[:, c], mine, local)
        keep.start()
        for chip in range(place.chips):
            started.append(copies.start(full.at[chip, 1 - c], twin.at[chip], place.sibling()))
    if phase == 1:

        @pl.loop(0, place.chips * place.rows * place.cols)
        def _(n):
            index = (n // (place.rows * place.cols), n // place.cols % place.rows, n % place.cols)
            add_into(mine, index, [(twin, index)])

        for k in range(1, place.chips):
            to, device = place.other("chip", k)
            started.append(copies.start(mine.at[to, :, low], low_chip.at[k - 1], device))
        for k in range(1, place.rows):
            to, device = place.other("row", k)
            started.append(copies.start(mine.at[:, to, high], high_row.at[k - 1], device))
    if phase == 2:

        @pl.loop(0, place.rows * half)
        def _(n):
            r, j = n // half, n % half
            add_into(mine, (y, r, j), [(low_chip, (k, r, j)) for k in range(place.chips - 1)])

        @pl.loop(0, place.chips * rest)
        def _(n):
            chip, j = n // rest, n % rest
            add_into(mine, (chip, x, half + j), [(high_row, (k, chip, j)) for k in range(place.rows - 1)])

        for k in range(1, place.rows):
            to, device = place.other("row", k)
            started.append(copies.start(mine.at[y, to, low], low_row.at[k - 1], device))
        for k in range(1, place.chips):
            to, device = place.other("chip", k)
            started.append(copies.start(mine.at[to, x, high], high_chip.at[k - 1], device))
    if phase == 3:
        for j in range(half):
            add_into(mine, (y, x, j), [(low_row, (k, j)) for k in range(place.rows - 1)])
        for j in range(rest):
            add_into(mine, (y, x, half + j), [(high_chip, (k, j)) for k in range(place.chips - 1)])
        for k in range(1, place.cols):
            to, device = place.other("col", k)
            started.append(copies.start(mine.at[y, x, to], along.at[k - 1], device))
    if phase == 4:
        total = mine[y, x, z].astype(F32)
        for k in range(place.cols - 1):
            total = total + along[k].astype(F32)
        out[...] = total
    return started, keep


def swap_steps(place):
    steps = [place.sibling()]
    bit = 1
    while bit < place.chips:
        flip = place.chip + bit - 2 * bit * (place.chip // bit % 2)
        steps.append({"img": flip * 2 + place.core})
        bit *= 2
    bit = 1
    while bit < place.rows:
        steps.append({"row": place.row + bit - 2 * bit * (place.row // bit % 2)})
        bit *= 2
    bit = 1
    while bit < place.cols:
        steps.append({"col": place.col + bit - 2 * bit * (place.col // bit % 2)})
        bit *= 2
    return steps


def scatter_kernel(groups, with_sum, *refs):
    count = sum(map(len, groups))
    refs = list(refs)

    def take(n):
        taken = refs[:n]
        del refs[:n]
        return taken

    fulls = take(count)
    term = take(1)[0] if with_sum else None
    outs = take(count)
    total = take(1)[0] if with_sum else None
    buffers = [take(7) for _ in range(count)]
    send_sems, recv_sems, local_sems = take(3)
    place = Place()
    greet(place, False)
    copies = Copies(send_sems, recv_sems)
    waiting = {}
    swaps = swap_steps(place) if with_sum else []
    if with_sum:
        held, arriving = take(2)
        held[0] = term[...]
    swap = None
    for step in range(max(len(groups) + 4, len(swaps) + 1)):
        if swap is not None:
            swap.wait_recv()
            held[step] = held[step - 1] + arriving[step - 1]
            swap = None
            if step == len(swaps):
                total[...] = held[step]
        if step < len(swaps):
            swap = copies.start(held.at[step], arriving.at[step], swaps[step])
        for number in range(len(groups)):
            phase = step - number
            if 0 <= phase <= 4:
                for item in groups[number]:
                    if phase > 0:
                        wait_phase(waiting.pop(item))
                    waiting[item] = scatter_phase(
                        place, copies, phase, fulls[item], outs[item], buffers[item], local_sems.at[item]
                    )
    copies.finish()


def scatter(fulls, groups, number, term=None):
    images, rows, cols = axis_sizes()
    chips = images // 2
    shapes = [full.shape[4:] for full in fulls]
    swaps = (images * rows * cols).bit_length() - 1
    extra = swaps if term is not None else 0
    each = scatter_copies(rows, cols, chips)
    anywhere = pl.BlockSpec(memory_space=pl.ANY)
    vmem = pl.BlockSpec(memory_space=pltpu.VMEM)
    scratch = sum([scatter_buffers(shape, rows, cols, chips) for shape in shapes], [])
    scratch += [
        pltpu.SemaphoreType.DMA((each * len(fulls) + extra,)),
        pltpu.SemaphoreType.DMA((each * len(fulls) + extra,)),
        pltpu.SemaphoreType.DMA((len(fulls),)),
    ]
    out_shape = [jax.ShapeDtypeStruct(shape, F32) for shape in shapes]
    operands = list(fulls)
    in_specs = [anywhere] * len(fulls)
    if term is not None:
        operands.append(term)
        in_specs.append(vmem)
        out_shape.append(jax.ShapeDtypeStruct(term.shape, F32))
        scratch += [pltpu.VMEM((swaps + 1,) + term.shape, F32), pltpu.VMEM((swaps,) + term.shape, F32)]
    return pl.pallas_call(
        functools.partial(scatter_kernel, groups, term is not None),
        out_shape=out_shape,
        in_specs=in_specs,
        out_specs=[vmem] * len(out_shape),
        scratch_shapes=scratch,
        compiler_params=params(collective_id=number, has_side_effects=True),
    )(*operands)


def exchange(place, copies, plan, source, target, back):
    me = place.row * place.cols + place.col
    first = copies.used
    for number, (giver, taker, out, into, count) in enumerate(plan["pairs"]):
        if back:
            giver, taker, out, into = taker, giver, into, out

        def describe(giver=giver, taker=taker, out=out, into=into, count=count, number=number):
            return pltpu.make_async_remote_copy(
                src_ref=source.at[pl.ds(out, count)],
                dst_ref=target.at[pl.ds(into, count)],
                send_sem=copies.send_sems.at[first + number],
                recv_sem=copies.recv_sems.at[first + number],
                device_id={"row": taker // place.cols, "col": taker % place.cols},
                device_id_type=MESH,
            )

        yield me, giver, taker, describe
    copies.used = first + len(plan["pairs"])


def windows_kernel(plan, back, *refs):
    count = len(refs) - 6
    arrays, pack_ref, place_ref = refs[: count // 2], refs[count // 2], refs[count // 2 + 1]
    outs = refs[count // 2 + 2 : count + 2]
    packed, landed, send_sems, recv_sems = refs[count + 2 : count + 6]
    landed[...] = jnp.zeros_like(landed)
    place = Place()
    greet(place, True)
    copies = Copies(send_sems, recv_sems)
    pick = one_hot(pack_ref[...], arrays[0].shape[0])
    for k, array in enumerate(arrays):
        packed[:, pl.ds(k * D, D)] = matmul(pick, array[...]).astype(BF16)
    listed = list(exchange(place, copies, plan, packed, landed, back))
    for me, giver, taker, describe in listed:

        @pl.when(me == giver)
        def _():
            describe().start()

    index = place_ref[...]
    here = one_hot(index, arrays[0].shape[0])
    for k, array in enumerate(arrays):
        outs[k][...] = matmul(here, array[...]).astype(BF16)
    for me, giver, taker, describe in listed:

        @pl.when(me == taker)
        def _():
            describe().wait_recv()

    there = one_hot(index - arrays[0].shape[0], landed.shape[0])
    for k in range(len(arrays)):
        outs[k][...] += matmul(there, landed[:, pl.ds(k * D, D)]).astype(BF16)
    for me, giver, taker, describe in listed:

        @pl.when(me == giver)
        def _():
            describe().wait_send()


def move_windows(plan, arrays, pick, index, back, number):
    length = index.shape[0]
    landed = plan["packed"] if back else plan["landed"]
    vmem = pl.BlockSpec(memory_space=pltpu.VMEM)

    def kernel(*refs):
        windows_kernel(plan, back, *refs)

    return pl.pallas_call(
        kernel,
        out_shape=[jax.ShapeDtypeStruct((length, D), BF16) for _ in arrays],
        in_specs=[vmem] * (len(arrays) + 2),
        out_specs=[vmem] * len(arrays),
        scratch_shapes=[
            pltpu.VMEM((pick.shape[0], len(arrays) * D), BF16),
            pltpu.VMEM((landed, len(arrays) * D), BF16),
            pltpu.SemaphoreType.DMA((len(plan["pairs"]),)),
            pltpu.SemaphoreType.DMA((len(plan["pairs"]),)),
        ],
        compiler_params=params(collective_id=number, has_side_effects=True),
    )(*arrays, pick, index)


def slab_shape(shape):
    return shape if shape[0] % 8 == 0 else (shape[0] * shape[1] // 128, 128)


def body(
    image_tokens, cotangent, content_mask, norm1_gain, norm1_bias, qkv_weight, query_bias, value_bias,
    rel_rows, rel_cols, proj_weight, proj_bias, norm2_gain, norm2_bias, fc1_weight, fc1_bias, fc2_weight, fc2_bias,
):
    images, rows, cols = axis_sizes()
    chips, devices = images // 2, images * rows * cols
    _, tile_rows, tile_cols, _ = image_tokens.shape
    plan = plan_windows(rows, cols, tile_rows, tile_cols)
    me = lax.axis_index("row") * cols + lax.axis_index("col")

    def own(table):
        return lax.dynamic_index_in_dim(jnp.asarray(table), me, keepdims=False)

    pick, slot_index = own(plan["pack_from"])[:, None], own(plan["slot_from"])[:, None]
    back_pick, tile_index = own(plan["back_from"])[:, None], own(plan["tile_from"])[:, None]
    where = own(plan["where"])

    vectors = [norm1_gain, norm1_bias, query_bias, value_bias, proj_bias, norm2_gain, norm2_bias, fc2_bias]
    piece, wide = norm1_gain.shape[0], fc1_bias.shape[0]
    flat = jnp.concatenate(vectors + [fc1_bias])
    used = flat.shape[0]
    padded = round_up(used, 2048)
    small = jnp.pad(flat, (0, padded - used)).reshape(padded // 128, 128)
    weights = [qkv_weight, proj_weight, fc1_weight, fc2_weight]
    shards = [small] + [w.reshape(slab_shape(w.shape)) for w in weights]

    tokens, grads = (a.reshape(tile_rows * tile_cols, D) for a in (image_tokens, cotangent))
    xs, gs = move_windows(plan, [tokens, grads], pick, slot_index, False, 0)
    fulls = gather(shards, [[0, 1], [2, 3], [4]], 1)
    lists = fulls[0].reshape(devices, padded)[:, :used].astype(F32)
    vec = lists[:, : 8 * piece].reshape(devices, 8, piece).transpose(1, 0, 2).reshape(8, devices * piece)
    b1 = lists[:, 8 * piece :].reshape(1, devices * wide)
    whole_weights = [
        full.reshape((devices * w.shape[0],) + w.shape[1:]) for full, w in zip(fulls[1:], weights)
    ]
    out, gx, dw_qkv, dw_proj, dw_fc1, dw_fc2, sums, db1, drel_rows, drel_cols = compute(
        plan, xs, gs, content_mask[0].astype(BF16), where, rel_rows, rel_cols, vec, b1, *whole_weights
    )
    split = jnp.concatenate(
        [sums.reshape(8, devices, piece).transpose(1, 0, 2).reshape(devices, 8 * piece), db1.reshape(devices, wide)],
        axis=1,
    ).astype(BF16)
    split = jnp.pad(split, ((0, 0), (0, padded - used))).reshape((devices,) + small.shape)
    term = jnp.concatenate([drel_rows, drel_cols], axis=1)
    term = jnp.pad(term, ((0, 32 - term.shape[0]), (0, 0)))
    partial = [split, dw_qkv, dw_proj, dw_fc1, dw_fc2]
    partial = [p.reshape((chips, 2, rows, cols) + s.shape) for p, s in zip(partial, shards)]
    *parts, rel_total = scatter(partial, [[3, 4], [2], [1, 0]], 2, term)
    out, gx = move_windows(plan, [out, gx], back_pick, tile_index, True, 3)
    flat = parts[0].reshape(padded)
    g_vec = [flat[k * piece : (k + 1) * piece] for k in range(8)]
    g_b1 = flat[8 * piece : 8 * piece + wide]
    g_qkv, g_proj, g_fc1, g_fc2 = (p.reshape(w.shape) for p, w in zip(parts[1:], weights))
    span = rel_rows.shape[0]
    return (
        out.reshape(image_tokens.shape), gx.reshape(image_tokens.shape),
        g_vec[0], g_vec[1], g_qkv, g_vec[2], g_vec[3],
        rel_total[:span, :HEAD_DIM], rel_total[:span, HEAD_DIM:],
        g_proj, g_vec[4], g_vec[5], g_vec[6], g_fc1, g_b1, g_fc2, g_vec[7],
    )


def solution(mesh):
    everywhere = ("img", "row", "col")
    tile, vector, matrix = P("img", "row", "col", None), P(everywhere), P(everywhere, None)
    in_specs = (
        tile, tile, P("img", None, None), vector, vector, matrix, vector, vector, P(), P(),
        matrix, vector, vector, vector, matrix, vector, matrix, vector,
    )
    out_specs = (
        tile, tile, vector, vector, matrix, vector, vector, P(), P(),
        matrix, vector, vector, vector, matrix, vector, matrix, vector,
    )
    return jax.shard_map(body, mesh=mesh, in_specs=in_specs, out_specs=out_specs, check_vma=False)
```

```python
import functools

import jax
import jax.numpy as jnp
import numpy as np
from jax import lax
from jax.experimental import pallas as pl
from jax.experimental.pallas import tpu as pltpu
from jax.sharding import PartitionSpec as P

D = 768
HEADS = 12
HEAD_DIM = 64
PAIRS = HEADS // 2
WIN = 14
CELLS = WIN * WIN
SLOT = 208
MESH = pl.DeviceIdType.MESH
F32 = jnp.float32
BF16 = jnp.bfloat16
VMEM_LIMIT = 60 * 2**20


def round_up(value, unit):
    return -(-value // unit) * unit


def plan_windows(rows, cols, tile_rows, tile_cols):
    devices = rows * cols
    height, width = rows * tile_rows, cols * tile_cols
    windows = []
    for top in range(0, height, WIN):
        for left in range(0, width, WIN):
            windows.append(
                [
                    (r, c, r - top, c - left)
                    for r in range(top, min(top + WIN, height))
                    for c in range(left, min(left + WIN, width))
                ]
            )
    bins = []
    for window in sorted(windows, key=len, reverse=True):
        for held in bins:
            if len(held) < 2 and sum(map(len, held)) + len(window) <= CELLS:
                held.append(window)
                break
        else:
            bins.append([window])
    slots = -(-len(bins) // devices)
    while len(bins) < slots * devices:
        bins.append([])

    def home(cell):
        return cell[0] // tile_rows * cols + cell[1] // tile_cols

    weights = np.zeros((len(bins), devices), np.int64)
    for number, held in enumerate(bins):
        for window in held:
            for cell in window:
                weights[number, home(cell)] += 1
    hops = np.zeros((devices, devices, rows * rows * cols + cols * cols * rows))
    for source in range(devices):
        for target in range(devices):
            r0, c0, r1, c1 = source // cols, source % cols, target // cols, target % cols
            step = 1 if r1 > r0 else -1
            for r in range(r0, r1, step):
                hops[source, target, (r * rows + r + step) * cols + c0] = 1
            step = 1 if c1 > c0 else -1
            for c in range(c0, c1, step):
                hops[source, target, rows * rows * cols + (c * cols + c + step) * rows + r1] = 1
    loads = np.einsum("bs,sdl->bdl", weights, hops)

    def cost(order):
        load = loads[np.arange(len(bins)), np.array(order) // slots].sum(axis=0)
        return load.max() * 100 + load.sum()

    order = [0] * len(bins)
    free = [slots] * devices
    for number in range(len(bins)):
        options = [d for d in range(devices) if free[d]]
        best = min(options, key=lambda d: (loads[number, d].sum(), d))
        order[number] = best * slots + slots - free[best]
        free[best] -= 1
    current = cost(order)
    while True:
        found = None
        for a in range(len(bins)):
            for b in range(a):
                if order[a] // slots != order[b] // slots:
                    order[a], order[b] = order[b], order[a]
                    trial = cost(order)
                    if trial < current:
                        current, found = trial, (a, b)
                    order[a], order[b] = order[b], order[a]
        if found is None:
            break
        a, b = found
        order[a], order[b] = order[b], order[a]
    total = slots * SLOT
    place = [[] for _ in range(devices)]
    for number in sorted(range(len(bins)), key=lambda n: order[n]):
        device, slot = order[number] // slots, order[number] % slots
        position = slot * SLOT
        for group, window in enumerate(bins[number]):
            for cell in window:
                place[device].append((position, cell, group))
                position += 1
    cells = tile_rows * tile_cols
    pairs = []
    sent, got = [0] * devices, [0] * devices
    moved = {}
    for source in range(devices):
        for target in range(devices):
            if source != target:
                listed = [e for e in place[target] if home(e[1]) == source]
                if listed:
                    count = round_up(len(listed), 16)
                    pairs.append((source, target, sent[source], got[target], count))
                    moved[source, target] = (listed, sent[source], got[target])
                    sent[source] += count
                    got[target] += count
    packed, landed = round_up(max(sent), 128), round_up(max(got), 128)
    pack_from = np.full((devices, packed), -1, np.int32)
    slot_from = np.full((devices, total), -1, np.int32)
    back_from = np.full((devices, landed), -1, np.int32)
    tile_from = np.full((devices, cells), -1, np.int32)
    where = np.full((devices, total, 8), -1, np.int32)
    for device in range(devices):
        for position, cell, group in place[device]:
            where[device, position, :5] = (cell[2], cell[3], group, cell[0], cell[1])
            if home(cell) == device:
                local = cell[0] % tile_rows * tile_cols + cell[1] % tile_cols
                slot_from[device, position] = local
                tile_from[device, local] = position
    for (source, target), (listed, out, into) in moved.items():
        for k, (position, cell, group) in enumerate(listed):
            local = cell[0] % tile_rows * tile_cols + cell[1] % tile_cols
            pack_from[source, out + k] = local
            slot_from[target, position] = cells + into + k
            back_from[target, into + k] = position
            tile_from[source, local] = total + out + k
    return dict(
        slots=slots, total=total, pairs=pairs, packed=packed, landed=landed, where=where,
        pack_from=pack_from, slot_from=slot_from, back_from=back_from, tile_from=tile_from,
    )


def matmul(a, b):
    return jnp.dot(a, b, preferred_element_type=F32)


def matmul_nt(a, b):
    return lax.dot_general(a, b, (((1,), (1,)), ((), ())), preferred_element_type=F32)


def matmul_tn(a, b):
    return lax.dot_general(a, b, (((0,), (0,)), ((), ())), preferred_element_type=F32)


def one_hot(index, width):
    return (index == lax.broadcasted_iota(jnp.int32, (index.shape[0], width), 1)).astype(BF16)


def normalized(values):
    offset = values - jnp.mean(values, axis=-1, keepdims=True)
    rate = lax.rsqrt(jnp.mean(offset * offset, axis=-1, keepdims=True) + 1e-06)
    return offset * rate, rate


def norm_back(cotangent, gain, hat, rate):
    e = cotangent * gain
    mean_e = jnp.mean(e, axis=-1, keepdims=True)
    mean_eh = jnp.mean(e * hat, axis=-1, keepdims=True)
    return rate * (e - mean_e - hat * mean_eh)


def column_sum(values):
    return jnp.sum(values, axis=0, keepdims=True)


def params(**more):
    return pltpu.CompilerParams(vmem_limit_bytes=VMEM_LIMIT, **more)


def head_halves(pair):
    low = lax.broadcasted_iota(jnp.int32, pair.shape, 1) < HEAD_DIM
    zero = jnp.zeros_like(pair)
    return jnp.concatenate([jnp.where(low, pair, zero), jnp.where(low, zero, pair)], axis=0)


def join_halves(stacked):
    low = lax.broadcasted_iota(jnp.int32, (SLOT, 2 * HEAD_DIM), 1) < HEAD_DIM
    return jnp.where(low, stacked[:SLOT], stacked[SLOT:])


REL = 512


def own_place(where_ref):
    lane = lax.broadcasted_iota(jnp.int32, (SLOT, REL), 1)
    row, col = where_ref[:, 0:1], where_ref[:, 1:2]
    first, second = row * WIN, REL // 2 + col * WIN
    hot = (lane >= first) & (lane < first + WIN) & (row >= 0)
    hot = hot | ((lane >= second) & (lane < second + WIN) & (col >= 0))
    return jnp.where(hot, 1.0, 0.0).astype(BF16)


def rel_tables(rel_rows, rel_cols):
    index = np.arange(WIN)[:, None] - np.arange(WIN)[None, :] + WIN - 1
    select = np.zeros((2, 2 * WIN - 1, REL // 2), np.float32)
    select[:, index.reshape(-1), np.arange(CELLS)] = 1
    rel = jnp.concatenate(
        [
            jnp.einsum("mc,ml->cl", table, select[0].astype(BF16), preferred_element_type=F32)
            for table in (rel_rows, rel_cols)
        ],
        axis=1,
    ).astype(BF16)
    fold = np.zeros((REL, 128), np.float32)
    for first in range(WIN):
        for second in range(WIN):
            fold[first * WIN + second, second] = 1
            fold[REL // 2 + first * WIN + second, WIN + second] = 1
    return jnp.concatenate([rel, rel], axis=0), jnp.asarray(fold, BF16), select[0]


def axis_sizes():
    return lax.axis_size("img"), lax.axis_size("row"), lax.axis_size("col")


class Place:
    def __init__(self):
        images, self.rows, self.cols = axis_sizes()
        self.chips = images // 2
        img = lax.axis_index("img")
        self.chip, self.core = img // 2, img % 2
        self.row, self.col = lax.axis_index("row"), lax.axis_index("col")

    def other(self, axis, k):
        if axis == "row":
            index = (self.row + k) % self.rows
            return index, {"row": index}
        if axis == "col":
            index = (self.col + k) % self.cols
            return index, {"col": index}
        index = (self.chip + k) % self.chips
        return index, {"img": index * 2 + self.core}

    def sibling(self):
        return {"img": self.chip * 2 + 1 - self.core}

    def count(self, axis):
        return {"row": self.rows, "col": self.cols, "chip": self.chips}[axis]


def greet(place, image_wide):
    barrier = pltpu.get_barrier_semaphore()
    heard = 1
    pl.semaphore_signal(barrier, inc=1, device_id=place.sibling(), device_id_type=MESH)
    for k in range(1, place.chips):
        pl.semaphore_signal(barrier, inc=1, device_id=place.other("chip", k)[1], device_id_type=MESH)
        heard += 1
    for r in range(place.rows):
        for c in range(place.cols):
            if (r, c) == (0, 0) or not (image_wide or r == 0 or c == 0):
                continue
            target = {"row": (place.row + r) % place.rows, "col": (place.col + c) % place.cols}
            pl.semaphore_signal(barrier, inc=1, device_id=target, device_id_type=MESH)
            heard += 1
    pl.semaphore_wait(barrier, heard)


class Copies:
    def __init__(self, send_sems, recv_sems):
        self.send_sems, self.recv_sems = send_sems, recv_sems
        self.used = 0
        self.open = []

    def start(self, source, target, device):
        copy = pltpu.make_async_remote_copy(
            src_ref=source,
            dst_ref=target,
            send_sem=self.send_sems.at[self.used],
            recv_sem=self.recv_sems.at[self.used],
            device_id=device,
            device_id_type=MESH,
        )
        self.used += 1
        copy.start()
        self.open.append(copy)
        return copy

    def finish(self):
        for copy in self.open:
            copy.wait_send()
        self.open = []


def swap_steps(place):
    steps = [place.sibling()]
    bit = 1
    while bit < place.chips:
        flip = place.chip + bit - 2 * bit * (place.chip // bit % 2)
        steps.append({"img": flip * 2 + place.core})
        bit *= 2
    bit = 1
    while bit < place.rows:
        steps.append({"row": place.row + bit - 2 * bit * (place.row // bit % 2)})
        bit *= 2
    bit = 1
    while bit < place.cols:
        steps.append({"col": place.col + bit - 2 * bit * (place.col // bit % 2)})
        bit *= 2
    return steps


class Unit:
    def __init__(self, rows, width, mode):
        self.rows, self.width, self.mode = rows, width, mode
        self.images, self.row_count, self.col_count = axis_sizes()
        self.chips = self.images // 2
        self.block = rows if mode == "sum" else rows * self.col_count
        self.line = self.block * self.row_count
        self.low = pl.ds(0, width // 2)
        self.high = pl.ds(width // 2, width - width // 2)
        self.half = width // 2

    def full_shape(self):
        return (2 * self.chips * self.line, self.width)

    def half_shape(self):
        return (self.chips * self.line, self.width)

    def stage_shape(self):
        return (self.col_count, self.rows, self.width)

    def rows_at(self, index, count=1):
        return pl.ds(pl.multiple_of(index * self.block, 8), count * self.block)

    def gather_count(self):
        c, r, n = self.chips, self.row_count, self.col_count
        return (n - 1) + (r - 1) + (c - 1) + (c - 1) + (r - 1) * c + c

    def scatter_count(self):
        c, r, n = self.chips, self.row_count, self.col_count
        return c + (c - 1) + (r - 1) * c + (r - 1) + (c - 1) + (n - 1)

    def spread(self, k):
        row = lax.broadcasted_iota(jnp.int32, (self.block, self.rows), 0)
        col = lax.broadcasted_iota(jnp.int32, (self.block, self.rows), 1)
        return jnp.where(row == col + k * self.rows, 1.0, 0.0).astype(BF16)


class Gather:
    def __init__(self, place, copies, unit, shard, full, stage, local):
        self.place, self.copies, self.unit = place, copies, unit
        self.shard, self.full, self.stage, self.local = shard, full, stage, local
        self.phase = 0
        self.waiting, self.sent = [], []

    def settle(self):
        for copy in self.sent:
            copy.wait_send()
        self.copies.open = [copy for copy in self.copies.open if not any(copy is own for own in self.sent)]
        self.sent = []

    def advance(self):
        place, unit, full = self.place, self.unit, self.full
        y, c, x, z = place.chip, place.core, place.row, place.col
        own = (y * 2 + c) * place.rows + x
        for copy in self.waiting:
            copy.wait_recv()
        self.waiting = []
        start = self.copies.start
        if self.phase == 0:
            if unit.mode == "plain":
                target = full.at[pl.ds(pl.multiple_of(own * unit.block + z * unit.rows, 8), unit.rows)]
            else:
                target = self.stage.at[z]
            self.keep = pltpu.make_async_copy(self.shard, target, self.local)
            self.keep.start()
            for k in range(1, place.cols):
                self.waiting.append(start(self.shard, target, place.other("col", k)[1]))
        if self.phase == 1:
            self.keep.wait()
            if unit.mode == "rows":
                total = None
                for k in range(place.cols):
                    term = matmul(unit.spread(k), self.stage[k])
                    total = term if total is None else total + term
                full[unit.rows_at(own), :] = total.astype(BF16)
            if unit.mode == "sum":
                total = self.stage[0].astype(F32)
                for k in range(1, place.cols):
                    total = total + self.stage[k].astype(F32)
                full[unit.rows_at(own), :] = total.astype(BF16)
            for k in range(1, place.rows):
                part = full.at[unit.rows_at(own), unit.low]
                self.waiting.append(start(part, part, place.other("row", k)[1]))
            for k in range(1, place.chips):
                part = full.at[unit.rows_at(own), unit.high]
                self.waiting.append(start(part, part, place.other("chip", k)[1]))
        if self.phase == 2:
            for k in range(1, place.chips):
                part = full.at[unit.rows_at((y * 2 + c) * place.rows, place.rows), unit.low]
                self.waiting.append(start(part, part, place.other("chip", k)[1]))
            for k in range(1, place.rows):
                for chip in range(place.chips):
                    part = full.at[unit.rows_at((chip * 2 + c) * place.rows + x), unit.high]
                    self.waiting.append(start(part, part, place.other("row", k)[1]))
        if self.phase == 3:
            for chip in range(place.chips):
                part = full.at[unit.rows_at((chip * 2 + c) * place.rows, place.rows)]
                self.waiting.append(start(part, part, place.sibling()))
        self.sent += self.waiting
        self.phase += 1


class Scatter:
    def __init__(self, place, copies, unit, full, half, buffers, out):
        self.place, self.copies, self.unit = place, copies, unit
        self.full, self.half, self.buffers, self.out = full, half, buffers, out
        self.phase = 0
        self.waiting = []

    @staticmethod
    def buffer_shapes(unit):
        c, r, n = unit.chips, unit.row_count, unit.col_count
        shapes = [
            (c - 1, unit.line, unit.half),
            (r - 1, c, unit.block, unit.half),
            (r - 1, unit.block, unit.half),
            (c - 1, unit.block, unit.half),
            (n - 1, unit.rows, unit.width),
        ]
        if unit.mode == "rows":
            shapes.append((n, unit.rows, unit.width))
        return [pltpu.VMEM(shape, BF16) for shape in shapes]

    def advance(self):
        place, unit, half = self.place, self.unit, self.half
        y, c, x, z = place.chip, place.core, place.row, place.col
        for copy in self.waiting:
            copy.wait_recv()
        self.waiting = []
        start = self.copies.start
        if self.phase == 0:
            for chip in range(place.chips):
                self.waiting.append(
                    start(
                        self.full.at[unit.rows_at((chip * 2 + 1 - c) * place.rows, place.rows)],
                        half.at[unit.rows_at(chip * place.rows, place.rows)],
                        place.sibling(),
                    )
                )
        if self.phase == 1:
            if self.full is not None:
                for chip in range(place.chips):
                    for row in range(place.rows):
                        at = unit.rows_at(chip * place.rows + row)
                        term = self.full[unit.rows_at((chip * 2 + c) * place.rows + row), :]
                        half[at, :] = (half[at, :].astype(F32) + term.astype(F32)).astype(BF16)
        if self.phase == 2:
            low_chip, high_row = self.buffers[:2]
            for k in range(1, place.chips):
                to, device = place.other("chip", k)
                part = half.at[unit.rows_at(to * place.rows, place.rows), unit.low]
                self.waiting.append(start(part, low_chip.at[k - 1], device))
            for k in range(1, place.rows):
                to, device = place.other("row", k)
                for chip in range(place.chips):
                    part = half.at[unit.rows_at(chip * place.rows + to), unit.high]
                    self.waiting.append(start(part, high_row.at[k - 1, chip], device))
        if self.phase == 3:
            low_chip, high_row, low_row, high_chip = self.buffers[:4]
            for row in range(place.rows):
                at = unit.rows_at(y * place.rows + row)
                total = half[at, unit.low].astype(F32)
                for k in range(place.chips - 1):
                    total = total + low_chip[k, pl.ds(row * unit.block, unit.block), :].astype(F32)
                half[at, unit.low] = total.astype(BF16)
            for chip in range(place.chips):
                at = unit.rows_at(chip * place.rows + x)
                total = half[at, unit.high].astype(F32)
                for k in range(place.rows - 1):
                    total = total + high_row[k, chip].astype(F32)
                half[at, unit.high] = total.astype(BF16)
            for k in range(1, place.rows):
                to, device = place.other("row", k)
                part = half.at[unit.rows_at(y * place.rows + to), unit.low]
                self.waiting.append(start(part, low_row.at[k - 1], device))
            for k in range(1, place.chips):
                to, device = place.other("chip", k)
                part = half.at[unit.rows_at(to * place.rows + x), unit.high]
                self.waiting.append(start(part, high_chip.at[k - 1], device))
        own = unit.rows_at(y * place.rows + x)
        if self.phase == 4:
            low_row, high_chip, along = self.buffers[2:5]
            total = half[own, unit.low].astype(F32)
            for k in range(place.rows - 1):
                total = total + low_row[k].astype(F32)
            half[own, unit.low] = total.astype(BF16)
            total = half[own, unit.high].astype(F32)
            for k in range(place.chips - 1):
                total = total + high_chip[k].astype(F32)
            half[own, unit.high] = total.astype(BF16)
            if unit.mode == "rows":
                cut = self.buffers[5]
                block = half[own, :]
                for k in range(place.cols):
                    cut[k] = matmul_tn(unit.spread(k), block).astype(BF16)
            for k in range(1, place.cols):
                to, device = place.other("col", k)
                if unit.mode == "rows":
                    part = self.buffers[5].at[to]
                elif unit.mode == "plain":
                    index = (y * place.rows + x) * unit.block + to * unit.rows
                    part = half.at[pl.ds(pl.multiple_of(index, 8), unit.rows)]
                else:
                    part = half.at[own]
                self.waiting.append(start(part, along.at[k - 1], device))
        if self.phase == 5:
            along = self.buffers[4]
            if unit.mode == "rows":
                total = self.buffers[5][z].astype(F32)
            elif unit.mode == "plain":
                index = (y * place.rows + x) * unit.block + z * unit.rows
                total = half[pl.ds(pl.multiple_of(index, 8), unit.rows), :].astype(F32)
            else:
                total = half[own, :].astype(F32)
            for k in range(place.cols - 1):
                total = total + along[k].astype(F32)
            self.out[...] = total
        self.phase += 1


class Exchange:
    def __init__(self, place, copies, plan, source, target, back):
        self.me = place.row * place.cols + place.col
        self.first, self.copies, self.cols = copies.used, copies, place.cols
        copies.used += len(plan["pairs"])
        self.pairs, self.source, self.target, self.back = plan["pairs"], source, target, back

    def listed(self):
        for number, (giver, taker, out, into, count) in enumerate(self.pairs):
            if self.back:
                giver, taker, out, into = taker, giver, into, out
            copy = pltpu.make_async_remote_copy(
                src_ref=self.source.at[pl.ds(out, count)],
                dst_ref=self.target.at[pl.ds(into, count)],
                send_sem=self.copies.send_sems.at[self.first + number],
                recv_sem=self.copies.recv_sems.at[self.first + number],
                device_id={"row": taker // self.cols, "col": taker % self.cols},
                device_id_type=MESH,
            )
            yield giver, taker, copy

    def start(self):
        for giver, taker, copy in self.listed():
            pl.when(self.me == giver)(copy.start)

    def wait(self):
        for giver, taker, copy in self.listed():
            pl.when(self.me == taker)(copy.wait_recv)

    def finish(self):
        for giver, taker, copy in self.listed():
            pl.when(self.me == giver)(copy.wait_send)


def run(kernel, inputs, outputs, scratch, number):
    names = list(inputs) + list(outputs) + list(scratch)

    def wrapped(*refs):
        kernel(dict(zip(names, refs)))

    outs = pl.pallas_call(
        wrapped,
        out_shape=[jax.ShapeDtypeStruct(shape, kind) for shape, kind, _ in outputs.values()],
        in_specs=[pl.BlockSpec(memory_space=space) for _, space in inputs.values()],
        out_specs=[pl.BlockSpec(memory_space=space) for _, _, space in outputs.values()],
        scratch_shapes=list(scratch.values()),
        compiler_params=params(collective_id=number, has_side_effects=True),
    )(*[array for array, _ in inputs.values()])
    return dict(zip(outputs, outs))


class Local:
    def __init__(self, sems):
        self.sems, self.open, self.used = sems, {}, 0

    def start(self, name, source, target):
        copy = pltpu.make_async_copy(source, target, self.sems.at[self.used])
        self.used += 1
        copy.start()
        self.open[name] = copy

    def wait(self, *names):
        for name in names:
            if name in self.open:
                self.open.pop(name).wait()

    def finish(self):
        self.wait(*list(self.open))


def units_of(shapes, ff):
    piece = shapes["qkv"][0]
    wide = shapes["fc2"][0]
    units = {"small": Unit(16, 512, "sum")}
    for name in ("q", "k", "v", "proj"):
        units[name] = Unit(piece, D, "rows")
    units["fc2"] = Unit(wide, D, "plain" if wide % 16 == 0 else "rows")
    for b in range(ff // D):
        units[f"fc1_{b}"] = Unit(piece, D, "rows")
    return units


def columns(ref, index):
    return ref.at[:, pl.ds(index * D, D)]


def attend(ref, s, p):
    at = pl.ds(pl.multiple_of(p * 128, 128), 128)
    rows = pl.ds(s * SLOT, SLOT)
    own, where, key = ref["own"][...], ref["where"][rows, :], ref["key"][rows, :]
    own2 = jnp.concatenate([own, own], axis=0)
    qs = head_halves(ref["q"][rows, at])
    spread = matmul(qs, ref["rel"][...]).astype(BF16) * own2
    group = lax.broadcasted_iota(jnp.int32, (SLOT, 128), 1) - 2 * WIN
    second = where[:, 2:3] == 1
    mark = jnp.where(((group == 0) & ~second) | ((group == 1) & second), 1.0, 0.0)
    near = matmul(spread, ref["fold"][...]) + jnp.concatenate([mark, mark], axis=0)
    left = jnp.concatenate([qs * BF16(0.125), near.astype(BF16)], axis=1)
    right = jnp.concatenate([ref["k"][rows, at], key], axis=1)
    scores = matmul_nt(left, right)
    weight = jnp.exp(scores - jnp.max(scores, axis=-1, keepdims=True))
    soft = (weight / jnp.sum(weight, axis=-1, keepdims=True)).astype(BF16)
    ref["soft"][s * PAIRS + p] = soft
    ref["o"][rows, at] = join_halves(matmul(soft, ref["v"][rows, at])).astype(BF16)


def attend_back(ref, s, p):
    at = pl.ds(pl.multiple_of(p * 128, 128), 128)
    rows = pl.ds(s * SLOT, SLOT)
    own, key = ref["own"][...], ref["key"][rows, :]
    own2 = jnp.concatenate([own, own], axis=0)
    qs, dos = head_halves(ref["q"][rows, at]), head_halves(ref["do"][rows, at])
    o = ref["o"][rows, at].astype(F32)
    soft = ref["soft"][s * PAIRS + p]
    inner = jnp.sum(dos.astype(F32) * jnp.concatenate([o, o], axis=0), axis=-1, keepdims=True)
    ds = (soft.astype(F32) * (matmul_nt(dos, ref["v"][rows, at]) - inner)).astype(BF16)
    right = jnp.concatenate([ref["k"][rows, at], key], axis=1)
    back = matmul(ds, right)
    spread = matmul_nt(back[:, 128:].astype(BF16), ref["fold"][...]).astype(BF16) * own2
    dq = back[:, :128] * 0.125 + matmul_nt(spread, ref["rel"][...])
    ref["dq"][rows, at] = join_halves(dq).astype(BF16)
    ref["drel"][...] += matmul_tn(qs, spread)
    ref["dk"][rows, at] = (matmul_tn(ds, qs) * 0.125).astype(BF16)
    ref["dv"][rows, at] = matmul_tn(soft, dos).astype(BF16)


def key_columns(ref):
    place = ref["where"][...]
    mask = ref["mask"][...]
    rows = matmul(one_hot(place[:, 3:4], mask.shape[0]), mask)
    lane = lax.broadcasted_iota(jnp.int32, rows.shape, 1)
    valid = jnp.sum(jnp.where(lane == place[:, 4:5], rows, 0.0), axis=1, keepdims=True)
    lane = lax.broadcasted_iota(jnp.int32, ref["key"].shape, 1)
    hot = (lane == place[:, 0:1]) | ((lane == place[:, 1:2] + WIN) & (place[:, 1:2] >= 0))
    group = lane - 2 * WIN
    shut = ((group == 0) | (group == 1)) & ((valid < 0.5) | (place[:, 2:3] != group))
    ref["key"][...] = jnp.where(shut, -1e30, jnp.where(hot, 1.0, 0.0)).astype(BF16)


def lane_place(rows, width, first):
    lane = lax.broadcasted_iota(jnp.int32, (rows, width), 1)
    row = lax.broadcasted_iota(jnp.int32, (rows, width), 0)
    return jnp.where(lane == row + first, 1.0, 0.0).astype(BF16)


def unpack_small(ref, blocks, piece, wide):
    vec = None
    for n in range(blocks):
        block = ref["full_small"][pl.ds(n * 16, 16), :]
        term = matmul(block[:, :piece], lane_place(piece, D, n * piece))
        vec = term if vec is None else vec + term
        if wide % 128 == 0:
            ref["b1"][:, pl.ds(n * wide, wide)] = block[:8, 128 : 128 + wide].astype(F32)
    ref["vec"][...] = vec
    if wide % 128:
        per = 128 // wide if 128 % wide == 0 else 384 // wide
        for m in range(blocks // per):
            row = None
            for j in range(per):
                block = ref["full_small"][pl.ds((m * per + j) * 16, 16), :]
                term = matmul(block[:, 128 : 128 + wide], lane_place(wide, per * wide, j * wide))
                row = term if row is None else row + term
            ref["b1"][:, pl.ds(m * per * wide, per * wide)] = row[:8]


KEPT = ["xs", "n1", "q", "k", "v", "key", "soft", "o", "dr", "do", "out", "vec", "sums", "db1"]


def first_kernel(plan, units, ff, ref):
    total, slots = plan["total"], plan["slots"]
    blocks = ff // D
    ref["dr"], ref["do"] = ref["acc"], ref["n2"]
    cells, packed, landed = ref["in_tokens"].shape[0], plan["packed"], plan["landed"]
    ref["dw_proj"], ref["dw_fc1_0"], ref["dw_fc1_1"] = (ref[f"full_{name}"] for name in "qkv")
    first = 0
    for name, size in (
        ("tokens", cells), ("cotangent", cells), ("packed0", packed), ("packed1", packed),
        ("landed0", landed), ("landed1", landed),
    ):
        ref[name] = ref["dw_fc2"].at[pl.ds(first, size)]
        first += size
    local = Local(ref["move_sems"])
    for name in ("tokens", "cotangent"):
        local.start(name, ref[f"in_{name}"], ref[name])

    def save(*names):
        for name in names:
            local.start(name, ref[name], ref[f"save_{name}"])

    for n in range(2):
        ref[f"landed{n}"][...] = jnp.zeros((landed, D), BF16)
    place = Place()
    greet(place, True)
    copies = Copies(ref["send_sems"], ref["recv_sems"])
    shard = {"small": ref["small"], "proj": ref["w_proj"], "fc2": ref["w_fc2"]}
    for n, name in enumerate("qkv"):
        shard[name] = columns(ref["w_qkv"], n)
    for b in range(blocks):
        shard[f"fc1_{b}"] = columns(ref["w_fc1"], b)
    order = ["small", "q", "k", "v", "proj", "fc2"] + [f"fc1_{b}" for b in range(blocks)]
    gathers = {
        name: Gather(
            place, copies, units[name], shard[name], ref[f"full_{name}"], ref.get(f"stage_{name}"), ref["local_sems"].at[n]
        )
        for n, name in enumerate(order)
    }
    begin = {"small": 0, "q": 0, "k": 1, "v": 2, "proj": 3, "fc2": 4}
    for b in range(blocks):
        begin[f"fc1_{b}"] = 5 + b
    clock = [0]

    def tick(until=None):
        while True:
            if until is not None and gathers[until].phase > 4:
                return
            for name in order:
                if clock[0] >= begin[name] and gathers[name].phase <= 4:
                    gathers[name].advance()
            clock[0] += 1
            if until is None:
                return

    tick()
    pick = one_hot(ref["pick"][...], cells)
    local.wait("tokens", "cotangent")
    moves = []
    for n, name in enumerate(("tokens", "cotangent")):
        ref[f"packed{n}"][...] = matmul(pick, ref[name][...]).astype(BF16)
        move = Exchange(place, copies, plan, ref[f"packed{n}"], ref[f"landed{n}"], False)
        move.start()
        moves.append(move)
    index = ref["slot_index"][...]
    here = one_hot(index, cells)
    there = one_hot(index - cells, landed)
    tick()
    for n, (name, out) in enumerate((("tokens", "xs"), ("cotangent", "gs"))):
        mine = matmul(here, ref[name][...])
        moves[n].wait()
        ref[out][...] = (mine + matmul(there, ref[f"landed{n}"][...])).astype(BF16)
    key_columns(ref)
    save("xs", "key")
    tick()
    hat, _ = normalized(ref["xs"][...].astype(F32))
    ref["r"][...] = hat
    tick("small")
    small = units["small"]
    unpack_small(ref, 2 * small.chips * small.row_count, place.cols * units["q"].rows, place.cols * units["fc2"].rows)
    vec = ref["vec"]
    ref["n1"][...] = (ref["r"][...] * vec[0:1, :] + vec[1:2, :]).astype(BF16)
    for name, bias in (("q", vec[2:3, :]), ("k", None), ("v", vec[3:4, :])):
        tick(name)
        out = matmul(ref["n1"][...], ref[f"full_{name}"][...])
        ref[name][...] = (out if bias is None else out + bias).astype(BF16)
        save(name, f"full_{name}")
    save("n1", "vec")
    for s in range(slots):
        ref["own"][...] = own_place(ref["where"][pl.ds(s * SLOT, SLOT), :])
        for third in range(2):

            @pl.loop(third * PAIRS // 2, (third + 1) * PAIRS // 2)
            def _(p):
                attend(ref, s, p)

            tick()
    save("soft", "o")
    tick("proj")
    r = ref["xs"][...].astype(F32) + matmul(ref["o"][...], ref["full_proj"][...]) + vec[4:5, :]
    ref["r"][...] = r
    hat, _ = normalized(r)
    ref["n2"][...] = (hat * vec[5:6, :] + vec[6:7, :]).astype(BF16)
    ref["acc"][...] = r + vec[7:8, :]
    for move in moves:
        move.finish()
    for name in "qkv":
        gathers[name].settle()
        local.wait(f"full_{name}")
    tick("fc2")
    scatters = []
    for b in range(blocks):
        tick(f"fc1_{b}")
        at = pl.ds(b * D, D)
        n2, g = ref["n2"][...], ref["gs"][...]
        for h in range(2):
            lanes = pl.ds(h * D // 2, D // 2)
            rows = pl.ds(b * D + h * D // 2, D // 2)
            w1, w2 = ref[f"full_fc1_{b}"][:, lanes], ref["full_fc2"][rows, :]
            u = matmul(n2, w1) + ref["b1"][0:1, rows]
            half = 0.5 + 0.5 * lax.erf(u * 0.7071067811865476)
            slope = half + u * jnp.exp(u * u * -0.5) * 0.3989422804014327
            a = (u * half).astype(BF16)
            ref["acc"][...] += matmul(a, w2)
            ref["dw_fc2"][rows, :] = matmul_tn(a, g).astype(BF16)
            du = (matmul_nt(g, w2) * slope).astype(BF16)
            ref["db1"][:, rows] = jnp.broadcast_to(column_sum(du.astype(F32)), (8, D // 2))
            ref[f"dw_fc1_{b}"][:, lanes] = matmul_tn(n2, du).astype(BF16)
            term = matmul_nt(du, w1)
            if b == 0 and h == 0:
                ref["dn2"][...] = term
            else:
                ref["dn2"][...] += term
        for scatter in scatters:
            scatter.advance()
            save(f"half_fc1_{b - 1}")
        name = f"fc1_{b}"
        scatters = [Scatter(place, copies, units[name], ref[f"dw_{name}"], ref[f"half_{name}"], None, None)]
        scatters[0].advance()
    scatters.append(Scatter(place, copies, units["fc2"], ref["dw_fc2"], ref["half_fc2"], None, None))
    scatters[1].advance()
    ref["out"][...] = ref["acc"][...].astype(BF16)
    save("out", "db1")
    hat, rate = normalized(ref["r"][...])
    dn2, g = ref["dn2"][...], ref["gs"][...].astype(F32)
    ref["sums"][...] = jnp.zeros_like(ref["sums"])
    ref["sums"][5:6, :] = column_sum(dn2 * hat)
    ref["sums"][6:7, :] = column_sum(dn2)
    ref["sums"][7:8, :] = column_sum(g)
    dr = g + norm_back(dn2, vec[5:6, :], hat, rate)
    ref["dr"][...] = dr
    db = dr.astype(BF16)
    ref["sums"][4:5, :] = column_sum(db.astype(F32))
    ref["dw_proj"][...] = matmul_tn(ref["o"][...], db).astype(BF16)
    scatters.append(Scatter(place, copies, units["proj"], ref["dw_proj"], ref["half_proj"], None, None))
    scatters[2].advance()
    ref["do"][...] = matmul_nt(db, ref["full_proj"][...]).astype(BF16)
    save("dr", "do", "sums")
    for scatter in scatters:
        scatter.advance()
    save("half_fc2", "half_proj", f"half_fc1_{blocks - 1}")
    copies.finish()
    local.finish()


def second_kernel(plan, units, ff, ref):
    slots = plan["slots"]
    blocks = ff // D
    local = Local(ref["move_sems"])
    names = [f"fc1_{b}" for b in range(blocks)] + ["fc2", "proj"]
    loaded = ["half_fc1_0", "out", "key", "q", "k", "v", "o", "do", "soft"] + [f"half_{n}" for n in names[1:]]
    loaded += ["n1", "full_q", "full_k", "full_v", "xs", "dr", "vec", "sums", "db1"]
    for name in loaded:
        local.start(name, ref[f"save_{name}"], ref[name])
    ref["landed"][...] = jnp.zeros_like(ref["landed"])
    place = Place()
    greet(place, True)
    copies = Copies(ref["send_sems"], ref["recv_sems"])
    scatters = {}

    def scatter(name, full, phase):
        buffers = [ref[f"buffer{k}_{name}"] for k in range(len(Scatter.buffer_shapes(units[name])))]
        scatters[name] = Scatter(place, copies, units[name], full, ref[f"half_{name}"], buffers, ref[f"grad_{name}"])
        scatters[name].phase = phase

    for name in names:
        scatter(name, None, 2)
    begin = {name: n for n, name in enumerate(names)}
    begin["proj"] = begin["fc2"]
    clock = [0]

    def tick():
        for name in list(scatters):
            if clock[0] >= begin[name] and scatters[name].phase <= 5:
                local.wait(f"half_{name}")
                scatters[name].advance()
        clock[0] += 1

    tick()
    cells = ref["tile_index"].shape[0]
    back_pick = one_hot(ref["back_pick"][...], ref["out"].shape[0])
    local.wait("out")
    ref["packed"][0] = matmul(back_pick, ref["out"][...]).astype(BF16)
    moves = [Exchange(place, copies, plan, ref["packed"].at[n], ref["landed"].at[n], True) for n in range(2)]
    moves[0].start()
    ref["drel"][...] = jnp.zeros_like(ref["drel"])
    local.wait("key", "q", "k", "v", "o", "do", "soft")
    for s in range(slots):
        ref["own"][...] = own_place(ref["where"][pl.ds(s * SLOT, SLOT), :])
        for third in range(2):

            @pl.loop(third * PAIRS // 2, (third + 1) * PAIRS // 2)
            def _(p):
                attend_back(ref, s, p)

            tick()
    drel = ref["drel"][:HEAD_DIM, :] + ref["drel"][HEAD_DIM:, :]
    select = ref["select"][...]
    for n in range(2):
        part = drel[:, n * (REL // 2) : (n + 1) * (REL // 2)]
        ref["held"][0, n] = lax.dot_general(
            select, part, (((1,), (1,)), ((), ())), preferred_element_type=F32, precision=lax.Precision.HIGHEST
        )
    swaps = swap_steps(place)
    state = {"step": 0, "copy": None}

    def swap():
        step = state["step"]
        if state["copy"] is not None:
            state["copy"].wait_recv()
            ref["held"][step] = ref["held"][step - 1] + ref["arriving"][step - 1]
            state["copy"] = None
        if step < len(swaps):
            state["copy"] = copies.start(ref["held"].at[step], ref["arriving"].at[step], swaps[step])
            state["step"] = step + 1
            return True
        return False

    swap()
    vec = ref["vec"]
    dn1 = None
    sums = ref["sums"]
    local.wait("n1", "full_q", "full_k", "full_v", "xs", "dr", "vec", "sums", "db1")
    for name in "qkv":
        d = ref[f"d{name}"][...]
        ref[f"dw_{name}"][...] = matmul_tn(ref["n1"][...], d).astype(BF16)
        scatter(name, ref[f"dw_{name}"], 0)
        begin[name] = 0
        tick()
        swap()
        term = matmul_nt(d, ref[f"full_{name}"][...])
        dn1 = term if dn1 is None else dn1 + term
    hat, rate = normalized(ref["xs"][...].astype(F32))
    sums[0:1, :] = column_sum(dn1 * hat)
    sums[1:2, :] = column_sum(dn1)
    sums[2:3, :] = column_sum(ref["dq"][...].astype(F32))
    sums[3:4, :] = column_sum(ref["dv"][...].astype(F32))
    small = units["small"]
    piece, wide = place.cols * units["q"].rows, place.cols * units["fc2"].rows
    ref["full_small"][...] = jnp.zeros_like(ref["full_small"])
    for n in range(2 * small.chips * small.row_count):
        rows = pl.ds(n * 16, 8)
        ref["full_small"][rows, 0:128] = matmul_nt(
            sums[...].astype(BF16), lane_place(128, D, n * piece)
        ).astype(BF16)
    for n in range(2 * small.chips * small.row_count):
        if wide % 128 == 0:
            ref["full_small"][pl.ds(n * 16, 8), 128 : 128 + wide] = ref["db1"][:, pl.ds(n * wide, wide)].astype(BF16)
        else:
            first = n * wide // 128 * 128
            span = min(round_up(n * wide + wide, 128), ff) - first
            ref["full_small"][pl.ds(n * 16, 8), 128:256] = matmul_nt(
                ref["db1"][:, pl.ds(first, span)].astype(BF16), lane_place(128, span, n * wide - first)
            ).astype(BF16)
    scatter("small", ref["full_small"], 0)
    begin["small"] = 0
    tick()
    swap()
    ref["gx"][...] = (ref["dr"][...] + norm_back(dn1, vec[0:1, :], hat, rate)).astype(BF16)
    ref["packed"][1] = matmul(back_pick, ref["gx"][...]).astype(BF16)
    moves[1].start()
    tick()
    swap()
    index = ref["tile_index"][...]
    here = one_hot(index, ref["out"].shape[0])
    there = one_hot(index - ref["out"].shape[0], ref["landed"].shape[1])
    for n, (name, tile) in enumerate((("out", "layer_out"), ("gx", "grad_tokens"))):
        mine = matmul(here, ref[name][...])
        moves[n].wait()
        ref[tile][...] = (mine + matmul(there, ref["landed"][n])).astype(BF16)
        tick()
        swap()
    while swap():
        tick()
    while any(s.phase <= 5 for s in scatters.values()):
        tick()
    ref["rel_sum"][...] = ref["held"][len(swaps)]
    copies.finish()
    for move in moves:
        move.finish()


def body(
    image_tokens, cotangent, content_mask, norm1_gain, norm1_bias, qkv_weight, query_bias, value_bias,
    rel_rows, rel_cols, proj_weight, proj_bias, norm2_gain, norm2_bias, fc1_weight, fc1_bias, fc2_weight, fc2_bias,
):
    images, rows, cols = axis_sizes()
    _, tile_rows, tile_cols, _ = image_tokens.shape
    cells = tile_rows * tile_cols
    plan = plan_windows(rows, cols, tile_rows, tile_cols)
    total, slots, packed, landed = plan["total"], plan["slots"], plan["packed"], plan["landed"]
    ff = fc1_weight.shape[1]
    blocks = ff // D
    me = lax.axis_index("row") * cols + lax.axis_index("col")
    units = units_of({"qkv": qkv_weight.shape, "fc2": fc2_weight.shape}, ff)
    names = [f"fc1_{b}" for b in range(blocks)] + ["fc2", "proj"]

    tables = [plan[t] for t in ("pack_from", "slot_from", "back_from", "tile_from")]
    joined = np.concatenate(tables + [plan["where"].reshape(rows * cols, -1)], axis=1)
    mine = lax.dynamic_index_in_dim(jnp.asarray(joined), me, keepdims=False)
    cut = np.cumsum([0] + [t.shape[1] for t in tables])
    pick, slot_index, back_pick, tile_index = (mine[cut[n] : cut[n + 1]][:, None] for n in range(4))
    where = mine[cut[4] :].reshape(total, 8)

    vectors = [norm1_gain, norm1_bias, query_bias, value_bias, proj_bias, norm2_gain, norm2_bias, fc2_bias]
    piece, wide = norm1_gain.shape[0], fc1_bias.shape[0]
    col = lax.axis_index("col")
    small = lax.dynamic_update_slice(jnp.zeros((16, 512), BF16), jnp.stack(vectors), (0, col * piece))
    small = lax.dynamic_update_slice(small, fc1_bias[None], (0, 128 + col * wide))
    rel, fold, select = rel_tables(rel_rows, rel_cols)

    vmem, anywhere = pltpu.VMEM, pl.ANY
    kept = {
        "xs": ((total, D), BF16), "n1": ((total, D), BF16), "q": ((total, D), BF16), "k": ((total, D), BF16),
        "v": ((total, D), BF16), "key": ((total, 128), BF16), "soft": ((slots * PAIRS, 2 * SLOT, SLOT), BF16),
        "o": ((total, D), BF16), "dr": ((total, D), F32), "do": ((total, D), BF16), "out": ((total, D), BF16),
        "vec": ((16, D), F32), "sums": ((8, D), F32), "db1": ((8, ff), F32),
    }
    for name in "qkv":
        kept[f"full_{name}"] = (units[name].full_shape(), BF16)
    for name in names:
        kept[f"half_{name}"] = (units[name].half_shape(), BF16)
    inputs = {
        "in_tokens": (image_tokens.reshape(cells, D), anywhere), "in_cotangent": (cotangent.reshape(cells, D), anywhere),
        "pick": (pick, vmem), "slot_index": (slot_index, vmem), "where": (where, vmem),
        "mask": (content_mask[0].astype(BF16), vmem), "rel": (rel, vmem), "fold": (fold, vmem), "small": (small, anywhere),
        "w_qkv": (qkv_weight, anywhere), "w_proj": (proj_weight, anywhere),
        "w_fc1": (fc1_weight, anywhere), "w_fc2": (fc2_weight, anywhere),
    }
    outputs = {f"save_{name}": (shape, kind, anywhere) for name, (shape, kind) in kept.items()}
    aliases = ("dr", "do")
    scratch = {name: vmem(shape, kind) for name, (shape, kind) in kept.items() if name not in aliases}
    scratch |= {
        "gs": vmem((total, D), BF16),
        "r": vmem((total, D), F32), "n2": vmem((total, D), BF16), "acc": vmem((total, D), F32),
        "dn2": vmem((total, D), F32), "own": vmem((SLOT, REL), BF16), "b1": vmem((8, ff), F32),
    }
    for name, unit in units.items():
        if f"full_{name}" not in scratch:
            scratch[f"full_{name}"] = vmem(unit.full_shape(), BF16)
        if unit.mode != "plain":
            scratch[f"stage_{name}"] = vmem(unit.stage_shape(), BF16)
        if name in names and name not in ("proj", "fc1_0", "fc1_1"):
            scratch[f"dw_{name}"] = vmem(unit.full_shape(), BF16)
    count = sum(u.gather_count() for u in units.values()) + len(names) * (images // 2) + 2 * len(plan["pairs"])
    scratch |= {
        "send_sems": pltpu.SemaphoreType.DMA((count,)), "recv_sems": pltpu.SemaphoreType.DMA((count,)),
        "local_sems": pltpu.SemaphoreType.DMA((len(units),)), "move_sems": pltpu.SemaphoreType.DMA((len(kept) + 2,)),
    }
    first = run(functools.partial(first_kernel, plan, units, ff), inputs, outputs, scratch, 0)

    inputs = {name: (array, anywhere) for name, array in first.items()}
    chosen = np.zeros((32, REL // 2), np.float32)
    chosen[: select.shape[0]] = select
    inputs |= {
        "back_pick": (back_pick, vmem), "tile_index": (tile_index, vmem), "where": (where, vmem),
        "rel": (rel, vmem), "fold": (fold, vmem), "select": (jnp.asarray(chosen), vmem),
    }
    outputs = {"layer_out": ((cells, D), BF16, vmem), "grad_tokens": ((cells, D), BF16, vmem)}
    for name, unit in units.items():
        outputs[f"grad_{name}"] = ((unit.rows, unit.width), F32, vmem)
    outputs["rel_sum"] = ((2, 32, HEAD_DIM), F32, vmem)
    swaps = (images * rows * cols).bit_length() - 1
    scratch = {name: vmem(shape, kind) for name, (shape, kind) in kept.items()}
    scratch |= {
        "dq": vmem((total, D), BF16), "dk": vmem((total, D), BF16), "dv": vmem((total, D), BF16),
        "gx": vmem((total, D), BF16), "drel": vmem((2 * HEAD_DIM, REL), F32), "own": vmem((SLOT, REL), BF16),
        "held": vmem((swaps + 1, 2, 32, HEAD_DIM), F32), "arriving": vmem((swaps, 2, 32, HEAD_DIM), F32),
        "packed": vmem((2, landed, D), BF16), "landed": vmem((2, packed, D), BF16),
        "full_small": vmem(units["small"].full_shape(), BF16), "half_small": vmem(units["small"].half_shape(), BF16),
    }
    for name in "qkv":
        scratch[f"dw_{name}"] = vmem(units[name].full_shape(), BF16)
        scratch[f"half_{name}"] = vmem(units[name].half_shape(), BF16)
    for name, unit in units.items():
        for n, buffer in enumerate(Scatter.buffer_shapes(unit)):
            scratch[f"buffer{n}_{name}"] = buffer
    count = sum(u.scatter_count() for u in units.values()) + swaps + 2 * len(plan["pairs"])
    scratch |= {
        "send_sems": pltpu.SemaphoreType.DMA((count,)), "recv_sems": pltpu.SemaphoreType.DMA((count,)),
        "move_sems": pltpu.SemaphoreType.DMA((len(kept),)),
    }
    second = run(functools.partial(second_kernel, plan, units, ff), inputs, outputs, scratch, 1)

    def lanes(first, size):
        return lax.dynamic_slice(second["grad_small"], (0, first + col * size), (8, size))

    g_vec, g_b1 = lanes(0, piece), lanes(128, wide)[0]
    g_qkv = jnp.concatenate([second[f"grad_{name}"] for name in "qkv"], axis=1)
    g_fc1 = jnp.concatenate([second[f"grad_fc1_{b}"] for b in range(blocks)], axis=1)
    span = rel_rows.shape[0]
    return (
        second["layer_out"].reshape(image_tokens.shape), second["grad_tokens"].reshape(image_tokens.shape),
        g_vec[0], g_vec[1], g_qkv, g_vec[2], g_vec[3], second["rel_sum"][0, :span], second["rel_sum"][1, :span],
        second["grad_proj"], g_vec[4], g_vec[5], g_vec[6], g_fc1, g_b1, second["grad_fc2"], g_vec[7],
    )


def solution(mesh):
    everywhere = ("img", "row", "col")
    tile, vector, matrix = P("img", "row", "col", None), P(everywhere), P(everywhere, None)
    in_specs = (
        tile, tile, P("img", None, None), vector, vector, matrix, vector, vector, P(), P(),
        matrix, vector, vector, vector, matrix, vector, matrix, vector,
    )
    out_specs = (
        tile, tile, vector, vector, matrix, vector, vector, P(), P(),
        matrix, vector, vector, vector, matrix, vector, matrix, vector,
    )
    return jax.shard_map(body, mesh=mesh, in_specs=in_specs, out_specs=out_specs, check_vma=False)
```

```python
import functools
import types

import jax
import jax.numpy as jnp
import numpy as np
from jax import lax
from jax.experimental import pallas as pl
from jax.experimental.pallas import tpu as pltpu
from jax.sharding import PartitionSpec as P

D = 768
HEADS = 12
HEAD_DIM = 64
PAIRS = HEADS // 2
WIN = 14
CELLS = WIN * WIN
SLOT = 208
MESH = pl.DeviceIdType.MESH
F32 = jnp.float32
BF16 = jnp.bfloat16
VMEM_LIMIT = 62 * 2**20


def round_up(value, unit):
    return -(-value // unit) * unit


def plan_windows(rows, cols, tile_rows, tile_cols):
    devices = rows * cols
    height, width = rows * tile_rows, cols * tile_cols
    windows = []
    for top in range(0, height, WIN):
        for left in range(0, width, WIN):
            windows.append(
                [
                    (r, c, r - top, c - left)
                    for r in range(top, min(top + WIN, height))
                    for c in range(left, min(left + WIN, width))
                ]
            )
    bins = []
    for window in sorted(windows, key=len, reverse=True):
        for held in bins:
            if len(held) < 2 and sum(map(len, held)) + len(window) <= CELLS:
                held.append(window)
                break
        else:
            bins.append([window])
    slots = -(-len(bins) // devices)
    while len(bins) < slots * devices:
        bins.append([])

    def home(cell):
        return cell[0] // tile_rows * cols + cell[1] // tile_cols

    weights = np.zeros((len(bins), devices), np.int64)
    for number, held in enumerate(bins):
        for window in held:
            for cell in window:
                weights[number, home(cell)] += 1
    hops = np.zeros((devices, devices, rows * rows * cols + cols * cols * rows))
    for source in range(devices):
        for target in range(devices):
            r0, c0, r1, c1 = source // cols, source % cols, target // cols, target % cols
            step = 1 if r1 > r0 else -1
            for r in range(r0, r1, step):
                hops[source, target, (r * rows + r + step) * cols + c0] = 1
            step = 1 if c1 > c0 else -1
            for c in range(c0, c1, step):
                hops[source, target, rows * rows * cols + (c * cols + c + step) * rows + r1] = 1
    loads = np.einsum("bs,sdl->bdl", weights, hops)

    def cost(order):
        load = loads[np.arange(len(bins)), np.array(order) // slots].sum(axis=0)
        return load.max() * 100 + load.sum()

    order = [0] * len(bins)
    free = [slots] * devices
    for number in range(len(bins)):
        options = [d for d in range(devices) if free[d]]
        best = min(options, key=lambda d: (loads[number, d].sum(), d))
        order[number] = best * slots + slots - free[best]
        free[best] -= 1
    current = cost(order)
    while True:
        found = None
        for a in range(len(bins)):
            for b in range(a):
                if order[a] // slots != order[b] // slots:
                    order[a], order[b] = order[b], order[a]
                    trial = cost(order)
                    if trial < current:
                        current, found = trial, (a, b)
                    order[a], order[b] = order[b], order[a]
        if found is None:
            break
        a, b = found
        order[a], order[b] = order[b], order[a]
    total = slots * SLOT
    place = [[] for _ in range(devices)]
    for number in sorted(range(len(bins)), key=lambda n: order[n]):
        device, slot = order[number] // slots, order[number] % slots
        position = slot * SLOT
        for group, window in enumerate(bins[number]):
            for cell in window:
                place[device].append((position, cell, group))
                position += 1
    cells = tile_rows * tile_cols
    pairs = []
    sent, got = [0] * devices, [0] * devices
    moved = {}
    for source in range(devices):
        for target in range(devices):
            if source != target:
                listed = [e for e in place[target] if home(e[1]) == source]
                if listed:
                    count = round_up(len(listed), 16)
                    pairs.append((source, target, sent[source], got[target], count))
                    moved[source, target] = (listed, sent[source], got[target])
                    sent[source] += count
                    got[target] += count
    packed, landed = round_up(max(sent), 128), round_up(max(got), 128)
    pack_from = np.full((devices, packed), -1, np.int32)
    slot_from = np.full((devices, total), -1, np.int32)
    back_from = np.full((devices, landed), -1, np.int32)
    tile_from = np.full((devices, cells), -1, np.int32)
    where = np.full((devices, total, 8), -1, np.int32)
    for device in range(devices):
        for position, cell, group in place[device]:
            where[device, position, :5] = (cell[2], cell[3], group, cell[0], cell[1])
            if home(cell) == device:
                local = cell[0] % tile_rows * tile_cols + cell[1] % tile_cols
                slot_from[device, position] = local
                tile_from[device, local] = position
    for (source, target), (listed, out, into) in moved.items():
        for k, (position, cell, group) in enumerate(listed):
            local = cell[0] % tile_rows * tile_cols + cell[1] % tile_cols
            pack_from[source, out + k] = local
            slot_from[target, position] = cells + into + k
            back_from[target, into + k] = position
            tile_from[source, local] = total + out + k
    return dict(
        slots=slots, total=total, pairs=pairs, packed=packed, landed=landed, where=where,
        pack_from=pack_from, slot_from=slot_from, back_from=back_from, tile_from=tile_from,
    )


def matmul(a, b):
    return jnp.dot(a, b, preferred_element_type=F32)


def matmul_nt(a, b):
    return lax.dot_general(a, b, (((1,), (1,)), ((), ())), preferred_element_type=F32)


def matmul_tn(a, b):
    return lax.dot_general(a, b, (((0,), (0,)), ((), ())), preferred_element_type=F32)


def one_hot(index, width):
    return (index == lax.broadcasted_iota(jnp.int32, (index.shape[0], width), 1)).astype(BF16)


def normalized(values):
    offset = values - jnp.mean(values, axis=-1, keepdims=True)
    rate = lax.rsqrt(jnp.mean(offset * offset, axis=-1, keepdims=True) + 1e-06)
    return offset * rate, rate


def norm_back(cotangent, gain, hat, rate):
    e = cotangent * gain
    mean_e = jnp.mean(e, axis=-1, keepdims=True)
    mean_eh = jnp.mean(e * hat, axis=-1, keepdims=True)
    return rate * (e - mean_e - hat * mean_eh)


def column_sum(values):
    return jnp.sum(values, axis=0, keepdims=True)


def params(**more):
    return pltpu.CompilerParams(vmem_limit_bytes=VMEM_LIMIT, **more)


def head_halves(pair):
    low = lax.broadcasted_iota(jnp.int32, pair.shape, 1) < HEAD_DIM
    zero = jnp.zeros_like(pair)
    return jnp.concatenate([jnp.where(low, pair, zero), jnp.where(low, zero, pair)], axis=0)


def join_halves(stacked):
    low = lax.broadcasted_iota(jnp.int32, (SLOT, 2 * HEAD_DIM), 1) < HEAD_DIM
    return jnp.where(low, stacked[:SLOT], stacked[SLOT:])


REL = 512


def axis_sizes():
    return lax.axis_size("img"), lax.axis_size("row"), lax.axis_size("col")


class Place:
    def __init__(self):
        images, self.rows, self.cols = axis_sizes()
        self.chips = images // 2
        img = lax.axis_index("img")
        self.chip, self.core = img // 2, img % 2
        self.row, self.col = lax.axis_index("row"), lax.axis_index("col")

    def other(self, axis, k):
        if axis == "row":
            index = (self.row + k) % self.rows
            return index, {"row": index}
        if axis == "col":
            index = (self.col + k) % self.cols
            return index, {"col": index}
        index = (self.chip + k) % self.chips
        return index, {"img": index * 2 + self.core}

    def sibling(self):
        return {"img": self.chip * 2 + 1 - self.core}

    def count(self, axis):
        return {"row": self.rows, "col": self.cols, "chip": self.chips}[axis]


def greet(place, image_wide):
    barrier = pltpu.get_barrier_semaphore()
    heard = 1
    pl.semaphore_signal(barrier, inc=1, device_id=place.sibling(), device_id_type=MESH)
    for k in range(1, place.chips):
        pl.semaphore_signal(barrier, inc=1, device_id=place.other("img", k)[1], device_id_type=MESH)
        heard += 1
    for r in range(place.rows):
        for c in range(place.cols):
            if (r, c) == (0, 0) or not (image_wide or r == 0 or c == 0):
                continue
            target = {"row": (place.row + r) % place.rows, "col": (place.col + c) % place.cols}
            pl.semaphore_signal(barrier, inc=1, device_id=target, device_id_type=MESH)
            heard += 1
    pl.semaphore_wait(barrier, heard)


class Copies:
    def __init__(self, send_sems, recv_sems):
        self.send_sems, self.recv_sems = send_sems, recv_sems
        self.used = 0

    def start(self, source, target, device):
        copy = pltpu.make_async_remote_copy(
            src_ref=source,
            dst_ref=target,
            send_sem=self.send_sems.at[self.used],
            recv_sem=self.recv_sems.at[self.used],
            device_id=device,
            device_id_type=MESH,
        )
        self.used += 1
        copy.start()
        return copy


def swap_steps(place):
    steps = [place.sibling()]
    bit = 1
    while bit < place.chips:
        flip = place.chip + bit - 2 * bit * (place.chip // bit % 2)
        steps.append({"img": flip * 2 + place.core})
        bit *= 2
    bit = 1
    while bit < place.rows:
        steps.append({"row": place.row + bit - 2 * bit * (place.row // bit % 2)})
        bit *= 2
    bit = 1
    while bit < place.cols:
        steps.append({"col": place.col + bit - 2 * bit * (place.col // bit % 2)})
        bit *= 2
    return steps


SMALL, Q, K, V, PROJ, FC2, FC1 = range(7)
ROWS, PLAIN, SUM = range(3)
ALONG, ACROSS, CORES = range(3)


class Unit:
    def __init__(self, rows, width, mode):
        self.rows, self.width, self.mode = rows, width, mode
        images, self.row_count, self.col_count = axis_sizes()
        self.chips = images // 2
        self.block = rows if mode == SUM else rows * self.col_count
        self.line = self.block * self.row_count
        self.half = width // 2
        self.low, self.high = pl.ds(0, self.half), pl.ds(self.half, width - self.half)
        self.size = 2 * self.chips * self.line * width / (D * D)

    def full_shape(self):
        return (2 * self.chips * self.line, self.width)

    def half_shape(self):
        return (self.chips * self.line, self.width)

    def stage_shape(self):
        return (self.col_count, self.rows, self.width)

    def buffer_shapes(self):
        c, r, n = self.chips, self.row_count, self.col_count
        return [
            (c - 1, self.line, self.half),
            (r - 1, c, self.block, self.half),
            (r - 1, self.block, self.half),
            (c - 1, self.block, self.half),
            (n - 1, self.rows, self.width),
        ]

    def rows_at(self, index, count=1):
        return pl.ds(pl.multiple_of(index * self.block, 8), count * self.block)

    def copies(self):
        c, r, n = self.chips, self.row_count, self.col_count
        return 2 * ((n - 1) + (r - 1) + (c - 1) + (c - 1) + (r - 1) * c + c)

    def spread(self, k):
        row = lax.broadcasted_iota(jnp.int32, (self.block, self.rows), 0)
        col = lax.broadcasted_iota(jnp.int32, (self.block, self.rows), 1)
        return jnp.where(row == col + k * self.rows, 1.0, 0.0).astype(BF16)


class Phased:
    last = 4

    def __init__(self, place, copies):
        self.place, self.copies = place, copies
        self.phase, self.waiting, self.sent = 0, [], []

    @property
    def done(self):
        return self.phase > self.last

    def send(self, source, target, device):
        copy = self.copies.start(source, target, device)
        self.waiting.append(copy)
        self.sent.append(copy)

    def advance(self):
        for copy in self.waiting:
            copy.wait_recv()
        self.waiting = []
        self.step()
        self.phase += 1

    def settle(self):
        for copy in self.sent:
            copy.wait_send()
        self.sent = []


class Gather(Phased):
    def __init__(self, place, copies, unit, shard, full, stage, local):
        super().__init__(place, copies)
        self.unit, self.shard, self.full, self.stage, self.local = unit, shard, full, stage, local

    def cost(self):
        size = self.unit.size
        return [(ALONG, 3.3 * size), (ACROSS, 1.7 * size), (ACROSS, 3.3 * size), (CORES, 0.95 * size), None][self.phase - 1]

    def step(self):
        place, unit, full = self.place, self.unit, self.full
        y, c, x, z = place.chip, place.core, place.row, place.col
        own = unit.rows_at((y * 2 + c) * place.rows + x)
        if self.phase == 0:
            if unit.mode == PLAIN:
                first = ((y * 2 + c) * place.rows + x) * unit.block + z * unit.rows
                target = full.at[pl.ds(pl.multiple_of(first, 8), unit.rows)]
            else:
                target = self.stage.at[z]
            self.keep = pltpu.make_async_copy(self.shard, target, self.local)
            self.keep.start()
            for k in range(1, place.cols):
                self.send(self.shard, target, place.other("col", k)[1])
        if self.phase == 1:
            self.keep.wait()
            if unit.mode != PLAIN:
                total = None
                for k in range(place.cols):
                    slab = self.stage[k]
                    term = slab.astype(F32) if unit.mode == SUM else matmul(unit.spread(k), slab)
                    total = term if total is None else total + term
                full[own, :] = total.astype(BF16)
            for k in range(1, place.rows):
                part = full.at[own, unit.low]
                self.send(part, part, place.other("row", k)[1])
            for k in range(1, place.chips):
                part = full.at[own, unit.high]
                self.send(part, part, place.other("img", k)[1])
        if self.phase == 2:
            for k in range(1, place.chips):
                part = full.at[unit.rows_at((y * 2 + c) * place.rows, place.rows), unit.low]
                self.send(part, part, place.other("img", k)[1])
            for k in range(1, place.rows):
                for chip in range(place.chips):
                    part = full.at[unit.rows_at((chip * 2 + c) * place.rows + x), unit.high]
                    self.send(part, part, place.other("row", k)[1])
        if self.phase == 3:
            for chip in range(place.chips):
                part = full.at[unit.rows_at((chip * 2 + c) * place.rows, place.rows)]
                self.send(part, part, place.sibling())


def add_to(ref, at, terms):
    total = ref[at].astype(F32)
    for term in terms:
        total = total + term.astype(F32)
    ref[at] = total.astype(BF16)


class Scatter(Phased):
    def __init__(self, place, copies, unit, full, half, buffers, cut, out):
        super().__init__(place, copies)
        self.unit, self.full, self.half, self.buffers, self.cut, self.out = unit, full, half, buffers, cut, out

    def cost(self):
        size = self.unit.size
        return [(CORES, 0.95 * size), (ACROSS, 3.3 * size), (ACROSS, 1.7 * size), (ALONG, 3.3 * size), None][self.phase - 1]

    def step(self):
        place, unit, half = self.place, self.unit, self.half
        y, c, x, z = place.chip, place.core, place.row, place.col
        low_chip, high_row, low_row, high_chip, along = self.buffers
        own = unit.rows_at(y * place.rows + x)

        def slab(index):
            if unit.mode == ROWS:
                return self.cut, index
            if unit.mode == SUM:
                return half, own
            first = (y * place.rows + x) * unit.block + index * unit.rows
            return half, pl.ds(pl.multiple_of(first, 8), unit.rows)

        if self.phase == 0:
            for chip in range(place.chips):
                part = self.full.at[unit.rows_at((chip * 2 + 1 - c) * place.rows, place.rows)]
                self.send(part, half.at[unit.rows_at(chip * place.rows, place.rows)], place.sibling())
        if self.phase == 1:
            for chip in range(place.chips):
                for row in range(place.rows):
                    term = self.full[unit.rows_at((chip * 2 + c) * place.rows + row), :]
                    add_to(half, (unit.rows_at(chip * place.rows + row), slice(None)), [term])
            for k in range(1, place.chips):
                to, device = place.other("img", k)
                part = half.at[unit.rows_at(to * place.rows, place.rows), unit.low]
                self.send(part, low_chip.at[k - 1], device)
            for k in range(1, place.rows):
                to, device = place.other("row", k)
                for chip in range(place.chips):
                    part = half.at[unit.rows_at(chip * place.rows + to), unit.high]
                    self.send(part, high_row.at[k - 1, chip], device)
        if self.phase == 2:
            for row in range(place.rows):
                rows = pl.ds(row * unit.block, unit.block)
                terms = [low_chip[k, rows, :] for k in range(place.chips - 1)]
                add_to(half, (unit.rows_at(y * place.rows + row), unit.low), terms)
            for chip in range(place.chips):
                terms = [high_row[k, chip] for k in range(place.rows - 1)]
                add_to(half, (unit.rows_at(chip * place.rows + x), unit.high), terms)
            for k in range(1, place.rows):
                to, device = place.other("row", k)
                self.send(half.at[unit.rows_at(y * place.rows + to), unit.low], low_row.at[k - 1], device)
            for k in range(1, place.chips):
                to, device = place.other("img", k)
                self.send(half.at[unit.rows_at(to * place.rows + x), unit.high], high_chip.at[k - 1], device)
        if self.phase == 3:
            add_to(half, (own, unit.low), [low_row[k] for k in range(place.rows - 1)])
            add_to(half, (own, unit.high), [high_chip[k] for k in range(place.chips - 1)])
            if unit.mode == ROWS:
                block = half[own, :]
                for k in range(place.cols):
                    self.cut[k] = matmul_tn(unit.spread(k), block).astype(BF16)
            for k in range(1, place.cols):
                to, device = place.other("col", k)
                ref, at = slab(to)
                self.send(ref.at[at], along.at[k - 1], device)
        if self.phase == 4:
            ref, at = slab(z)
            total = ref[at].astype(F32)
            for k in range(place.cols - 1):
                total = total + along[k].astype(F32)
            self.out[...] = total


class Doubling(Phased):
    def __init__(self, place, copies, held, arriving):
        super().__init__(place, copies)
        self.held, self.arriving = held, arriving
        self.partners = swap_steps(place)
        self.last = len(self.partners)

    def cost(self):
        return None if self.done else (CORES, 0.5)

    def step(self):
        n = self.phase
        if n > 0:
            self.held[n] = self.held[n - 1] + self.arriving[n - 1]
        if n < len(self.partners):
            self.send(self.held.at[n], self.arriving.at[n], self.partners[n])


class Exchange:
    def __init__(self, place, copies, plan, source, target, back):
        self.me = place.row * place.cols + place.col
        self.first, self.copies, self.cols = copies.used, copies, place.cols
        copies.used += len(plan["pairs"])
        self.pairs, self.source, self.target, self.back = plan["pairs"], source, target, back

    def listed(self):
        for number, (giver, taker, out, into, count) in enumerate(self.pairs):
            if self.back:
                giver, taker, out, into = taker, giver, into, out
            copy = pltpu.make_async_remote_copy(
                src_ref=self.source.at[pl.ds(out, count)],
                dst_ref=self.target.at[pl.ds(into, count)],
                send_sem=self.copies.send_sems.at[self.first + number],
                recv_sem=self.copies.recv_sems.at[self.first + number],
                device_id={"row": taker // self.cols, "col": taker % self.cols},
                device_id_type=MESH,
            )
            yield giver, taker, copy

    def start(self):
        for giver, taker, copy in self.listed():
            pl.when(self.me == giver)(copy.start)

    def wait(self):
        for giver, taker, copy in self.listed():
            pl.when(self.me == taker)(copy.wait_recv)

    def finish(self):
        for giver, taker, copy in self.listed():
            pl.when(self.me == giver)(copy.wait_send)


class Timeline:
    def __init__(self):
        self.now, self.free, self.flying, self.queue = 0.0, [0.0, 0.0, 0.0], [], []

    def launch(self, op):
        op.advance()
        if not op.done:
            server, time = op.cost()
            self.free[server] = max(self.free[server], self.now) + time
            self.flying.append((self.free[server] + 2.0, len(self.flying), op))

    def next_up(self):
        entry = min(self.flying, key=lambda e: e[:2])
        self.flying.remove(entry)
        return entry

    def poll(self):
        while True:
            while self.queue and self.free[ALONG] < self.now + 5.0:
                self.launch(self.queue.pop(0))
            if not self.flying or min(e[0] for e in self.flying) > self.now:
                return
            self.launch(self.next_up()[2])

    def spend(self, time):
        self.now += time
        self.poll()

    def need(self, *ops):
        while not all(op.done for op in ops):
            if not self.flying:
                self.launch(self.queue.pop(0))
                continue
            entry = self.next_up()
            self.now = max(self.now, entry[0])
            self.launch(entry[2])
            self.poll()

    def finish(self):
        while self.flying:
            entry = self.next_up()
            self.now = max(self.now, entry[0])
            self.launch(entry[2])


class Item:
    def __init__(self, value, kind=None, space=pltpu.VMEM):
        self.value, self.kind, self.space = value, kind, space


def run(kernel, inputs, outputs, scratch):
    leaves, tree = jax.tree.flatten((inputs, outputs, scratch))
    ins, outs = jax.tree.leaves(inputs), jax.tree.leaves(outputs)

    def wrapped(*refs):
        named = jax.tree.unflatten(tree, refs)
        kernel(types.SimpleNamespace(**named[0], **named[1], **named[2]))

    results = pl.pallas_call(
        wrapped,
        out_shape=[jax.ShapeDtypeStruct(item.value, item.kind) for item in outs],
        in_specs=[pl.BlockSpec(memory_space=item.space) for item in ins],
        out_specs=[pl.BlockSpec(memory_space=item.space) for item in outs],
        scratch_shapes=[
            item.value if item.kind is None else item.space(item.value, item.kind) for item in leaves[len(ins) + len(outs) :]
        ],
        compiler_params=params(collective_id=0, has_side_effects=True),
    )(*[item.value for item in ins])
    return types.SimpleNamespace(**jax.tree.unflatten(jax.tree.structure(outputs), results))


def lane_place(rows, width, first):
    lane = lax.broadcasted_iota(jnp.int32, (rows, width), 1)
    row = lax.broadcasted_iota(jnp.int32, (rows, width), 0)
    return jnp.where(lane == row + first, 1.0, 0.0).astype(BF16)


def slot_rows(s):
    return pl.ds(pl.multiple_of(s * SLOT, SLOT), SLOT)


def pair_lanes(p):
    return pl.ds(pl.multiple_of(p * 128, 128), 128)


def attend(m, s, p):
    rows, at = slot_rows(s), pair_lanes(p)
    own2 = jnp.concatenate([m.own[...], m.own[...]], axis=0)
    qs = head_halves(m.q[rows, at])
    spread = matmul(qs, m.rel[...]).astype(BF16) * own2
    group = lax.broadcasted_iota(jnp.int32, (SLOT, 128), 1) - 2 * WIN
    second = m.table[rows, 2:3] == 1
    mark = jnp.where(((group == 0) & ~second) | ((group == 1) & second), 1.0, 0.0)
    near = matmul(spread, m.fold[...]) + jnp.concatenate([mark, mark], axis=0)
    left = jnp.concatenate([qs * BF16(0.125), near.astype(BF16)], axis=1)
    right = jnp.concatenate([m.k[rows, at], m.key[rows, :]], axis=1)
    scores = matmul_nt(left, right)
    weight = jnp.exp(scores - jnp.max(scores, axis=-1, keepdims=True))
    soft = (weight / jnp.sum(weight, axis=-1, keepdims=True)).astype(BF16)
    m.soft[s * PAIRS + p] = soft
    m.o[rows, at] = join_halves(matmul(soft, m.v[rows, at])).astype(BF16)


def attend_back(m, s, p):
    rows, at = slot_rows(s), pair_lanes(p)
    own2 = jnp.concatenate([m.own[...], m.own[...]], axis=0)
    qs, dos = head_halves(m.q[rows, at]), head_halves(m.do[rows, at])
    o = m.o[rows, at].astype(F32)
    soft = m.soft[s * PAIRS + p]
    inner = jnp.sum(dos.astype(F32) * jnp.concatenate([o, o], axis=0), axis=-1, keepdims=True)
    ds = (soft.astype(F32) * (matmul_nt(dos, m.v[rows, at]) - inner)).astype(BF16)
    right = jnp.concatenate([m.k[rows, at], m.key[rows, :]], axis=1)
    back = matmul(ds, right)
    spread = matmul_nt(back[:, 128:].astype(BF16), m.fold[...]).astype(BF16) * own2
    dq = back[:, :128] * 0.125 + matmul_nt(spread, m.rel[...])
    m.dq[rows, at] = join_halves(dq).astype(BF16)
    m.drel[...] += matmul_tn(qs, spread)
    m.dk[rows, at] = (matmul_tn(ds, qs) * 0.125).astype(BF16)
    m.dv[rows, at] = matmul_tn(soft, dos).astype(BF16)


def own_place(table):
    lane = lax.broadcasted_iota(jnp.int32, (SLOT, REL), 1)
    row, col = table[:, 0:1], table[:, 1:2]
    first, second = row * WIN, REL // 2 + col * WIN
    hot = (lane >= first) & (lane < first + WIN) & (row >= 0)
    hot = hot | ((lane >= second) & (lane < second + WIN) & (col >= 0))
    return jnp.where(hot, 1.0, 0.0).astype(BF16)


def key_columns(m, total):
    place = m.table[0:total, :]
    mask = m.mask[...].astype(F32).astype(BF16)
    rows = matmul(one_hot(place[:, 3:4], mask.shape[0]), mask)
    lane = lax.broadcasted_iota(jnp.int32, rows.shape, 1)
    valid = jnp.sum(jnp.where(lane == place[:, 4:5], rows, 0.0), axis=1, keepdims=True)
    lane = lax.broadcasted_iota(jnp.int32, m.key.shape, 1)
    hot = (lane == place[:, 0:1]) | ((lane == place[:, 1:2] + WIN) & (place[:, 1:2] >= 0))
    group = lane - 2 * WIN
    shut = ((group == 0) | (group == 1)) & ((valid < 0.5) | (place[:, 2:3] != group))
    m.key[...] = jnp.where(shut, -1e30, jnp.where(hot, 1.0, 0.0)).astype(BF16)


def pack_small(m, place, piece, wide):
    flat = m.vectors[...].astype(F32)
    count = flat.shape[1]
    lane = lax.broadcasted_iota(jnp.int32, (16, count), 1)
    row = lax.broadcasted_iota(jnp.int32, (16, count), 0)
    lines = jnp.where(lane // piece == row, flat, 0.0)
    lines = jnp.where((row < 8) | (lane >= 8 * piece), lines, 0.0)
    lines = jnp.where((lane >= 8 * piece) & (row != 0), 0.0, jnp.where((lane >= 8 * piece), flat, lines)).astype(BF16)
    source = lax.broadcasted_iota(jnp.int32, (count, 512), 0)
    target = lax.broadcasted_iota(jnp.int32, (count, 512), 1)
    first = jnp.where(
        source < 8 * piece, source % piece + place.col * piece, source - 8 * piece + 128 + place.col * wide
    )
    m.small[...] = matmul(lines, jnp.where(first == target, 1.0, 0.0).astype(BF16)).astype(BF16)


def unpack_small(m, blocks, piece, wide):
    full = m.full[SMALL]
    vec = None
    for n in range(blocks):
        term = matmul(full[pl.ds(n * 16, 16), 0:piece], lane_place(piece, D, n * piece))
        vec = term if vec is None else vec + term
    m.vec[...] = vec
    per = 1 if wide % 128 == 0 else 4
    for n in range(0, blocks, per):
        row = None
        for j in range(per):
            block = full[pl.ds((n + j) * 16, 16), 128 : 128 + wide]
            term = block.astype(F32) if per == 1 else matmul(block, lane_place(wide, per * wide, j * wide))
            row = term if row is None else row + term
        m.b1[:, pl.ds(n * wide, per * wide)] = row[:8]


def split_small(m, blocks, piece, wide, ff):
    full = m.grad_small
    sums, db1 = m.sums[...].astype(BF16), m.db1[...].astype(BF16)
    full[...] = jnp.zeros_like(full)
    for n in range(blocks):
        rows = pl.ds(n * 16, 8)
        full[rows, 0:128] = matmul_nt(sums, lane_place(128, D, n * piece)).astype(BF16)
        if wide % 128 == 0:
            full[rows, 128 : 128 + wide] = db1[:, n * wide : (n + 1) * wide]
        else:
            first = n * wide // 128 * 128
            last = min(round_up(n * wide + wide, 128), ff)
            place = lane_place(128, last - first, n * wide - first)
            full[rows, 128:256] = matmul_nt(db1[:, first:last], place).astype(BF16)


def pick_cells(target, table, column, near, far, step):
    @pl.loop(0, target.shape[0] // step)
    def _(n):
        rows = pl.ds(pl.multiple_of(n * step, 16), step)
        index = table[rows, column : column + 1]
        here, there = one_hot(index, near.shape[0]), one_hot(index - near.shape[0], far.shape[0])
        target[rows, :] = (matmul(here, near[...]) + matmul(there, far[...])).astype(BF16)


def layer_kernel(plan, units, m):
    total, slots = plan["total"], plan["slots"]
    packed, landed = plan["packed"], plan["landed"]
    blocks = len(units) - FC1
    cells = m.in_tokens.shape[0]
    first = 0
    early = []
    for size in (cells, cells, packed, packed, landed, landed):
        early.append(m.dw_fc2.at[pl.ds(first, size)])
        first += size
    tiles, packets, arrivals = early[:2], early[2:4], early[4:]
    m.acc, m.do, m.gx = m.dr, m.n2, m.xs
    late = [m.full[FC2].at[pl.ds(n * total, total)] for n in range(4)]
    m.dq, m.dk, m.dv, m.out = late
    back_packets = [m.full[FC2].at[pl.ds(4 * total, landed)], m.full[FC2].at[pl.ds(0, landed)]]
    grads = {Q: m.full[FC1], K: m.full[FC1 + 1], V: m.full[FC1 + 2], PROJ: m.full[FC1 + 3], FC2: m.dw_fc2, SMALL: m.grad_small}
    for b in range(blocks):
        grads[FC1 + b] = m.dw_fc1[b]

    place = Place()
    me = place.row * place.cols + place.col
    table = pltpu.make_async_copy(m.in_table.at[me], m.table, m.local_sems.at[len(units)])
    table.start()
    loads = []
    for n, source in enumerate((m.in_tokens, m.in_cotangent)):
        loads.append(pltpu.make_async_copy(source, tiles[n], m.local_sems.at[len(units) + 1 + n]))
        loads[n].start()
    for n in range(2):
        arrivals[n][...] = jnp.zeros((landed, D), BF16)
        m.back_arrivals[n][...] = jnp.zeros((packed, D), BF16)
    piece, wide = units[Q].rows, units[FC2].rows
    pack_small(m, place, piece, wide)
    greet(place, True)
    copies = Copies(m.send_sems, m.recv_sems)
    line = Timeline()

    shards = {SMALL: m.small, PROJ: m.w_proj, FC2: m.w_fc2}
    for part in (Q, K, V):
        shards[part] = m.w_qkv.at[:, pl.ds((part - Q) * D, D)]
    for b in range(blocks):
        shards[FC1 + b] = m.w_fc1.at[:, pl.ds(b * D, D)]
    gathers = [
        Gather(place, copies, units[n], shards[n], m.full[n], m.stage[n], m.local_sems.at[n]) for n in range(len(units))
    ]
    outs = {PROJ: m.g_proj, FC2: m.g_fc2, SMALL: m.g_small}
    for part in (Q, K, V):
        outs[part] = m.g_qkv.at[:, pl.ds((part - Q) * D, D)]
    for b in range(blocks):
        outs[FC1 + b] = m.g_fc1.at[:, pl.ds(b * D, D)]
    scatters = {}

    def scatter(n):
        scatters[n] = Scatter(place, copies, units[n], grads[n], m.half[n], m.buffers[n], m.stage[n], outs[n])
        line.launch(scatters[n])

    line.queue = list(gathers)
    for n in range(2):
        line.launch(line.queue.pop(0))
    table.wait()
    loads[0].wait()
    loads[1].wait()
    moves = []
    for n in range(2):
        packets[n][...] = matmul(one_hot(m.table[0:packed, 6:7], cells), tiles[n][...]).astype(BF16)
        moves.append(Exchange(place, copies, plan, packets[n], arrivals[n], False))
        moves[n].start()
        line.spend(2.0)
    m.fold[...] = fold_matrix()
    rel = jnp.concatenate([matmul_tn(r[...], m.select[...]).astype(BF16) for r in (m.rel_rows, m.rel_cols)], axis=1)
    m.rel[...] = jnp.concatenate([rel, rel], axis=0)
    key_columns(m, total)
    line.spend(2.0)
    for n, target in enumerate((m.xs, m.gs)):
        moves[n].wait()
        pick_cells(target, m.table, 5, tiles[n], arrivals[n], SLOT)
        line.spend(3.0)
    line.need(gathers[SMALL])
    small = units[SMALL]
    line_count = 2 * small.chips * small.row_count
    unpack_small(m, line_count, place.cols * piece, place.cols * wide)
    vec = m.vec

    @pl.loop(0, slots)
    def _(s):
        rows = slot_rows(s)
        hat, _ = normalized(m.xs[rows, :].astype(F32))
        m.n1[rows, :] = (hat * vec[0:1, :] + vec[1:2, :]).astype(BF16)

    line.spend(3.0)
    for n, target, bias in ((Q, m.q, vec[2:3, :]), (K, m.k, None), (V, m.v, vec[3:4, :])):
        line.need(gathers[n])
        for h in range(3):
            lanes = pl.ds(h * (D // 3), D // 3)
            out = matmul(m.n1[...], m.full[n][:, lanes])
            target[:, lanes] = (out if bias is None else out + bias[:, lanes.start : lanes.start + D // 3]).astype(BF16)
        line.spend(1.5)

    def pairs_of(s, part, function):
        first = part * PAIRS // 2

        @pl.loop(first, first + PAIRS // 2)
        def _(p):
            function(m, s, p)

    for s in range(slots):
        m.own[...] = own_place(m.table[slot_rows(s), :])
        for part in range(2):
            pairs_of(s, part, attend)
            line.spend(3.2)
    line.need(gathers[PROJ])

    @pl.loop(0, slots)
    def _(s):
        rows = slot_rows(s)
        r = m.xs[rows, :].astype(F32) + matmul(m.o[rows, :], m.full[PROJ][...]) + vec[4:5, :]
        m.r[rows, :] = r
        hat, _ = normalized(r)
        m.n2[rows, :] = (hat * vec[5:6, :] + vec[6:7, :]).astype(BF16)
        m.acc[rows, :] = r + vec[7:8, :]

    line.spend(4.5)
    for move in moves:
        move.finish()
    line.need(gathers[FC2])
    thirds = 3
    size = D // thirds
    for b in range(blocks):
        line.need(gathers[FC1 + b])
        for h in range(thirds):
            lanes, rows = pl.ds(h * size, size), pl.ds(b * D + h * size, size)
            w1, w2 = m.full[FC1 + b][:, lanes], m.full[FC2][rows, :]
            u = matmul(m.n2[...], w1) + m.b1[0:1, rows]
            half = 0.5 + 0.5 * lax.erf(u * 0.7071067811865476)
            a = (u * half).astype(BF16)
            m.acc[...] += matmul(a, w2)
            m.dw_fc2[rows, :] = matmul_tn(a, m.gs[...]).astype(BF16)
            slope = half + u * jnp.exp(u * u * -0.5) * 0.3989422804014327
            du = (matmul_nt(m.gs[...], w2) * slope).astype(BF16)
            m.db1[:, rows] = jnp.broadcast_to(column_sum(du.astype(F32)), (8, size))
            m.dw_fc1[b][:, lanes] = matmul_tn(m.n2[...], du).astype(BF16)
            term = matmul_nt(du, w1)
            if b == 0 and h == 0:
                m.dn2[...] = term
            else:
                m.dn2[...] += term
            line.spend(2.2)
        scatter(FC1 + b)
    for gather in gathers:
        gather.settle()
    scatter(FC2)

    m.sums[...] = jnp.zeros_like(m.sums)

    @pl.loop(0, slots)
    def _(s):
        rows = slot_rows(s)
        m.out[rows, :] = m.acc[rows, :].astype(BF16)
        hat, rate = normalized(m.r[rows, :])
        dn2, g = m.dn2[rows, :], m.gs[rows, :].astype(F32)
        m.sums[5:6, :] += column_sum(dn2 * hat)
        m.sums[6:7, :] += column_sum(dn2)
        m.sums[7:8, :] += column_sum(g)
        dr = g + norm_back(dn2, vec[5:6, :], hat, rate)
        m.dr[rows, :] = dr
        m.sums[4:5, :] += column_sum(dr.astype(BF16).astype(F32))

    line.spend(3.5)
    db = m.dr[...].astype(BF16)
    grads[PROJ][...] = matmul_tn(m.o[...], db).astype(BF16)
    scatter(PROJ)
    m.do[...] = matmul_nt(db, m.full[PROJ][...]).astype(BF16)
    line.spend(4.0)
    back_packets[0][...] = matmul(one_hot(m.table[0:landed, 7:8], total), m.out[...]).astype(BF16)
    moves = [Exchange(place, copies, plan, back_packets[n], m.back_arrivals[n], True) for n in range(2)]
    moves[0].start()
    line.spend(1.5)

    m.drel[...] = jnp.zeros_like(m.drel)
    for s in range(slots):
        m.own[...] = own_place(m.table[slot_rows(s), :])
        for part in range(2):
            pairs_of(s, part, attend_back)
            line.spend(3.4)
    drel = m.drel[:HEAD_DIM, :] + m.drel[HEAD_DIM:, :]
    for n in range(2):
        part = drel[:, n * (REL // 2) : (n + 1) * (REL // 2)]
        m.held[0, n] = lax.dot_general(
            m.select[...].astype(F32), part, (((1,), (1,)), ((), ())), preferred_element_type=F32,
            precision=lax.Precision.HIGHEST,
        )
    doubling = Doubling(place, copies, m.held, m.arriving)
    line.launch(doubling)

    for n, d in ((Q, m.dq), (K, m.dk), (V, m.dv)):
        grads[n][...] = matmul_tn(m.n1[...], d[...]).astype(BF16)
        scatter(n)
        line.spend(2.0)
    dn1 = m.dn2
    for n, d in ((Q, m.dq), (K, m.dk), (V, m.dv)):
        term = matmul_nt(d[...], m.full[n][...])
        if n == Q:
            dn1[...] = term
        else:
            dn1[...] += term
        line.spend(1.7)

    @pl.loop(0, slots)
    def _(s):
        rows = slot_rows(s)
        hat, rate = normalized(m.xs[rows, :].astype(F32))
        d = dn1[rows, :]
        m.sums[0:1, :] += column_sum(d * hat)
        m.sums[1:2, :] += column_sum(d)
        m.sums[2:3, :] += column_sum(m.dq[rows, :].astype(F32))
        m.sums[3:4, :] += column_sum(m.dv[rows, :].astype(F32))
        m.gx[rows, :] = (m.dr[rows, :] + norm_back(d, vec[0:1, :], hat, rate)).astype(BF16)

    back_packets[1][...] = matmul(one_hot(m.table[0:landed, 7:8], total), m.gx[...]).astype(BF16)
    moves[1].start()
    line.spend(4.5)
    split_small(m, line_count, place.cols * piece, place.cols * wide, blocks * D)
    scatter(SMALL)
    stores = []
    results = [m.dk, m.dv]
    for n, source in enumerate((m.out, m.gx)):
        moves[n].wait()
        tile = results[n].at[pl.ds(0, cells)]
        pick_cells(tile, m.table, 8, source, m.back_arrivals[n], 128)
        stores.append(pltpu.make_async_copy(tile, (m.layer_out, m.grad_tokens)[n], m.local_sems.at[n]))
        stores[n].start()
        line.spend(2.0)
    line.finish()
    m.rel_sum[...] = m.held[doubling.last]
    lane_pick = lane_place(512, 512, -place.col * piece)
    lane_pick2 = lane_place(512, 512, -128 - place.col * wide)
    for target, picked in ((m.g_vec, lane_pick), (m.g_b1, lane_pick2)):
        target[...] = jnp.dot(
            m.g_small[...], picked[:, : target.shape[1]].astype(F32),
            preferred_element_type=F32, precision=lax.Precision.HIGHEST,
        )
    for op in [*scatters.values(), doubling]:
        op.settle()
    for move in moves:
        move.finish()
    for store in stores:
        store.wait()


def fold_matrix():
    row = lax.broadcasted_iota(jnp.int32, (REL, 128), 0)
    lane = lax.broadcasted_iota(jnp.int32, (REL, 128), 1)
    half = REL // 2
    inside = jnp.where(row < half, row, row - half)
    target = inside % WIN + jnp.where(row < half, 0, WIN)
    return jnp.where((lane == target) & (inside < CELLS), 1.0, 0.0).astype(BF16)


def body(
    image_tokens, cotangent, content_mask, norm1_gain, norm1_bias, qkv_weight, query_bias, value_bias,
    rel_rows, rel_cols, proj_weight, proj_bias, norm2_gain, norm2_bias, fc1_weight, fc1_bias, fc2_weight, fc2_bias,
):
    images, rows, cols = axis_sizes()
    _, tile_rows, tile_cols, _ = image_tokens.shape
    cells = tile_rows * tile_cols
    plan = plan_windows(rows, cols, tile_rows, tile_cols)
    total, slots, packed, landed = plan["total"], plan["slots"], plan["packed"], plan["landed"]
    piece, wide, ff = qkv_weight.shape[0], fc2_weight.shape[0], fc1_weight.shape[1]
    blocks = ff // D
    line = Unit(piece, D, ROWS)
    units = [Unit(16, 512, SUM), line, line, line, line, Unit(wide, D, ROWS if wide % 16 else PLAIN)] + [line] * blocks

    height = max(total, packed, landed, cells)
    table = np.full((rows * cols, height, 16), -1, np.int32)
    table[:, :total, :5] = plan["where"][:, :, :5]
    for n, name in enumerate(("slot_from", "pack_from", "back_from", "tile_from")):
        table[:, : plan[name].shape[1], 5 + n] = plan[name]
    index = np.arange(WIN)[:, None] - np.arange(WIN)[None, :] + WIN - 1
    span = rel_rows.shape[0]
    select = np.zeros((span, REL // 2), np.float32)
    select[index.reshape(-1), np.arange(CELLS)] = 1
    vectors = [norm1_gain, norm1_bias, query_bias, value_bias, proj_bias, norm2_gain, norm2_bias, fc2_bias, fc1_bias]

    def everywhere(value):
        return Item(value, space=pl.ANY)

    def vmem(*shape, kind=BF16):
        return Item(shape, kind)

    inputs = dict(
        in_tokens=everywhere(image_tokens.reshape(cells, D)), in_cotangent=everywhere(cotangent.reshape(cells, D)),
        in_table=everywhere(jnp.asarray(table)), mask=Item(content_mask[0]), vectors=Item(jnp.concatenate(vectors)[None]),
        rel_rows=Item(rel_rows), rel_cols=Item(rel_cols), select=Item(jnp.asarray(select, BF16)),
        w_qkv=everywhere(qkv_weight), w_proj=everywhere(proj_weight), w_fc1=everywhere(fc1_weight), w_fc2=everywhere(fc2_weight),
    )
    outputs = dict(
        layer_out=Item((cells, D), BF16, pl.ANY), grad_tokens=Item((cells, D), BF16, pl.ANY),
        g_qkv=vmem(piece, 3 * D, kind=F32), g_proj=vmem(piece, D, kind=F32),
        g_fc1=vmem(piece, ff, kind=F32), g_fc2=vmem(wide, D, kind=F32),
        g_vec=vmem(16, 128, kind=F32), g_b1=vmem(16, round_up(wide, 128), kind=F32), rel_sum=vmem(2, span, HEAD_DIM, kind=F32),
    )
    swaps = (images * rows * cols).bit_length() - 1
    count = sum(u.copies() for u in units) + swaps + 4 * len(plan["pairs"])
    sems = pltpu.SemaphoreType.DMA
    scratch = dict(
        table=vmem(height, 16, kind=jnp.int32), small=vmem(16, 512), rel=vmem(2 * HEAD_DIM, REL), fold=vmem(REL, 128),
        xs=vmem(total, D), gs=vmem(total, D), n1=vmem(total, D), q=vmem(total, D), k=vmem(total, D), v=vmem(total, D),
        key=vmem(total, 128), soft=vmem(slots * PAIRS, 2 * SLOT, SLOT), o=vmem(total, D), n2=vmem(total, D),
        r=vmem(total, D, kind=F32), dr=vmem(total, D, kind=F32), dn2=vmem(total, D, kind=F32), own=vmem(SLOT, REL),
        vec=vmem(16, D, kind=F32), b1=vmem(8, ff, kind=F32), db1=vmem(8, ff, kind=F32), sums=vmem(8, D, kind=F32),
        drel=vmem(2 * HEAD_DIM, REL, kind=F32), held=vmem(swaps + 1, 2, span, HEAD_DIM, kind=F32),
        arriving=vmem(swaps, 2, span, HEAD_DIM, kind=F32), g_small=vmem(16, 512, kind=F32),
        grad_small=vmem(*units[SMALL].full_shape()), back_arrivals=[vmem(packed, D)] * 2,
        full=[vmem(*u.full_shape()) for u in units], half=[vmem(*u.half_shape()) for u in units],
        stage=[vmem(*(u.stage_shape() if u.mode != PLAIN else (8, 128))) for u in units],
        buffers=[[vmem(*shape) for shape in u.buffer_shapes()] for u in units],
        dw_fc1=[vmem(*line.full_shape())] * blocks, dw_fc2=vmem(*units[FC2].full_shape()),
        send_sems=Item(sems((count,))), recv_sems=Item(sems((count,))), local_sems=Item(sems((len(units) + 3,))),
    )
    done = run(functools.partial(layer_kernel, plan, units), inputs, outputs, scratch)
    g_vec, g_b1 = done.g_vec[:8, :piece], done.g_b1[0, :wide]
    return (
        done.layer_out.reshape(image_tokens.shape), done.grad_tokens.reshape(image_tokens.shape),
        g_vec[0], g_vec[1], done.g_qkv, g_vec[2], g_vec[3], done.rel_sum[0], done.rel_sum[1],
        done.g_proj, g_vec[4], g_vec[5], g_vec[6], done.g_fc1, g_b1, done.g_fc2, g_vec[7],
    )


def solution(mesh):
    everywhere = ("img", "row", "col")
    tile, vector, matrix = P("img", "row", "col", None), P(everywhere), P(everywhere, None)
    in_specs = (
        tile, tile, P("img", None, None), vector, vector, matrix, vector, vector, P(), P(),
        matrix, vector, vector, vector, matrix, vector, matrix, vector,
    )
    out_specs = (
        tile, tile, vector, vector, matrix, vector, vector, P(), P(),
        matrix, vector, vector, vector, matrix, vector, matrix, vector,
    )
    return jax.shard_map(body, mesh=mesh, in_specs=in_specs, out_specs=out_specs, check_vma=False)
```

```python
import functools
import types

import jax
import jax.numpy as jnp
import numpy as np
from jax import lax
from jax.experimental import pallas as pl
from jax.experimental.pallas import tpu as pltpu
from jax.sharding import PartitionSpec as P

D = 768
HEADS = 12
HEAD_DIM = 64
PAIRS = HEADS // 2
WIN = 14
CELLS = WIN * WIN
SLOT = 208
MESH = pl.DeviceIdType.MESH
F32 = jnp.float32
BF16 = jnp.bfloat16
VMEM_LIMIT = 62 * 2**20


def round_up(value, unit):
    return -(-value // unit) * unit


def plan_windows(rows, cols, tile_rows, tile_cols):
    devices = rows * cols
    height, width = rows * tile_rows, cols * tile_cols
    windows = []
    for top in range(0, height, WIN):
        for left in range(0, width, WIN):
            windows.append(
                [
                    (r, c, r - top, c - left)
                    for r in range(top, min(top + WIN, height))
                    for c in range(left, min(left + WIN, width))
                ]
            )
    bins = []
    for window in sorted(windows, key=len, reverse=True):
        for held in bins:
            if len(held) < 2 and sum(map(len, held)) + len(window) <= CELLS:
                held.append(window)
                break
        else:
            bins.append([window])
    slots = -(-len(bins) // devices)
    while len(bins) < slots * devices:
        bins.append([])

    def home(cell):
        return cell[0] // tile_rows * cols + cell[1] // tile_cols

    weights = np.zeros((len(bins), devices), np.int64)
    for number, held in enumerate(bins):
        for window in held:
            for cell in window:
                weights[number, home(cell)] += 1
    hops = np.zeros((devices, devices, rows * rows * cols + cols * cols * rows))
    for source in range(devices):
        for target in range(devices):
            r0, c0, r1, c1 = source // cols, source % cols, target // cols, target % cols
            step = 1 if r1 > r0 else -1
            for r in range(r0, r1, step):
                hops[source, target, (r * rows + r + step) * cols + c0] = 1
            step = 1 if c1 > c0 else -1
            for c in range(c0, c1, step):
                hops[source, target, rows * rows * cols + (c * cols + c + step) * rows + r1] = 1
    loads = np.einsum("bs,sdl->bdl", weights, hops)

    def cost(order):
        load = loads[np.arange(len(bins)), np.array(order) // slots].sum(axis=0)
        return load.max() * 100 + load.sum()

    order = [0] * len(bins)
    free = [slots] * devices
    for number in range(len(bins)):
        options = [d for d in range(devices) if free[d]]
        best = min(options, key=lambda d: (loads[number, d].sum(), d))
        order[number] = best * slots + slots - free[best]
        free[best] -= 1
    current = cost(order)
    while True:
        found = None
        for a in range(len(bins)):
            for b in range(a):
                if order[a] // slots != order[b] // slots:
                    order[a], order[b] = order[b], order[a]
                    trial = cost(order)
                    if trial < current:
                        current, found = trial, (a, b)
                    order[a], order[b] = order[b], order[a]
        if found is None:
            break
        a, b = found
        order[a], order[b] = order[b], order[a]
    total = slots * SLOT
    place = [[] for _ in range(devices)]
    for number in sorted(range(len(bins)), key=lambda n: order[n]):
        device, slot = order[number] // slots, order[number] % slots
        position = slot * SLOT
        for group, window in enumerate(bins[number]):
            for cell in window:
                place[device].append((position, cell, group))
                position += 1
    cells = tile_rows * tile_cols
    pairs = []
    sent, got = [0] * devices, [0] * devices
    moved = {}
    for source in range(devices):
        for target in range(devices):
            if source != target:
                listed = [e for e in place[target] if home(e[1]) == source]
                if listed:
                    count = round_up(len(listed), 16)
                    pairs.append((source, target, sent[source], got[target], count))
                    moved[source, target] = (listed, sent[source], got[target])
                    sent[source] += count
                    got[target] += count
    packed, landed = round_up(max(sent), 128), round_up(max(got), 128)
    pack_from = np.full((devices, packed), -1, np.int32)
    slot_from = np.full((devices, total), -1, np.int32)
    back_from = np.full((devices, landed), -1, np.int32)
    tile_from = np.full((devices, cells), -1, np.int32)
    where = np.full((devices, total, 8), -1, np.int32)
    for device in range(devices):
        for position, cell, group in place[device]:
            where[device, position, :5] = (cell[2], cell[3], group, cell[0], cell[1])
            if home(cell) == device:
                local = cell[0] % tile_rows * tile_cols + cell[1] % tile_cols
                slot_from[device, position] = local
                tile_from[device, local] = position
    for (source, target), (listed, out, into) in moved.items():
        for k, (position, cell, group) in enumerate(listed):
            local = cell[0] % tile_rows * tile_cols + cell[1] % tile_cols
            pack_from[source, out + k] = local
            slot_from[target, position] = cells + into + k
            back_from[target, into + k] = position
            tile_from[source, local] = total + out + k
    return dict(
        slots=slots, total=total, pairs=pairs, packed=packed, landed=landed, where=where,
        pack_from=pack_from, slot_from=slot_from, back_from=back_from, tile_from=tile_from,
    )


def matmul(a, b):
    return jnp.dot(a, b, preferred_element_type=F32)


def matmul_nt(a, b):
    return lax.dot_general(a, b, (((1,), (1,)), ((), ())), preferred_element_type=F32)


def matmul_tn(a, b):
    return lax.dot_general(a, b, (((0,), (0,)), ((), ())), preferred_element_type=F32)


def one_hot(index, width):
    return (index == lax.broadcasted_iota(jnp.int32, (index.shape[0], width), 1)).astype(BF16)


def normalized(values):
    offset = values - jnp.mean(values, axis=-1, keepdims=True)
    rate = lax.rsqrt(jnp.mean(offset * offset, axis=-1, keepdims=True) + 1e-06)
    return offset * rate, rate


def norm_back(cotangent, gain, hat, rate):
    e = cotangent * gain
    mean_e = jnp.mean(e, axis=-1, keepdims=True)
    mean_eh = jnp.mean(e * hat, axis=-1, keepdims=True)
    return rate * (e - mean_e - hat * mean_eh)


def column_sum(values):
    return jnp.sum(values, axis=0, keepdims=True)


def params(**more):
    return pltpu.CompilerParams(vmem_limit_bytes=VMEM_LIMIT, **more)


def head_halves(pair):
    low = lax.broadcasted_iota(jnp.int32, pair.shape, 1) < HEAD_DIM
    zero = jnp.zeros_like(pair)
    return jnp.concatenate([jnp.where(low, pair, zero), jnp.where(low, zero, pair)], axis=0)


def join_halves(stacked):
    low = lax.broadcasted_iota(jnp.int32, (SLOT, 2 * HEAD_DIM), 1) < HEAD_DIM
    return jnp.where(low, stacked[:SLOT], stacked[SLOT:])


REL = 512


def axis_sizes():
    return lax.axis_size("img"), lax.axis_size("row"), lax.axis_size("col")


class Place:
    def __init__(self):
        images, self.rows, self.cols = axis_sizes()
        self.chips = images // 2
        img = lax.axis_index("img")
        self.chip, self.core = img // 2, img % 2
        self.row, self.col = lax.axis_index("row"), lax.axis_index("col")

    def other(self, axis, k):
        if axis == "row":
            index = (self.row + k) % self.rows
            return index, {"row": index}
        if axis == "col":
            index = (self.col + k) % self.cols
            return index, {"col": index}
        index = (self.chip + k) % self.chips
        return index, {"img": index * 2 + self.core}

    def sibling(self):
        return {"img": self.chip * 2 + 1 - self.core}

    def count(self, axis):
        return {"row": self.rows, "col": self.cols, "chip": self.chips}[axis]


def greet(place):
    barrier = pltpu.get_barrier_semaphore()
    heard = 1
    pl.semaphore_signal(barrier, inc=1, device_id=place.sibling(), device_id_type=MESH)
    for k in range(1, place.chips):
        pl.semaphore_signal(barrier, inc=1, device_id=place.other("img", k)[1], device_id_type=MESH)
        heard += 1
    for r in range(place.rows):
        for c in range(place.cols):
            if (r, c) == (0, 0):
                continue
            target = {"row": (place.row + r) % place.rows, "col": (place.col + c) % place.cols}
            pl.semaphore_signal(barrier, inc=1, device_id=target, device_id_type=MESH)
            heard += 1
    return heard


class Copies:
    def __init__(self, send_sems, recv_sems):
        self.send_sems, self.recv_sems = send_sems, recv_sems
        self.used = 0

    def start(self, source, target, device):
        copy = pltpu.make_async_remote_copy(
            src_ref=source,
            dst_ref=target,
            send_sem=self.send_sems.at[self.used],
            recv_sem=self.recv_sems.at[self.used],
            device_id=device,
            device_id_type=MESH,
        )
        self.used += 1
        copy.start()
        return copy


def swap_steps(place):
    steps = [place.sibling()]
    bit = 1
    while bit < place.chips:
        flip = place.chip + bit - 2 * bit * (place.chip // bit % 2)
        steps.append({"img": flip * 2 + place.core})
        bit *= 2
    bit = 1
    while bit < place.rows:
        steps.append({"row": place.row + bit - 2 * bit * (place.row // bit % 2)})
        bit *= 2
    bit = 1
    while bit < place.cols:
        steps.append({"col": place.col + bit - 2 * bit * (place.col // bit % 2)})
        bit *= 2
    return steps


SMALL, QKV, _, _, PROJ, FC2, FC1 = range(7)
ROWS, PLAIN, SUM = range(3)
ALONG, ACROSS, CORES = range(3)


class Unit:
    def __init__(self, rows, width, mode):
        self.rows, self.width, self.mode = rows, width, mode
        images, self.row_count, self.col_count = axis_sizes()
        self.chips = images // 2
        self.block = rows if mode == SUM else rows * self.col_count
        self.line = self.block * self.row_count
        self.half = width // 2
        self.low, self.high = pl.ds(0, self.half), pl.ds(self.half, width - self.half)
        self.size = 2 * self.chips * self.line * width / (D * D)

    def full_shape(self):
        return (2 * self.chips * self.line, self.width)

    def half_shape(self):
        return (self.chips * self.line, self.width)

    def stage_shape(self):
        return (self.col_count, self.rows, self.width)

    def buffer_shapes(self):
        c, r, n = self.chips, self.row_count, self.col_count
        return [
            (c - 1, self.line, self.half),
            (r - 1, c, self.block, self.half),
            (r - 1, self.block, self.half),
            (c - 1, self.block, self.half),
            (n - 1, self.rows, self.width),
        ]

    def rows_at(self, index, count=1):
        return pl.ds(pl.multiple_of(index * self.block, 8), count * self.block)

    def copies(self):
        c, r, n = self.chips, self.row_count, self.col_count
        return 2 * ((n - 1) + (r - 1) + (c - 1) + (c - 1) + (r - 1) * c + c)

    def spread(self, k):
        row = lax.broadcasted_iota(jnp.int32, (self.block, self.rows), 0)
        col = lax.broadcasted_iota(jnp.int32, (self.block, self.rows), 1)
        return jnp.where(row == col + k * self.rows, 1.0, 0.0).astype(BF16)


class Phased:
    last = 4

    def __init__(self, place, copies):
        self.place, self.copies = place, copies
        self.phase, self.waiting, self.sent = 0, [], []

    @property
    def done(self):
        return self.phase > self.last

    def send(self, source, target, device):
        copy = self.copies.start(source, target, device)
        self.waiting.append(copy)
        self.sent.append(copy)

    def advance(self):
        for copy in self.waiting:
            copy.wait_recv()
        self.waiting = []
        self.step()
        self.phase += 1

    def settle(self):
        for copy in self.sent:
            copy.wait_send()
        self.sent = []


class Gather(Phased):
    def __init__(self, place, copies, unit, shard, full, stage, local):
        super().__init__(place, copies)
        self.unit, self.shard, self.full, self.stage, self.local = unit, shard, full, stage, local

    def cost(self):
        size = self.unit.size
        return [(ALONG, 3.3 * size), (ACROSS, 1.7 * size), (ACROSS, 3.3 * size), (CORES, 0.95 * size), None][self.phase - 1]

    def step(self):
        place, unit, full = self.place, self.unit, self.full
        y, c, x, z = place.chip, place.core, place.row, place.col
        own = unit.rows_at((y * 2 + c) * place.rows + x)
        if self.phase == 0:
            if unit.mode == PLAIN:
                first = ((y * 2 + c) * place.rows + x) * unit.block + z * unit.rows
                target = full.at[pl.ds(pl.multiple_of(first, 8), unit.rows)]
            else:
                target = self.stage.at[z]
            self.keep = pltpu.make_async_copy(self.shard, target, self.local)
            self.keep.start()
            for k in range(1, place.cols):
                self.send(self.shard, target, place.other("col", k)[1])
        if self.phase == 1:
            self.keep.wait()
            if unit.mode != PLAIN:
                total = None
                for k in range(place.cols):
                    slab = self.stage[k]
                    term = slab.astype(F32) if unit.mode == SUM else matmul(unit.spread(k), slab)
                    total = term if total is None else total + term
                full[own, :] = total.astype(BF16)
            for k in range(1, place.rows):
                part = full.at[own, unit.low]
                self.send(part, part, place.other("row", k)[1])
            for k in range(1, place.chips):
                part = full.at[own, unit.high]
                self.send(part, part, place.other("img", k)[1])
        if self.phase == 2:
            for k in range(1, place.chips):
                part = full.at[unit.rows_at((y * 2 + c) * place.rows, place.rows), unit.low]
                self.send(part, part, place.other("img", k)[1])
            for k in range(1, place.rows):
                for chip in range(place.chips):
                    part = full.at[unit.rows_at((chip * 2 + c) * place.rows + x), unit.high]
                    self.send(part, part, place.other("row", k)[1])
        if self.phase == 3:
            for chip in range(place.chips):
                part = full.at[unit.rows_at((chip * 2 + c) * place.rows, place.rows)]
                self.send(part, part, place.sibling())


def add_to(ref, at, terms):
    total = ref[at].astype(F32)
    for term in terms:
        total = total + term.astype(F32)
    ref[at] = total.astype(BF16)


class Scatter(Phased):
    def __init__(self, place, copies, unit, full, half, buffers, cut, out):
        super().__init__(place, copies)
        self.unit, self.full, self.half, self.buffers, self.cut, self.out = unit, full, half, buffers, cut, out

    def cost(self):
        size = self.unit.size
        return [(CORES, 0.95 * size), (ACROSS, 3.3 * size), (ACROSS, 1.7 * size), (ALONG, 3.3 * size), None][self.phase - 1]

    def step(self):
        place, unit, half = self.place, self.unit, self.half
        y, c, x, z = place.chip, place.core, place.row, place.col
        low_chip, high_row, low_row, high_chip, along = self.buffers
        own = unit.rows_at(y * place.rows + x)

        def slab(index):
            if unit.mode == ROWS:
                return self.cut, index
            if unit.mode == SUM:
                return half, own
            first = (y * place.rows + x) * unit.block + index * unit.rows
            return half, pl.ds(pl.multiple_of(first, 8), unit.rows)

        if self.phase == 0:
            for chip in range(place.chips):
                part = self.full.at[unit.rows_at((chip * 2 + 1 - c) * place.rows, place.rows)]
                self.send(part, half.at[unit.rows_at(chip * place.rows, place.rows)], place.sibling())
        if self.phase == 1:
            for chip in range(place.chips):
                for row in range(place.rows):
                    term = self.full[unit.rows_at((chip * 2 + c) * place.rows + row), :]
                    add_to(half, (unit.rows_at(chip * place.rows + row), slice(None)), [term])
            for k in range(1, place.chips):
                to, device = place.other("img", k)
                part = half.at[unit.rows_at(to * place.rows, place.rows), unit.low]
                self.send(part, low_chip.at[k - 1], device)
            for k in range(1, place.rows):
                to, device = place.other("row", k)
                for chip in range(place.chips):
                    part = half.at[unit.rows_at(chip * place.rows + to), unit.high]
                    self.send(part, high_row.at[k - 1, chip], device)
        if self.phase == 2:
            for row in range(place.rows):
                rows = pl.ds(row * unit.block, unit.block)
                terms = [low_chip[k, rows, :] for k in range(place.chips - 1)]
                add_to(half, (unit.rows_at(y * place.rows + row), unit.low), terms)
            for chip in range(place.chips):
                terms = [high_row[k, chip] for k in range(place.rows - 1)]
                add_to(half, (unit.rows_at(chip * place.rows + x), unit.high), terms)
            for k in range(1, place.rows):
                to, device = place.other("row", k)
                self.send(half.at[unit.rows_at(y * place.rows + to), unit.low], low_row.at[k - 1], device)
            for k in range(1, place.chips):
                to, device = place.other("img", k)
                self.send(half.at[unit.rows_at(to * place.rows + x), unit.high], high_chip.at[k - 1], device)
        if self.phase == 3:
            add_to(half, (own, unit.low), [low_row[k] for k in range(place.rows - 1)])
            add_to(half, (own, unit.high), [high_chip[k] for k in range(place.chips - 1)])
            if unit.mode == ROWS:
                block = half[own, :]
                for k in range(place.cols):
                    self.cut[k] = matmul_tn(unit.spread(k), block).astype(BF16)
            for k in range(1, place.cols):
                to, device = place.other("col", k)
                ref, at = slab(to)
                self.send(ref.at[at], along.at[k - 1], device)
        if self.phase == 4:
            ref, at = slab(z)
            total = ref[at].astype(F32)
            for k in range(place.cols - 1):
                total = total + along[k].astype(F32)
            first = 0
            for out in self.out:
                out[...] = total[:, first : first + out.shape[1]]
                first += out.shape[1]


class Doubling(Phased):
    def __init__(self, place, copies, held, arriving):
        super().__init__(place, copies)
        self.held, self.arriving = held, arriving
        self.partners = swap_steps(place)
        self.last = len(self.partners)

    def cost(self):
        return None if self.done else (CORES, 0.5)

    def step(self):
        n = self.phase
        if n > 0:
            self.held[n] = self.held[n - 1] + self.arriving[n - 1]
        if n < len(self.partners):
            self.send(self.held.at[n], self.arriving.at[n], self.partners[n])


class Exchange:
    def __init__(self, place, copies, plan, source, target, back):
        self.me = place.row * place.cols + place.col
        self.first, self.copies, self.cols = copies.used, copies, place.cols
        copies.used += len(plan["pairs"])
        self.pairs, self.source, self.target, self.back = plan["pairs"], source, target, back

    def listed(self):
        for number, (giver, taker, out, into, count) in enumerate(self.pairs):
            if self.back:
                giver, taker, out, into = taker, giver, into, out
            copy = pltpu.make_async_remote_copy(
                src_ref=self.source.at[pl.ds(out, count)],
                dst_ref=self.target.at[pl.ds(into, count)],
                send_sem=self.copies.send_sems.at[self.first + number],
                recv_sem=self.copies.recv_sems.at[self.first + number],
                device_id={"row": taker // self.cols, "col": taker % self.cols},
                device_id_type=MESH,
            )
            yield giver, taker, copy

    def start(self):
        for giver, taker, copy in self.listed():
            pl.when(self.me == giver)(copy.start)

    def wait(self):
        for giver, taker, copy in self.listed():
            pl.when(self.me == taker)(copy.wait_recv)

    def finish(self):
        for giver, taker, copy in self.listed():
            pl.when(self.me == giver)(copy.wait_send)


class Timeline:
    def __init__(self):
        self.now, self.free, self.flying, self.queue = 0.0, [0.0, 0.0, 0.0], [], []

    def load(self, server, time):
        self.free[server] = max(self.free[server], self.now) + time

    def need_time(self, time):
        if self.now < time:
            self.spend(time - self.now)

    def launch(self, op):
        op.advance()
        if not op.done:
            server, time = op.cost()
            self.free[server] = max(self.free[server], self.now) + time
            self.flying.append((self.free[server] + 3.0, len(self.flying), op))

    def next_up(self):
        entry = min(self.flying, key=lambda e: e[:2])
        self.flying.remove(entry)
        return entry

    def poll(self):
        while True:
            while self.queue and self.free[ALONG] < self.now:
                self.launch(self.queue.pop(0))
            if not self.flying or min(e[0] for e in self.flying) > self.now:
                return
            self.launch(self.next_up()[2])

    def spend(self, time):
        self.now += time
        self.poll()

    def need(self, *ops):
        while not all(op.done for op in ops):
            if not self.flying:
                self.launch(self.queue.pop(0))
                continue
            entry = self.next_up()
            self.now = max(self.now, entry[0])
            self.launch(entry[2])
            self.poll()

    def finish(self):
        while self.flying:
            entry = self.next_up()
            self.now = max(self.now, entry[0])
            self.launch(entry[2])


class Item:
    def __init__(self, value, kind=None, space=pltpu.VMEM):
        self.value, self.kind, self.space = value, kind, space


def run(kernel, inputs, outputs, scratch):
    leaves, tree = jax.tree.flatten((inputs, outputs, scratch))
    ins, outs = jax.tree.leaves(inputs), jax.tree.leaves(outputs)

    def wrapped(*refs):
        named = jax.tree.unflatten(tree, refs)
        kernel(types.SimpleNamespace(**named[0], **named[1], **named[2]))

    results = pl.pallas_call(
        wrapped,
        out_shape=[jax.ShapeDtypeStruct(item.value, item.kind) for item in outs],
        in_specs=[pl.BlockSpec(memory_space=item.space) for item in ins],
        out_specs=[pl.BlockSpec(memory_space=item.space) for item in outs],
        scratch_shapes=[
            item.value if item.kind is None else item.space(item.value, item.kind) for item in leaves[len(ins) + len(outs) :]
        ],
        compiler_params=params(collective_id=0, has_side_effects=True),
    )(*[item.value for item in ins])
    return types.SimpleNamespace(**jax.tree.unflatten(jax.tree.structure(outputs), results))


def lane_place(rows, width, first):
    lane = lax.broadcasted_iota(jnp.int32, (rows, width), 1)
    row = lax.broadcasted_iota(jnp.int32, (rows, width), 0)
    return jnp.where(lane == row + first, 1.0, 0.0).astype(BF16)


def slot_rows(s):
    return pl.ds(pl.multiple_of(s * SLOT, SLOT), SLOT)


def pair_lanes(p):
    return pl.ds(pl.multiple_of(p * 128, 128), 128)


def attend(m, s, p):
    rows, at = slot_rows(s), pair_lanes(p)
    own2 = jnp.concatenate([m.own[rows, :], m.own[rows, :]], axis=0)
    qs = head_halves(m.q[rows, at])
    spread = matmul(qs, m.rel[...]).astype(BF16) * own2
    group = lax.broadcasted_iota(jnp.int32, (SLOT, 128), 1) - 2 * WIN
    second = m.table[rows, 2:3] == 1
    mark = jnp.where(((group == 0) & ~second) | ((group == 1) & second), 1.0, 0.0)
    near = matmul(spread, m.fold[...]) + jnp.concatenate([mark, mark], axis=0)
    left = jnp.concatenate([qs * BF16(0.125), near.astype(BF16)], axis=1)
    right = jnp.concatenate([m.k[rows, at], m.key[rows, :]], axis=1)
    scores = matmul_nt(left, right)
    weight = jnp.exp(scores - jnp.max(scores, axis=-1, keepdims=True))
    soft = (weight / jnp.sum(weight, axis=-1, keepdims=True)).astype(BF16)
    m.soft[s * PAIRS + p] = soft
    m.o[rows, at] = join_halves(matmul(soft, m.v[rows, at])).astype(BF16)


def attend_back(m, s, p):
    rows, at = slot_rows(s), pair_lanes(p)
    own2 = jnp.concatenate([m.own[rows, :], m.own[rows, :]], axis=0)
    qs, dos = head_halves(m.q[rows, at]), head_halves(m.do[rows, at])
    o = m.o[rows, at].astype(F32)
    soft = m.soft[s * PAIRS + p]
    inner = jnp.sum(dos.astype(F32) * jnp.concatenate([o, o], axis=0), axis=-1, keepdims=True)
    ds = (soft.astype(F32) * (matmul_nt(dos, m.v[rows, at]) - inner)).astype(BF16)
    right = jnp.concatenate([m.k[rows, at], m.key[rows, :]], axis=1)
    back = matmul(ds, right)
    spread = matmul_nt(back[:, 128:].astype(BF16), m.fold[...]).astype(BF16) * own2
    dq = back[:, :128] * 0.125 + matmul_nt(spread, m.rel[...])
    m.dq[rows, at] = join_halves(dq).astype(BF16)
    m.drel[...] += matmul_tn(qs, spread)
    m.dk[rows, at] = (matmul_tn(ds, qs) * 0.125).astype(BF16)
    m.dv[rows, at] = matmul_tn(soft, dos).astype(BF16)


def own_place(table):
    lane = lax.broadcasted_iota(jnp.int32, (SLOT, REL), 1)
    row, col = table[:, 0:1], table[:, 1:2]
    first, second = row * WIN, REL // 2 + col * WIN
    hot = (lane >= first) & (lane < first + WIN) & (row >= 0)
    hot = hot | ((lane >= second) & (lane < second + WIN) & (col >= 0))
    return jnp.where(hot, 1.0, 0.0).astype(BF16)


def key_columns(m, total):
    place = m.table[0:total, :]
    mask = m.mask[...].astype(F32).astype(BF16)
    rows = matmul(one_hot(place[:, 3:4], mask.shape[0]), mask)
    lane = lax.broadcasted_iota(jnp.int32, rows.shape, 1)
    valid = jnp.sum(jnp.where(lane == place[:, 4:5], rows, 0.0), axis=1, keepdims=True)
    lane = lax.broadcasted_iota(jnp.int32, m.key.shape, 1)
    hot = (lane == place[:, 0:1]) | ((lane == place[:, 1:2] + WIN) & (place[:, 1:2] >= 0))
    group = lane - 2 * WIN
    shut = ((group == 0) | (group == 1)) & ((valid < 0.5) | (place[:, 2:3] != group))
    m.key[...] = jnp.where(shut, -1e30, jnp.where(hot, 1.0, 0.0)).astype(BF16)


def pack_small(m, place, piece, wide):
    first, second = lane_place(piece, 128, place.col * piece), lane_place(wide, 384, place.col * wide)
    m.small[...] = jnp.zeros_like(m.small)
    m.small[0:8, 0:128] = matmul(m.vectors[...], first).astype(BF16)
    m.small[0:1, 128:512] = matmul(m.bias[...], second).astype(BF16)


def unpack_small(m, blocks, piece, wide):
    full = m.full[SMALL]
    vec = None
    for n in range(blocks):
        term = matmul(full[pl.ds(n * 16, 16), 0:piece], lane_place(piece, D, n * piece))
        vec = term if vec is None else vec + term
    m.vec[...] = vec
    per = 1 if wide % 128 == 0 else 4
    for n in range(0, blocks, per):
        row = None
        for j in range(per):
            block = full[pl.ds((n + j) * 16, 16), 128 : 128 + wide]
            term = block.astype(F32) if per == 1 else matmul(block, lane_place(wide, per * wide, j * wide))
            row = term if row is None else row + term
        m.b1[:, pl.ds(n * wide, per * wide)] = row[:8]


def split_small(m, blocks, piece, wide, ff):
    full = m.grad_small
    sums, db1 = m.sums[...].astype(BF16), m.db1[...].astype(BF16)
    full[...] = jnp.zeros_like(full)
    for n in range(blocks):
        rows = pl.ds(n * 16, 8)
        full[rows, 0:128] = matmul_nt(sums, lane_place(128, D, n * piece)).astype(BF16)
        if wide % 128 == 0:
            full[rows, 128 : 128 + wide] = db1[:, n * wide : (n + 1) * wide]
        else:
            first = n * wide // 128 * 128
            last = min(round_up(n * wide + wide, 128), ff)
            place = lane_place(128, last - first, n * wide - first)
            full[rows, 128:256] = matmul_nt(db1[:, first:last], place).astype(BF16)


def pick_cells(target, table, column, near, far, step):
    @pl.loop(0, target.shape[0] // step)
    def _(n):
        rows = pl.ds(pl.multiple_of(n * step, 16), step)
        index = table[rows, column : column + 1]
        here, there = one_hot(index, near.shape[0]), one_hot(index - near.shape[0], far.shape[0])
        target[rows, :] = (matmul(here, near[...]) + matmul(there, far[...])).astype(BF16)


def layer_kernel(plan, units, m):
    total, slots = plan["total"], plan["slots"]
    packed, landed = plan["packed"], plan["landed"]
    blocks = len(units) - FC1
    cells = m.in_tokens.shape[0]
    first = 0
    early = []
    for size in (cells, cells, packed, packed, landed, landed):
        early.append(m.dw_fc2.at[pl.ds(first, size)])
        first += size
    tiles, packets, arrivals = early[:2], early[2:4], early[4:]
    m.acc, m.do, m.gx = m.dr, m.n2, m.xs
    late = [m.full[FC2].at[pl.ds(n * total, total)] for n in range(4)]
    m.dq, m.dk, m.dv, m.out = late
    back_packets = [m.full[FC2].at[pl.ds(4 * total, landed)], m.full[FC2].at[pl.ds(0, landed)]]
    grads = {PROJ: m.full[FC1 + 3], FC2: m.dw_fc2, SMALL: m.grad_small}
    for third in range(3):
        grads[QKV + third] = m.full[FC1 + third]
    for b in range(blocks):
        grads[FC1 + b] = m.dw_fc1[b]

    place = Place()
    me = place.row * place.cols + place.col
    table = pltpu.make_async_copy(m.in_table.at[me], m.table, m.local_sems.at[len(units)])
    table.start()
    loads = []
    for n, source in enumerate((m.in_tokens, m.in_cotangent)):
        loads.append(pltpu.make_async_copy(source, tiles[n], m.local_sems.at[len(units) + 1 + n]))
        loads[n].start()
    width = D // 3
    thirds = []
    for third in range(3):
        for n in range(3):
            source = m.w_qkv.at[:, pl.ds(n * D + third * width, width)]
            target = m.thirds[third].at[:, pl.ds(n * width, width)]
            thirds.append(pltpu.make_async_copy(source, target, m.third_sems.at[third * 3 + n]))
            thirds[-1].start()
    for n in range(2):
        arrivals[n][...] = jnp.zeros((landed, D), BF16)
        m.back_arrivals[n][...] = jnp.zeros((packed, D), BF16)
    heard = greet(place)
    copies = Copies(m.send_sems, m.recv_sems)
    line = Timeline()
    piece, wide = units[PROJ].rows, units[FC2].rows
    pack_small(m, place, piece, wide)
    table.wait()
    loads[0].wait()
    moves = [Exchange(place, copies, plan, packets[n], arrivals[n], False) for n in range(2)]

    def post(n):
        packets[n][...] = matmul(one_hot(m.table[0:packed, 6:7], cells), tiles[n][...]).astype(BF16)
        if n == 0:
            pl.semaphore_wait(pltpu.get_barrier_semaphore(), heard)
        moves[n].start()
        line.load(ALONG, 8.0)
        line.load(ACROSS, 5.0)
        line.spend(1.5)

    def receive(n):
        moves[n].wait()
        pick_cells((m.xs, m.gs)[n], m.table, 5, tiles[n], arrivals[n], SLOT)
        line.spend(2.0)

    post(0)
    shards = {SMALL: m.small, PROJ: m.w_proj, FC2: m.w_fc2}
    for third in range(3):
        shards[QKV + third] = m.thirds[third]
    for b in range(blocks):
        shards[FC1 + b] = m.w_fc1.at[:, pl.ds(b * D, D)]
    gathers = [
        Gather(place, copies, units[n], shards[n], m.full[n], m.stage[n], m.local_sems.at[n]) for n in range(len(units))
    ]
    outs = {PROJ: [m.g_proj], FC2: [m.g_fc2], SMALL: [m.g_small]}
    for third in range(3):
        outs[QKV + third] = [m.g_qkv.at[:, pl.ds(n * D + third * width, width)] for n in range(3)]
    for b in range(blocks):
        outs[FC1 + b] = [m.g_fc1.at[:, pl.ds(b * D, D)]]
    scatters = {}

    def scatter(n):
        scatters[n] = Scatter(place, copies, units[n], grads[n], m.half[n], m.buffers[n], m.stage[n], outs[n])
        line.launch(scatters[n])

    line.queue = list(gathers)
    for copy in thirds:
        copy.wait()
    for n in range(2):
        line.launch(line.queue.pop(0))
    m.fold[...] = fold_matrix()
    rel = jnp.concatenate([matmul_tn(r[...], m.select[...]).astype(BF16) for r in (m.rel_rows, m.rel_cols)], axis=1)
    m.rel[...] = jnp.concatenate([rel, rel], axis=0)
    key_columns(m, total)

    @pl.loop(0, slots)
    def _(s):
        m.own[slot_rows(s), :] = own_place(m.table[slot_rows(s), :])

    line.spend(4.0)
    line.need_time(12.0)
    receive(0)
    line.need(gathers[SMALL])
    small = units[SMALL]
    line_count = 2 * small.chips * small.row_count
    unpack_small(m, line_count, place.cols * piece, place.cols * wide)
    vec = m.vec

    @pl.loop(0, slots)
    def _(s):
        rows = slot_rows(s)
        hat, _ = normalized(m.xs[rows, :].astype(F32))
        m.n1[rows, :] = (hat * vec[0:1, :] + vec[1:2, :]).astype(BF16)

    line.spend(3.0)
    def pairs_of(s, pairs, function):
        @pl.loop(pairs.start, pairs.stop)
        def _(p):
            function(m, s, p)

    for third in range(3):
        line.need(gathers[QKV + third])
        lanes = pl.ds(third * width, width)
        for n, (target, bias) in enumerate(((m.q, vec[2:3, :]), (m.k, None), (m.v, vec[3:4, :]))):
            out = matmul(m.n1[...], m.full[QKV + third][:, pl.ds(n * width, width)])
            if bias is not None:
                out = out + bias[:, third * width : (third + 1) * width]
            target[:, lanes] = out.astype(BF16)
        line.spend(1.5)
        if third == 0:
            loads[1].wait()
            post(1)
        for s in range(slots):
            pairs_of(s, range(third * PAIRS // 3, (third + 1) * PAIRS // 3), attend)
            line.spend(2.1)
        if third == 1:
            receive(1)
    line.need(gathers[PROJ])

    @pl.loop(0, slots)
    def _(s):
        rows = slot_rows(s)
        r = m.xs[rows, :].astype(F32) + matmul(m.o[rows, :], m.full[PROJ][...]) + vec[4:5, :]
        m.r[rows, :] = r
        hat, _ = normalized(r)
        m.n2[rows, :] = (hat * vec[5:6, :] + vec[6:7, :]).astype(BF16)
        m.acc[rows, :] = r + vec[7:8, :]

    line.spend(4.5)
    for move in moves:
        move.finish()
    line.need(gathers[FC2])
    size = width
    for b in range(blocks):
        line.need(gathers[FC1 + b])
        for h in range(3):
            lanes, rows = pl.ds(h * size, size), pl.ds(b * D + h * size, size)
            w1, w2 = m.full[FC1 + b][:, lanes], m.full[FC2][rows, :]
            u = matmul(m.n2[...], w1) + m.b1[0:1, rows]
            half = 0.5 + 0.5 * lax.erf(u * 0.7071067811865476)
            a = (u * half).astype(BF16)
            m.acc[...] += matmul(a, w2)
            m.dw_fc2[rows, :] = matmul_tn(a, m.gs[...]).astype(BF16)
            slope = half + u * jnp.exp(u * u * -0.5) * 0.3989422804014327
            du = (matmul_nt(m.gs[...], w2) * slope).astype(BF16)
            m.db1[:, rows] = jnp.broadcast_to(column_sum(du.astype(F32)), (8, size))
            m.dw_fc1[b][:, lanes] = matmul_tn(m.n2[...], du).astype(BF16)
            term = matmul_nt(du, w1)
            if b == 0 and h == 0:
                m.dn2[...] = term
            else:
                m.dn2[...] += term
            line.spend(2.2)
        scatter(FC1 + b)
    for gather in gathers:
        gather.settle()
    scatter(FC2)

    m.sums[...] = jnp.zeros_like(m.sums)

    @pl.loop(0, slots)
    def _(s):
        rows = slot_rows(s)
        m.out[rows, :] = m.acc[rows, :].astype(BF16)
        hat, rate = normalized(m.r[rows, :])
        dn2, g = m.dn2[rows, :], m.gs[rows, :].astype(F32)
        m.sums[5:6, :] += column_sum(dn2 * hat)
        m.sums[6:7, :] += column_sum(dn2)
        m.sums[7:8, :] += column_sum(g)
        dr = g + norm_back(dn2, vec[5:6, :], hat, rate)
        m.dr[rows, :] = dr
        m.sums[4:5, :] += column_sum(dr.astype(BF16).astype(F32))

    line.spend(3.5)
    db = m.dr[...].astype(BF16)
    grads[PROJ][...] = matmul_tn(m.o[...], db).astype(BF16)
    scatter(PROJ)
    m.do[...] = matmul_nt(db, m.full[PROJ][...]).astype(BF16)
    line.spend(4.0)
    back_packets[0][...] = matmul(one_hot(m.table[0:landed, 7:8], total), m.out[...]).astype(BF16)
    moves = [Exchange(place, copies, plan, back_packets[n], m.back_arrivals[n], True) for n in range(2)]
    moves[0].start()
    line.spend(1.5)

    m.drel[...] = jnp.zeros_like(m.drel)
    dn1 = m.dn2
    for third in range(3):
        for s in range(slots):
            pairs_of(s, range(third * PAIRS // 3, (third + 1) * PAIRS // 3), attend_back)
            line.spend(2.3)
        own = pl.ds(third * width, width)
        for n, d in enumerate((m.dq, m.dk, m.dv)):
            lanes = pl.ds(n * width, width)
            grads[QKV + third][:, lanes] = matmul_tn(m.n1[...], d[:, own]).astype(BF16)
        line.spend(2.2)
        scatter(QKV + third)
        for n, d in enumerate((m.dq, m.dk, m.dv)):
            term = matmul_nt(d[:, own], m.full[QKV + third][:, pl.ds(n * width, width)])
            if third == 0 and n == 0:
                dn1[...] = term
            else:
                dn1[...] += term
        line.spend(1.9)
    drel = m.drel[:HEAD_DIM, :] + m.drel[HEAD_DIM:, :]
    for n in range(2):
        part = drel[:, n * (REL // 2) : (n + 1) * (REL // 2)]
        m.held[0, n] = lax.dot_general(
            m.select[...].astype(F32), part, (((1,), (1,)), ((), ())), preferred_element_type=F32,
            precision=lax.Precision.HIGHEST,
        )
    doubling = Doubling(place, copies, m.held, m.arriving)
    line.launch(doubling)

    @pl.loop(0, slots)
    def _(s):
        rows = slot_rows(s)
        hat, rate = normalized(m.xs[rows, :].astype(F32))
        d = dn1[rows, :]
        m.sums[0:1, :] += column_sum(d * hat)
        m.sums[1:2, :] += column_sum(d)
        m.sums[2:3, :] += column_sum(m.dq[rows, :].astype(F32))
        m.sums[3:4, :] += column_sum(m.dv[rows, :].astype(F32))
        m.gx[rows, :] = (m.dr[rows, :] + norm_back(d, vec[0:1, :], hat, rate)).astype(BF16)

    back_packets[1][...] = matmul(one_hot(m.table[0:landed, 7:8], total), m.gx[...]).astype(BF16)
    moves[1].start()
    line.spend(4.5)
    split_small(m, line_count, place.cols * piece, place.cols * wide, blocks * D)
    scatter(SMALL)
    stores = []
    results = [m.dk, m.dv]
    for n, source in enumerate((m.out, m.gx)):
        moves[n].wait()
        tile = results[n].at[pl.ds(0, cells)]
        pick_cells(tile, m.table, 8, source, m.back_arrivals[n], 128)
        stores.append(pltpu.make_async_copy(tile, (m.layer_out, m.grad_tokens)[n], m.local_sems.at[n]))
        stores[n].start()
        line.spend(2.0)
    line.finish()
    m.rel_sum[...] = m.held[doubling.last]
    lane_pick = lane_place(512, 512, -place.col * piece)
    lane_pick2 = lane_place(512, 512, -128 - place.col * wide)
    for target, picked in ((m.g_vec, lane_pick), (m.g_b1, lane_pick2)):
        target[...] = jnp.dot(
            m.g_small[...], picked[:, : target.shape[1]].astype(F32),
            preferred_element_type=F32, precision=lax.Precision.HIGHEST,
        )
    for op in [*scatters.values(), doubling]:
        op.settle()
    for move in moves:
        move.finish()
    for store in stores:
        store.wait()


def fold_matrix():
    row = lax.broadcasted_iota(jnp.int32, (REL, 128), 0)
    lane = lax.broadcasted_iota(jnp.int32, (REL, 128), 1)
    half = REL // 2
    inside = jnp.where(row < half, row, row - half)
    target = inside % WIN + jnp.where(row < half, 0, WIN)
    return jnp.where((lane == target) & (inside < CELLS), 1.0, 0.0).astype(BF16)


def body(
    image_tokens, cotangent, content_mask, norm1_gain, norm1_bias, qkv_weight, query_bias, value_bias,
    rel_rows, rel_cols, proj_weight, proj_bias, norm2_gain, norm2_bias, fc1_weight, fc1_bias, fc2_weight, fc2_bias,
):
    images, rows, cols = axis_sizes()
    _, tile_rows, tile_cols, _ = image_tokens.shape
    cells = tile_rows * tile_cols
    plan = plan_windows(rows, cols, tile_rows, tile_cols)
    total, slots, packed, landed = plan["total"], plan["slots"], plan["packed"], plan["landed"]
    piece, wide, ff = qkv_weight.shape[0], fc2_weight.shape[0], fc1_weight.shape[1]
    blocks = ff // D
    line = Unit(piece, D, ROWS)
    units = [Unit(16, 512, SUM), line, line, line, line, Unit(wide, D, ROWS if wide % 16 else PLAIN)] + [line] * blocks

    height = max(total, packed, landed, cells)
    table = np.full((rows * cols, height, 16), -1, np.int32)
    table[:, :total, :5] = plan["where"][:, :, :5]
    for n, name in enumerate(("slot_from", "pack_from", "back_from", "tile_from")):
        table[:, : plan[name].shape[1], 5 + n] = plan[name]
    index = np.arange(WIN)[:, None] - np.arange(WIN)[None, :] + WIN - 1
    span = rel_rows.shape[0]
    select = np.zeros((span, REL // 2), np.float32)
    select[index.reshape(-1), np.arange(CELLS)] = 1
    vectors = [norm1_gain, norm1_bias, query_bias, value_bias, proj_bias, norm2_gain, norm2_bias, fc2_bias]

    def everywhere(value):
        return Item(value, space=pl.ANY)

    def vmem(*shape, kind=BF16):
        return Item(shape, kind)

    inputs = dict(
        in_tokens=everywhere(image_tokens.reshape(cells, D)), in_cotangent=everywhere(cotangent.reshape(cells, D)),
        in_table=everywhere(jnp.asarray(table)), mask=Item(content_mask[0]), vectors=Item(jnp.stack(vectors)), bias=Item(fc1_bias[None]),
        rel_rows=Item(rel_rows), rel_cols=Item(rel_cols), select=Item(jnp.asarray(select, BF16)),
        w_qkv=everywhere(qkv_weight), w_proj=everywhere(proj_weight), w_fc1=everywhere(fc1_weight), w_fc2=everywhere(fc2_weight),
    )
    outputs = dict(
        layer_out=Item((cells, D), BF16, pl.ANY), grad_tokens=Item((cells, D), BF16, pl.ANY),
        g_qkv=vmem(piece, 3 * D, kind=F32), g_proj=vmem(piece, D, kind=F32),
        g_fc1=vmem(piece, ff, kind=F32), g_fc2=vmem(wide, D, kind=F32),
        g_vec=vmem(16, 128, kind=F32), g_b1=vmem(16, round_up(wide, 128), kind=F32), rel_sum=vmem(2, span, HEAD_DIM, kind=F32),
    )
    swaps = (images * rows * cols).bit_length() - 1
    count = sum(u.copies() for u in units) + swaps + 4 * len(plan["pairs"])
    sems = pltpu.SemaphoreType.DMA
    scratch = dict(
        table=vmem(height, 16, kind=jnp.int32), small=vmem(16, 512), thirds=[vmem(piece, D)] * 3, third_sems=Item(pltpu.SemaphoreType.DMA((9,))), rel=vmem(2 * HEAD_DIM, REL), fold=vmem(REL, 128),
        xs=vmem(total, D), gs=vmem(total, D), n1=vmem(total, D), q=vmem(total, D), k=vmem(total, D), v=vmem(total, D),
        key=vmem(total, 128), soft=vmem(slots * PAIRS, 2 * SLOT, SLOT), o=vmem(total, D), n2=vmem(total, D),
        r=vmem(total, D, kind=F32), dr=vmem(total, D, kind=F32), dn2=vmem(total, D, kind=F32), own=vmem(total, REL),
        vec=vmem(16, D, kind=F32), b1=vmem(8, ff, kind=F32), db1=vmem(8, ff, kind=F32), sums=vmem(8, D, kind=F32),
        drel=vmem(2 * HEAD_DIM, REL, kind=F32), held=vmem(swaps + 1, 2, span, HEAD_DIM, kind=F32),
        arriving=vmem(swaps, 2, span, HEAD_DIM, kind=F32), g_small=vmem(16, 512, kind=F32),
        grad_small=vmem(*units[SMALL].full_shape()), back_arrivals=[vmem(packed, D)] * 2,
        full=[vmem(*u.full_shape()) for u in units], half=[vmem(*u.half_shape()) for u in units],
        stage=[vmem(*(u.stage_shape() if u.mode != PLAIN else (8, 128))) for u in units],
        buffers=[[vmem(*shape) for shape in u.buffer_shapes()] for u in units],
        dw_fc1=[vmem(*line.full_shape())] * blocks, dw_fc2=vmem(*units[FC2].full_shape()),
        send_sems=Item(sems((count,))), recv_sems=Item(sems((count,))), local_sems=Item(sems((len(units) + 3,))),
    )
    done = run(functools.partial(layer_kernel, plan, units), inputs, outputs, scratch)
    g_vec, g_b1 = done.g_vec[:8, :piece], done.g_b1[0, :wide]
    return (
        done.layer_out.reshape(image_tokens.shape), done.grad_tokens.reshape(image_tokens.shape),
        g_vec[0], g_vec[1], done.g_qkv, g_vec[2], g_vec[3], done.rel_sum[0], done.rel_sum[1],
        done.g_proj, g_vec[4], g_vec[5], g_vec[6], done.g_fc1, g_b1, done.g_fc2, g_vec[7],
    )


def solution(mesh):
    everywhere = ("img", "row", "col")
    tile, vector, matrix = P("img", "row", "col", None), P(everywhere), P(everywhere, None)
    in_specs = (
        tile, tile, P("img", None, None), vector, vector, matrix, vector, vector, P(), P(),
        matrix, vector, vector, vector, matrix, vector, matrix, vector,
    )
    out_specs = (
        tile, tile, vector, vector, matrix, vector, vector, P(), P(),
        matrix, vector, vector, vector, matrix, vector, matrix, vector,
    )
    return jax.shard_map(body, mesh=mesh, in_specs=in_specs, out_specs=out_specs, check_vma=False)
```

```python
import functools
import types

import jax
import jax.numpy as jnp
import numpy as np
from jax import lax
from jax.experimental import pallas as pl
from jax.experimental.pallas import tpu as pltpu
from jax.sharding import PartitionSpec as P

D = 768
HEADS = 12
HEAD_DIM = 64
PAIRS = HEADS // 2
WIN = 14
CELLS = WIN * WIN
SLOT = 208
MESH = pl.DeviceIdType.MESH
F32 = jnp.float32
BF16 = jnp.bfloat16
VMEM_LIMIT = 62 * 2**20


def round_up(value, unit):
    return -(-value // unit) * unit


def plan_windows(rows, cols, tile_rows, tile_cols):
    devices = rows * cols
    height, width = rows * tile_rows, cols * tile_cols
    windows = []
    for top in range(0, height, WIN):
        for left in range(0, width, WIN):
            windows.append(
                [
                    (r, c, r - top, c - left)
                    for r in range(top, min(top + WIN, height))
                    for c in range(left, min(left + WIN, width))
                ]
            )
    bins = []
    for window in sorted(windows, key=len, reverse=True):
        for held in bins:
            if len(held) < 2 and sum(map(len, held)) + len(window) <= CELLS:
                held.append(window)
                break
        else:
            bins.append([window])
    slots = -(-len(bins) // devices)
    while len(bins) < slots * devices:
        bins.append([])

    def home(cell):
        return cell[0] // tile_rows * cols + cell[1] // tile_cols

    weights = np.zeros((len(bins), devices), np.int64)
    for number, held in enumerate(bins):
        for window in held:
            for cell in window:
                weights[number, home(cell)] += 1
    hops = np.zeros((devices, devices, rows * rows * cols + cols * cols * rows))
    for source in range(devices):
        for target in range(devices):
            r0, c0, r1, c1 = source // cols, source % cols, target // cols, target % cols
            step = 1 if r1 > r0 else -1
            for r in range(r0, r1, step):
                hops[source, target, (r * rows + r + step) * cols + c0] = 1
            step = 1 if c1 > c0 else -1
            for c in range(c0, c1, step):
                hops[source, target, rows * rows * cols + (c * cols + c + step) * rows + r1] = 1
    loads = np.einsum("bs,sdl->bdl", weights, hops)

    def cost(order):
        load = loads[np.arange(len(bins)), np.array(order) // slots].sum(axis=0)
        return load.max() * 100 + load.sum()

    order = [0] * len(bins)
    free = [slots] * devices
    for number in range(len(bins)):
        options = [d for d in range(devices) if free[d]]
        best = min(options, key=lambda d: (loads[number, d].sum(), d))
        order[number] = best * slots + slots - free[best]
        free[best] -= 1
    current = cost(order)
    while True:
        found = None
        for a in range(len(bins)):
            for b in range(a):
                if order[a] // slots != order[b] // slots:
                    order[a], order[b] = order[b], order[a]
                    trial = cost(order)
                    if trial < current:
                        current, found = trial, (a, b)
                    order[a], order[b] = order[b], order[a]
        if found is None:
            break
        a, b = found
        order[a], order[b] = order[b], order[a]
    total = slots * SLOT
    place = [[] for _ in range(devices)]
    for number in sorted(range(len(bins)), key=lambda n: order[n]):
        device, slot = order[number] // slots, order[number] % slots
        position = slot * SLOT
        for group, window in enumerate(bins[number]):
            for cell in window:
                place[device].append((position, cell, group))
                position += 1
    cells = tile_rows * tile_cols
    pairs = []
    sent, got = [0] * devices, [0] * devices
    moved = {}
    for source in range(devices):
        for target in range(devices):
            if source != target:
                listed = [e for e in place[target] if home(e[1]) == source]
                if listed:
                    count = round_up(len(listed), 16)
                    pairs.append((source, target, sent[source], got[target], count))
                    moved[source, target] = (listed, sent[source], got[target])
                    sent[source] += count
                    got[target] += count
    packed, landed = round_up(max(sent), 128), round_up(max(got), 128)
    pack_from = np.full((devices, packed), -1, np.int32)
    slot_from = np.full((devices, total), -1, np.int32)
    back_from = np.full((devices, landed), -1, np.int32)
    tile_from = np.full((devices, cells), -1, np.int32)
    where = np.full((devices, total, 8), -1, np.int32)
    for device in range(devices):
        for position, cell, group in place[device]:
            where[device, position, :5] = (cell[2], cell[3], group, cell[0], cell[1])
            if home(cell) == device:
                local = cell[0] % tile_rows * tile_cols + cell[1] % tile_cols
                slot_from[device, position] = local
                tile_from[device, local] = position
    for (source, target), (listed, out, into) in moved.items():
        for k, (position, cell, group) in enumerate(listed):
            local = cell[0] % tile_rows * tile_cols + cell[1] % tile_cols
            pack_from[source, out + k] = local
            slot_from[target, position] = cells + into + k
            back_from[target, into + k] = position
            tile_from[source, local] = total + out + k
    return dict(
        slots=slots, total=total, pairs=pairs, packed=packed, landed=landed, where=where,
        pack_from=pack_from, slot_from=slot_from, back_from=back_from, tile_from=tile_from,
    )


def matmul(a, b):
    return jnp.dot(a, b, preferred_element_type=F32)


def matmul_nt(a, b):
    return lax.dot_general(a, b, (((1,), (1,)), ((), ())), preferred_element_type=F32)


def matmul_tn(a, b):
    return lax.dot_general(a, b, (((0,), (0,)), ((), ())), preferred_element_type=F32)


def one_hot(index, width):
    return (index == lax.broadcasted_iota(jnp.int32, (index.shape[0], width), 1)).astype(BF16)


def normalized(values):
    offset = values - jnp.mean(values, axis=-1, keepdims=True)
    rate = lax.rsqrt(jnp.mean(offset * offset, axis=-1, keepdims=True) + 1e-06)
    return offset * rate, rate


def norm_back(cotangent, gain, hat, rate):
    e = cotangent * gain
    mean_e = jnp.mean(e, axis=-1, keepdims=True)
    mean_eh = jnp.mean(e * hat, axis=-1, keepdims=True)
    return rate * (e - mean_e - hat * mean_eh)


def column_sum(values):
    return jnp.sum(values, axis=0, keepdims=True)


def params(**more):
    return pltpu.CompilerParams(vmem_limit_bytes=VMEM_LIMIT, **more)


def head_halves(pair):
    low = lax.broadcasted_iota(jnp.int32, pair.shape, 1) < HEAD_DIM
    zero = jnp.zeros_like(pair)
    return jnp.concatenate([jnp.where(low, pair, zero), jnp.where(low, zero, pair)], axis=0)


def join_halves(stacked):
    low = lax.broadcasted_iota(jnp.int32, (SLOT, 2 * HEAD_DIM), 1) < HEAD_DIM
    return jnp.where(low, stacked[:SLOT], stacked[SLOT:])


REL = 512


def axis_sizes():
    return lax.axis_size("img"), lax.axis_size("row"), lax.axis_size("col")


class Place:
    def __init__(self):
        images, self.rows, self.cols = axis_sizes()
        self.chips = images // 2
        img = lax.axis_index("img")
        self.chip, self.core = img // 2, img % 2
        self.row, self.col = lax.axis_index("row"), lax.axis_index("col")

    def other(self, axis, k):
        if axis == "row":
            index = (self.row + k) % self.rows
            return index, {"row": index}
        if axis == "col":
            index = (self.col + k) % self.cols
            return index, {"col": index}
        index = (self.chip + k) % self.chips
        return index, {"img": index * 2 + self.core}

    def sibling(self):
        return {"img": self.chip * 2 + 1 - self.core}

    def count(self, axis):
        return {"row": self.rows, "col": self.cols, "chip": self.chips}[axis]


def greet(place):
    barrier = pltpu.get_barrier_semaphore()
    heard = 1
    pl.semaphore_signal(barrier, inc=1, device_id=place.sibling(), device_id_type=MESH)
    for k in range(1, place.chips):
        pl.semaphore_signal(barrier, inc=1, device_id=place.other("img", k)[1], device_id_type=MESH)
        heard += 1
    for r in range(place.rows):
        for c in range(place.cols):
            if (r, c) == (0, 0):
                continue
            target = {"row": (place.row + r) % place.rows, "col": (place.col + c) % place.cols}
            pl.semaphore_signal(barrier, inc=1, device_id=target, device_id_type=MESH)
            heard += 1
    return heard


class Copies:
    def __init__(self, send_sems, recv_sems):
        self.send_sems, self.recv_sems = send_sems, recv_sems
        self.used = 0

    def start(self, source, target, device):
        copy = pltpu.make_async_remote_copy(
            src_ref=source,
            dst_ref=target,
            send_sem=self.send_sems.at[self.used],
            recv_sem=self.recv_sems.at[self.used],
            device_id=device,
            device_id_type=MESH,
        )
        self.used += 1
        copy.start()
        return copy


def swap_steps(place):
    steps = [place.sibling()]
    bit = 1
    while bit < place.chips:
        flip = place.chip + bit - 2 * bit * (place.chip // bit % 2)
        steps.append({"img": flip * 2 + place.core})
        bit *= 2
    bit = 1
    while bit < place.rows:
        steps.append({"row": place.row + bit - 2 * bit * (place.row // bit % 2)})
        bit *= 2
    bit = 1
    while bit < place.cols:
        steps.append({"col": place.col + bit - 2 * bit * (place.col // bit % 2)})
        bit *= 2
    return steps


SMALL, QKV, _, _, PROJ, FC2, _, _, FC1 = range(9)
ROWS, PLAIN, SUM = range(3)
ALONG, ACROSS, CORES = range(3)


class Unit:
    def __init__(self, rows, width, mode):
        self.rows, self.width, self.mode = rows, width, mode
        images, self.row_count, self.col_count = axis_sizes()
        self.chips = images // 2
        self.block = rows if mode == SUM else rows * self.col_count
        self.line = self.block * self.row_count
        self.half = width // 2
        self.low, self.high = pl.ds(0, self.half), pl.ds(self.half, width - self.half)
        self.size = 2 * self.chips * self.line * width / (D * D)

    def full_shape(self):
        return (2 * self.chips * self.line, self.width)

    def half_shape(self):
        return (self.chips * self.line, self.width)

    def stage_shape(self):
        return (self.col_count, self.rows, self.width)

    def buffer_shapes(self):
        c, r, n = self.chips, self.row_count, self.col_count
        return [
            (c - 1, self.line, self.half),
            (r - 1, c, self.block, self.half),
            (r - 1, self.block, self.half),
            (c - 1, self.block, self.half),
            (n - 1, self.rows, self.width),
        ]

    def rows_at(self, index, count=1):
        return pl.ds(pl.multiple_of(index * self.block, 8), count * self.block)

    def copies(self):
        c, r, n = self.chips, self.row_count, self.col_count
        return 2 * ((n - 1) + (r - 1) + (c - 1) + (c - 1) + (r - 1) * c + c)

    def spread(self, k):
        row = lax.broadcasted_iota(jnp.int32, (self.block, self.rows), 0)
        col = lax.broadcasted_iota(jnp.int32, (self.block, self.rows), 1)
        return jnp.where(row == col + k * self.rows, 1.0, 0.0).astype(BF16)


class Phased:
    last = 4

    def __init__(self, place, copies):
        self.place, self.copies = place, copies
        self.phase, self.waiting, self.sent = 0, [], []

    @property
    def done(self):
        return self.phase > self.last

    def send(self, source, target, device):
        copy = self.copies.start(source, target, device)
        self.waiting.append(copy)
        self.sent.append(copy)

    def advance(self):
        for copy in self.waiting:
            copy.wait_recv()
        self.waiting = []
        self.step()
        self.phase += 1

    def settle(self):
        for copy in self.sent:
            copy.wait_send()
        self.sent = []


class Gather(Phased):
    def __init__(self, place, copies, unit, shard, full, stage, local):
        super().__init__(place, copies)
        self.unit, self.shard, self.full, self.stage, self.local = unit, shard, full, stage, local

    def cost(self):
        size = self.unit.size
        return [(ALONG, 3.3 * size), (ACROSS, 1.7 * size), (ACROSS, 3.3 * size), (CORES, 0.95 * size), None][self.phase - 1]

    def step(self):
        place, unit, full = self.place, self.unit, self.full
        y, c, x, z = place.chip, place.core, place.row, place.col
        own = unit.rows_at((y * 2 + c) * place.rows + x)
        if self.phase == 0:
            if unit.mode == PLAIN:
                first = ((y * 2 + c) * place.rows + x) * unit.block + z * unit.rows
                target = full.at[pl.ds(pl.multiple_of(first, 8), unit.rows)]
            else:
                target = self.stage.at[z]
            self.keep = pltpu.make_async_copy(self.shard, target, self.local)
            self.keep.start()
            for k in range(1, place.cols):
                self.send(self.shard, target, place.other("col", k)[1])
        if self.phase == 1:
            self.keep.wait()
            if unit.mode != PLAIN:
                total = None
                for k in range(place.cols):
                    slab = self.stage[k]
                    term = slab.astype(F32) if unit.mode == SUM else matmul(unit.spread(k), slab)
                    total = term if total is None else total + term
                full[own, :] = total.astype(BF16)
            for k in range(1, place.rows):
                part = full.at[own, unit.low]
                self.send(part, part, place.other("row", k)[1])
            for k in range(1, place.chips):
                part = full.at[own, unit.high]
                self.send(part, part, place.other("img", k)[1])
        if self.phase == 2:
            for k in range(1, place.chips):
                part = full.at[unit.rows_at((y * 2 + c) * place.rows, place.rows), unit.low]
                self.send(part, part, place.other("img", k)[1])
            for k in range(1, place.rows):
                for chip in range(place.chips):
                    part = full.at[unit.rows_at((chip * 2 + c) * place.rows + x), unit.high]
                    self.send(part, part, place.other("row", k)[1])
        if self.phase == 3:
            for chip in range(place.chips):
                part = full.at[unit.rows_at((chip * 2 + c) * place.rows, place.rows)]
                self.send(part, part, place.sibling())


def add_rows(ref, start, count, lanes, terms):
    step = 32 if count % 32 == 0 else count

    def add(first):
        rows = pl.ds(pl.multiple_of(start + first, 8), step)
        total = ref[rows, lanes].astype(F32)
        for term in terms:
            total = total + term(pl.ds(pl.multiple_of(first, 8), step)).astype(F32)
        ref[rows, lanes] = total.astype(BF16)

    if step == count:
        add(0)
    else:
        pl.loop(0, count // step)(lambda n: add(n * step))


class Scatter(Phased):
    def __init__(self, place, copies, unit, full, half, buffers, cut, out):
        super().__init__(place, copies)
        self.unit, self.full, self.half, self.buffers, self.cut, self.out = unit, full, half, buffers, cut, out

    def cost(self):
        size = self.unit.size
        return [(CORES, 0.95 * size), (ACROSS, 3.3 * size), (ACROSS, 1.7 * size), (ALONG, 3.3 * size), None][self.phase - 1]

    def step(self):
        place, unit, half = self.place, self.unit, self.half
        y, c, x, z = place.chip, place.core, place.row, place.col
        low_chip, high_row, low_row, high_chip, along = self.buffers
        own = unit.rows_at(y * place.rows + x)

        def slab(index):
            if unit.mode == ROWS:
                return self.cut, index
            if unit.mode == SUM:
                return half, own
            first = (y * place.rows + x) * unit.block + index * unit.rows
            return half, pl.ds(pl.multiple_of(first, 8), unit.rows)

        if self.phase == 0:
            for chip in range(place.chips):
                part = self.full.at[unit.rows_at((chip * 2 + 1 - c) * place.rows, place.rows)]
                self.send(part, half.at[unit.rows_at(chip * place.rows, place.rows)], place.sibling())
        if self.phase == 1:
            for chip in range(place.chips):
                first = (chip * 2 + c) * unit.line
                term = lambda rows, first=first: self.full[pl.ds(pl.multiple_of(first + rows.start, 8), rows.size), :]
                add_rows(half, chip * unit.line, unit.line, slice(None), [term])
            for k in range(1, place.chips):
                to, device = place.other("img", k)
                part = half.at[unit.rows_at(to * place.rows, place.rows), unit.low]
                self.send(part, low_chip.at[k - 1], device)
            for k in range(1, place.rows):
                to, device = place.other("row", k)
                for chip in range(place.chips):
                    part = half.at[unit.rows_at(chip * place.rows + to), unit.high]
                    self.send(part, high_row.at[k - 1, chip], device)
        if self.phase == 2:
            terms = [lambda rows, k=k: low_chip[k, rows, :] for k in range(place.chips - 1)]
            add_rows(half, y * unit.line, unit.line, unit.low, terms)
            for chip in range(place.chips):
                terms = [lambda rows, k=k, chip=chip: high_row[k, chip, rows, :] for k in range(place.rows - 1)]
                add_rows(half, chip * unit.line + x * unit.block, unit.block, unit.high, terms)
            for k in range(1, place.rows):
                to, device = place.other("row", k)
                self.send(half.at[unit.rows_at(y * place.rows + to), unit.low], low_row.at[k - 1], device)
            for k in range(1, place.chips):
                to, device = place.other("img", k)
                self.send(half.at[unit.rows_at(to * place.rows + x), unit.high], high_chip.at[k - 1], device)
        if self.phase == 3:
            first = (y * place.rows + x) * unit.block
            terms = [lambda rows, k=k: low_row[k, rows, :] for k in range(place.rows - 1)]
            add_rows(half, first, unit.block, unit.low, terms)
            terms = [lambda rows, k=k: high_chip[k, rows, :] for k in range(place.chips - 1)]
            add_rows(half, first, unit.block, unit.high, terms)
            if unit.mode == ROWS:
                block = half[own, :]
                for k in range(place.cols):
                    self.cut[k] = matmul_tn(unit.spread(k), block).astype(BF16)
            for k in range(1, place.cols):
                to, device = place.other("col", k)
                ref, at = slab(to)
                self.send(ref.at[at], along.at[k - 1], device)
        if self.phase == 4:
            ref, at = slab(z)
            total = ref[at].astype(F32)
            for k in range(place.cols - 1):
                total = total + along[k].astype(F32)
            first = 0
            for out in self.out:
                out[...] = total[:, first : first + out.shape[1]]
                first += out.shape[1]


class Doubling(Phased):
    def __init__(self, place, copies, held, arriving):
        super().__init__(place, copies)
        self.held, self.arriving = held, arriving
        self.partners = swap_steps(place)
        self.last = len(self.partners)

    def cost(self):
        return None if self.done else (CORES, 0.5)

    def step(self):
        n = self.phase
        if n > 0:
            self.held[n] = self.held[n - 1] + self.arriving[n - 1]
        if n < len(self.partners):
            self.send(self.held.at[n], self.arriving.at[n], self.partners[n])


class Exchange:
    def __init__(self, place, copies, plan, source, target, back):
        self.me = place.row * place.cols + place.col
        self.first, self.copies, self.cols = copies.used, copies, place.cols
        copies.used += len(plan["pairs"])
        self.pairs, self.source, self.target, self.back = plan["pairs"], source, target, back

    def listed(self):
        for number, (giver, taker, out, into, count) in enumerate(self.pairs):
            if self.back:
                giver, taker, out, into = taker, giver, into, out
            copy = pltpu.make_async_remote_copy(
                src_ref=self.source.at[pl.ds(out, count)],
                dst_ref=self.target.at[pl.ds(into, count)],
                send_sem=self.copies.send_sems.at[self.first + number],
                recv_sem=self.copies.recv_sems.at[self.first + number],
                device_id={"row": taker // self.cols, "col": taker % self.cols},
                device_id_type=MESH,
            )
            yield giver, taker, copy

    def start(self):
        for giver, taker, copy in self.listed():
            pl.when(self.me == giver)(copy.start)

    def wait(self):
        for giver, taker, copy in self.listed():
            pl.when(self.me == taker)(copy.wait_recv)

    def finish(self):
        for giver, taker, copy in self.listed():
            pl.when(self.me == giver)(copy.wait_send)


class Timeline:
    def __init__(self):
        self.now, self.free, self.flying, self.queue = 0.0, [0.0, 0.0, 0.0], [], []

    def load(self, server, time):
        self.free[server] = max(self.free[server], self.now) + time

    def need_time(self, time):
        if self.now < time:
            self.spend(time - self.now)

    def launch(self, op):
        op.advance()
        if not op.done:
            server, time = op.cost()
            early = isinstance(op, Gather)
            self.free[server] = max(self.free[server], self.now) + time * (0.8 if early else 1.0)
            self.flying.append((self.free[server] + (2.0 if early else 3.0), len(self.flying), op))

    def next_up(self):
        entry = min(self.flying, key=lambda e: e[:2])
        self.flying.remove(entry)
        return entry

    def poll(self):
        while True:
            while self.queue and self.free[ALONG] < self.now:
                self.launch(self.queue.pop(0))
            if not self.flying or min(e[0] for e in self.flying) > self.now:
                return
            self.launch(self.next_up()[2])

    def spend(self, time):
        self.now += time
        self.poll()

    def need(self, *ops):
        while not all(op.done for op in ops):
            if not self.flying:
                self.launch(self.queue.pop(0))
                continue
            entry = self.next_up()
            self.now = max(self.now, entry[0])
            self.launch(entry[2])
            self.poll()

    def finish(self):
        while self.flying:
            entry = self.next_up()
            self.now = max(self.now, entry[0])
            self.launch(entry[2])


class Item:
    def __init__(self, value, kind=None, space=pltpu.VMEM):
        self.value, self.kind, self.space = value, kind, space


def run(kernel, inputs, outputs, scratch):
    leaves, tree = jax.tree.flatten((inputs, outputs, scratch))
    ins, outs = jax.tree.leaves(inputs), jax.tree.leaves(outputs)

    def wrapped(*refs):
        named = jax.tree.unflatten(tree, refs)
        kernel(types.SimpleNamespace(**named[0], **named[1], **named[2]))

    results = pl.pallas_call(
        wrapped,
        out_shape=[jax.ShapeDtypeStruct(item.value, item.kind) for item in outs],
        in_specs=[pl.BlockSpec(memory_space=item.space) for item in ins],
        out_specs=[pl.BlockSpec(memory_space=item.space) for item in outs],
        scratch_shapes=[
            item.value if item.kind is None else item.space(item.value, item.kind) for item in leaves[len(ins) + len(outs) :]
        ],
        compiler_params=params(collective_id=0, has_side_effects=True),
    )(*[item.value for item in ins])
    return types.SimpleNamespace(**jax.tree.unflatten(jax.tree.structure(outputs), results))


def lane_place(rows, width, first):
    lane = lax.broadcasted_iota(jnp.int32, (rows, width), 1)
    row = lax.broadcasted_iota(jnp.int32, (rows, width), 0)
    return jnp.where(lane == row + first, 1.0, 0.0).astype(BF16)


def slot_rows(s):
    return pl.ds(pl.multiple_of(s * SLOT, SLOT), SLOT)


def pair_lanes(p):
    return pl.ds(pl.multiple_of(p * 128, 128), 128)


def attend(m, s, p):
    rows, at = slot_rows(s), pair_lanes(p)
    own2 = jnp.concatenate([m.own[rows, :], m.own[rows, :]], axis=0)
    qs = head_halves(m.q[rows, at])
    spread = matmul(qs, m.rel[...]).astype(BF16) * own2
    group = lax.broadcasted_iota(jnp.int32, (SLOT, 128), 1) - 2 * WIN
    second = m.table[rows, 2:3] == 1
    mark = jnp.where(((group == 0) & ~second) | ((group == 1) & second), 1.0, 0.0)
    near = matmul(spread, m.fold[...]) + jnp.concatenate([mark, mark], axis=0)
    left = jnp.concatenate([qs * BF16(0.125), near.astype(BF16)], axis=1)
    right = jnp.concatenate([m.k[rows, at], m.key[rows, :]], axis=1)
    scores = matmul_nt(left, right)
    weight = jnp.exp(scores - jnp.max(scores, axis=-1, keepdims=True))
    soft = (weight / jnp.sum(weight, axis=-1, keepdims=True)).astype(BF16)
    m.soft[s * PAIRS + p] = soft
    m.o[rows, at] = join_halves(matmul(soft, m.v[rows, at])).astype(BF16)


def attend_back(m, s, p):
    rows, at = slot_rows(s), pair_lanes(p)
    own2 = jnp.concatenate([m.own[rows, :], m.own[rows, :]], axis=0)
    qs, dos = head_halves(m.q[rows, at]), head_halves(m.do[rows, at])
    o = m.o[rows, at].astype(F32)
    soft = m.soft[s * PAIRS + p]
    inner = jnp.sum(dos.astype(F32) * jnp.concatenate([o, o], axis=0), axis=-1, keepdims=True)
    ds = (soft.astype(F32) * (matmul_nt(dos, m.v[rows, at]) - inner)).astype(BF16)
    right = jnp.concatenate([m.k[rows, at], m.key[rows, :]], axis=1)
    back = matmul(ds, right)
    spread = matmul_nt(back[:, 128:].astype(BF16), m.fold[...]).astype(BF16) * own2
    dq = back[:, :128] * 0.125 + matmul_nt(spread, m.rel[...])
    m.dq[rows, at] = join_halves(dq).astype(BF16)
    m.drel[...] += matmul_tn(qs, spread)
    m.dk[rows, at] = (matmul_tn(ds, qs) * 0.125).astype(BF16)
    m.dv[rows, at] = matmul_tn(soft, dos).astype(BF16)


def own_place(table):
    lane = lax.broadcasted_iota(jnp.int32, (SLOT, REL), 1)
    row, col = table[:, 0:1], table[:, 1:2]
    first, second = row * WIN, REL // 2 + col * WIN
    hot = (lane >= first) & (lane < first + WIN) & (row >= 0)
    hot = hot | ((lane >= second) & (lane < second + WIN) & (col >= 0))
    return jnp.where(hot, 1.0, 0.0).astype(BF16)


def key_columns(m, total):
    place = m.table[0:total, :]
    mask = m.mask[...].astype(F32).astype(BF16)
    rows = matmul(one_hot(place[:, 3:4], mask.shape[0]), mask)
    lane = lax.broadcasted_iota(jnp.int32, rows.shape, 1)
    valid = jnp.sum(jnp.where(lane == place[:, 4:5], rows, 0.0), axis=1, keepdims=True)
    lane = lax.broadcasted_iota(jnp.int32, m.key.shape, 1)
    hot = (lane == place[:, 0:1]) | ((lane == place[:, 1:2] + WIN) & (place[:, 1:2] >= 0))
    group = lane - 2 * WIN
    shut = ((group == 0) | (group == 1)) & ((valid < 0.5) | (place[:, 2:3] != group))
    m.key[...] = jnp.where(shut, -1e30, jnp.where(hot, 1.0, 0.0)).astype(BF16)


def pack_small(m, place, piece, wide):
    first, second = lane_place(piece, 128, place.col * piece), lane_place(wide, 384, place.col * wide)
    m.small[...] = jnp.zeros_like(m.small)
    m.small[0:8, 0:128] = matmul(m.vectors[...], first).astype(BF16)
    m.small[0:1, 128:512] = matmul(m.bias[...], second).astype(BF16)


def unpack_small(m, blocks, piece, wide):
    full = m.full[SMALL]
    vec = None
    for n in range(blocks):
        term = matmul(full[pl.ds(n * 16, 16), 0:piece], lane_place(piece, D, n * piece))
        vec = term if vec is None else vec + term
    m.vec[...] = vec
    per = 1 if wide % 128 == 0 else 4
    for n in range(0, blocks, per):
        row = None
        for j in range(per):
            block = full[pl.ds((n + j) * 16, 16), 128 : 128 + wide]
            term = block.astype(F32) if per == 1 else matmul(block, lane_place(wide, per * wide, j * wide))
            row = term if row is None else row + term
        m.b1[:, pl.ds(n * wide, per * wide)] = row[:8]


def split_small(m, blocks, piece, wide, ff):
    full = m.grad_small
    sums, db1 = m.sums[...].astype(BF16), m.db1[...].astype(BF16)
    full[...] = jnp.zeros_like(full)
    for n in range(blocks):
        rows = pl.ds(n * 16, 8)
        full[rows, 0:128] = matmul_nt(sums, lane_place(128, D, n * piece)).astype(BF16)
        if wide % 128 == 0:
            full[rows, 128 : 128 + wide] = db1[:, n * wide : (n + 1) * wide]
        else:
            first = n * wide // 128 * 128
            last = min(round_up(n * wide + wide, 128), ff)
            place = lane_place(128, last - first, n * wide - first)
            full[rows, 128:256] = matmul_nt(db1[:, first:last], place).astype(BF16)


def pick_cells(target, table, column, near, far, step):
    @pl.loop(0, target.shape[0] // step)
    def _(n):
        rows = pl.ds(pl.multiple_of(n * step, 16), step)
        index = table[rows, column : column + 1]
        here, there = one_hot(index, near.shape[0]), one_hot(index - near.shape[0], far.shape[0])
        target[rows, :] = (matmul(here, near[...]) + matmul(there, far[...])).astype(BF16)


def layer_kernel(plan, units, m):
    total, slots = plan["total"], plan["slots"]
    packed, landed = plan["packed"], plan["landed"]
    blocks = len(units) - FC1
    cells = m.in_tokens.shape[0]
    first = 0
    early = []
    for size in (cells, cells, packed, packed, landed, landed):
        early.append(m.dw_fc2.at[pl.ds(first, size)])
        first += size
    tiles, packets, arrivals = early[:2], early[2:4], early[4:]
    m.acc, m.do, m.gx = m.dr, m.n2, m.xs
    late = [m.fc2.at[pl.ds(n * total, total)] for n in range(4)]
    m.dq, m.dk, m.dv, m.out = late
    back_packets = [m.fc2.at[pl.ds(4 * total, landed)], m.fc2.at[pl.ds(0, landed)]]
    width = D // 3
    thirds_of = [pl.ds(third * width, width) for third in range(3)]
    full, halves = list(m.full), list(m.half)
    for third in range(3):
        full[FC2 + third], halves[FC2 + third] = m.fc2.at[:, thirds_of[third]], m.half_fc2.at[:, thirds_of[third]]
    grads = {PROJ: full[FC1 + 3], SMALL: m.grad_small}
    for third in range(3):
        grads[QKV + third] = full[FC1 + third]
        grads[FC2 + third] = m.dw_fc2.at[:, thirds_of[third]]
    for b in range(blocks):
        grads[FC1 + b] = m.dw_fc1[b]

    place = Place()
    me = place.row * place.cols + place.col
    table = pltpu.make_async_copy(m.in_table.at[me], m.table, m.local_sems.at[len(units)])
    table.start()
    loads = []
    for n, source in enumerate((m.in_tokens, m.in_cotangent)):
        loads.append(pltpu.make_async_copy(source, tiles[n], m.local_sems.at[len(units) + 1 + n]))
        loads[n].start()
    thirds = []
    for third in range(3):
        for n in range(3):
            source = m.w_qkv.at[:, pl.ds(n * D + third * width, width)]
            target = m.thirds[third].at[:, pl.ds(n * width, width)]
            thirds.append(pltpu.make_async_copy(source, target, m.third_sems.at[third * 3 + n]))
            thirds[-1].start()
    for n in range(2):
        arrivals[n][...] = jnp.zeros((landed, D), BF16)
        m.back_arrivals[n][...] = jnp.zeros((packed, D), BF16)
    heard = greet(place)
    copies = Copies(m.send_sems, m.recv_sems)
    line = Timeline()
    piece, wide = units[PROJ].rows, units[FC2].rows
    pack_small(m, place, piece, wide)
    moves = [Exchange(place, copies, plan, packets[n], arrivals[n], False) for n in range(2)]

    def post(n):
        packets[n][...] = matmul(one_hot(m.table[0:packed, 6:7], cells), tiles[n][...]).astype(BF16)
        moves[n].start()
        line.load(ALONG, 8.0)
        line.load(ACROSS, 5.0)
        line.spend(1.5)

    def receive(n):
        moves[n].wait()
        pick_cells((m.xs, m.gs)[n], m.table, 5, tiles[n], arrivals[n], SLOT)
        line.spend(2.0)

    shards = {SMALL: m.small, PROJ: m.w_proj}
    for third in range(3):
        shards[FC2 + third] = m.w_fc2.at[:, thirds_of[third]]
        shards[QKV + third] = m.thirds[third]
    for b in range(blocks):
        shards[FC1 + b] = m.w_fc1.at[:, pl.ds(b * D, D)]
    gathers = [
        Gather(place, copies, units[n], shards[n], full[n], m.stage[n], m.local_sems.at[n]) for n in range(len(units))
    ]
    outs = {PROJ: [m.g_proj], SMALL: [m.g_small]}
    for third in range(3):
        outs[FC2 + third] = [m.g_fc2.at[:, thirds_of[third]]]
        outs[QKV + third] = [m.g_qkv.at[:, pl.ds(n * D + third * width, width)] for n in range(3)]
    for b in range(blocks):
        outs[FC1 + b] = [m.g_fc1.at[:, pl.ds(b * D, D)]]
    scatters = {}

    def scatter(n):
        scatters[n] = Scatter(place, copies, units[n], grads[n], halves[n], m.buffers[n], m.stage[n], outs[n])
        line.launch(scatters[n])

    line.queue = list(gathers)
    for copy in thirds:
        copy.wait()
    pl.semaphore_wait(pltpu.get_barrier_semaphore(), heard)
    for n in range(2):
        line.launch(line.queue.pop(0))
    table.wait()
    loads[0].wait()
    post(0)
    m.fold[...] = fold_matrix()
    rel = jnp.concatenate([matmul_tn(r[...], m.select[...]).astype(BF16) for r in (m.rel_rows, m.rel_cols)], axis=1)
    m.rel[...] = jnp.concatenate([rel, rel], axis=0)
    key_columns(m, total)

    @pl.loop(0, slots)
    def _(s):
        m.own[slot_rows(s), :] = own_place(m.table[slot_rows(s), :])

    line.spend(4.0)
    line.need_time(12.0)
    receive(0)
    line.need(gathers[SMALL])
    small = units[SMALL]
    line_count = 2 * small.chips * small.row_count
    unpack_small(m, line_count, place.cols * piece, place.cols * wide)
    vec = m.vec

    @pl.loop(0, slots)
    def _(s):
        rows = slot_rows(s)
        hat, _ = normalized(m.xs[rows, :].astype(F32))
        m.n1[rows, :] = (hat * vec[0:1, :] + vec[1:2, :]).astype(BF16)

    line.spend(3.0)
    def pairs_of(s, pairs, function):
        @pl.loop(pairs.start, pairs.stop)
        def _(p):
            function(m, s, p)

    for third in range(3):
        line.need(gathers[QKV + third])
        lanes = pl.ds(third * width, width)
        for n, (target, bias) in enumerate(((m.q, vec[2:3, :]), (m.k, None), (m.v, vec[3:4, :]))):
            out = matmul(m.n1[...], m.full[QKV + third][:, pl.ds(n * width, width)])
            if bias is not None:
                out = out + bias[:, third * width : (third + 1) * width]
            target[:, lanes] = out.astype(BF16)
        line.spend(1.5)
        if third == 0:
            loads[1].wait()
            post(1)
        for s in range(slots):
            pairs_of(s, range(third * PAIRS // 3, (third + 1) * PAIRS // 3), attend)
            line.spend(2.1)
        if third == 1:
            receive(1)
    line.need(gathers[PROJ])

    @pl.loop(0, slots)
    def _(s):
        rows = slot_rows(s)
        r = m.xs[rows, :].astype(F32) + matmul(m.o[rows, :], m.full[PROJ][...]) + vec[4:5, :]
        m.r[rows, :] = r
        hat, _ = normalized(r)
        m.n2[rows, :] = (hat * vec[5:6, :] + vec[6:7, :]).astype(BF16)
        m.acc[rows, :] = r + vec[7:8, :]

    line.spend(4.5)
    for move in moves:
        move.finish()
    line.need(*gathers[FC2 : FC2 + 3])
    size = width
    for b in range(blocks):
        line.need(gathers[FC1 + b])
        for h in range(3):
            lanes, rows = pl.ds(h * size, size), pl.ds(b * D + h * size, size)
            w1, w2 = m.full[FC1 + b][:, lanes], m.fc2[rows, :]
            u = matmul(m.n2[...], w1) + m.b1[0:1, rows]
            half = 0.5 + 0.5 * lax.erf(u * 0.7071067811865476)
            a = (u * half).astype(BF16)
            m.acc[...] += matmul(a, w2)
            m.dw_fc2[rows, :] = matmul_tn(a, m.gs[...]).astype(BF16)
            slope = half + u * jnp.exp(u * u * -0.5) * 0.3989422804014327
            du = (matmul_nt(m.gs[...], w2) * slope).astype(BF16)
            m.db1[:, rows] = jnp.broadcast_to(column_sum(du.astype(F32)), (8, size))
            m.dw_fc1[b][:, lanes] = matmul_tn(m.n2[...], du).astype(BF16)
            term = matmul_nt(du, w1)
            if b == 0 and h == 0:
                m.dn2[...] = term
            else:
                m.dn2[...] += term
        line.spend(6.6)
        scatter(FC1 + b)
    for gather in gathers:
        gather.settle()
    for third in range(3):
        scatter(FC2 + third)

    m.sums[...] = jnp.zeros_like(m.sums)

    @pl.loop(0, slots)
    def _(s):
        rows = slot_rows(s)
        m.out[rows, :] = m.acc[rows, :].astype(BF16)
        hat, rate = normalized(m.r[rows, :])
        dn2, g = m.dn2[rows, :], m.gs[rows, :].astype(F32)
        m.sums[5:6, :] += column_sum(dn2 * hat)
        m.sums[6:7, :] += column_sum(dn2)
        m.sums[7:8, :] += column_sum(g)
        dr = g + norm_back(dn2, vec[5:6, :], hat, rate)
        m.dr[rows, :] = dr
        m.sums[4:5, :] += column_sum(dr.astype(BF16).astype(F32))

    line.spend(3.5)
    db = m.dr[...].astype(BF16)
    grads[PROJ][...] = matmul_tn(m.o[...], db).astype(BF16)
    scatter(PROJ)
    m.do[...] = matmul_nt(db, m.full[PROJ][...]).astype(BF16)
    line.spend(4.0)
    back_packets[0][...] = matmul(one_hot(m.table[0:landed, 7:8], total), m.out[...]).astype(BF16)
    moves = [Exchange(place, copies, plan, back_packets[n], m.back_arrivals[n], True) for n in range(2)]
    moves[0].start()
    line.spend(1.5)

    m.drel[...] = jnp.zeros_like(m.drel)
    dn1 = m.dn2
    for third in range(3):
        for s in range(slots):
            pairs_of(s, range(third * PAIRS // 3, (third + 1) * PAIRS // 3), attend_back)
            line.spend(2.3)
        own = pl.ds(third * width, width)
        for n, d in enumerate((m.dq, m.dk, m.dv)):
            lanes = pl.ds(n * width, width)
            grads[QKV + third][:, lanes] = matmul_tn(m.n1[...], d[:, own]).astype(BF16)
        line.spend(2.2)
        scatter(QKV + third)
        for n, d in enumerate((m.dq, m.dk, m.dv)):
            term = matmul_nt(d[:, own], m.full[QKV + third][:, pl.ds(n * width, width)])
            if third == 0 and n == 0:
                dn1[...] = term
            else:
                dn1[...] += term
        line.spend(1.9)
    drel = m.drel[:HEAD_DIM, :] + m.drel[HEAD_DIM:, :]
    for n in range(2):
        part = drel[:, n * (REL // 2) : (n + 1) * (REL // 2)]
        m.held[0, n] = lax.dot_general(
            m.select[...].astype(F32), part, (((1,), (1,)), ((), ())), preferred_element_type=F32,
            precision=lax.Precision.HIGHEST,
        )
    doubling = Doubling(place, copies, m.held, m.arriving)
    line.launch(doubling)

    @pl.loop(0, slots)
    def _(s):
        rows = slot_rows(s)
        hat, rate = normalized(m.xs[rows, :].astype(F32))
        d = dn1[rows, :]
        m.sums[0:1, :] += column_sum(d * hat)
        m.sums[1:2, :] += column_sum(d)
        m.sums[2:3, :] += column_sum(m.dq[rows, :].astype(F32))
        m.sums[3:4, :] += column_sum(m.dv[rows, :].astype(F32))
        m.gx[rows, :] = (m.dr[rows, :] + norm_back(d, vec[0:1, :], hat, rate)).astype(BF16)

    back_packets[1][...] = matmul(one_hot(m.table[0:landed, 7:8], total), m.gx[...]).astype(BF16)
    moves[1].start()
    line.spend(4.5)
    split_small(m, line_count, place.cols * piece, place.cols * wide, blocks * D)
    scatter(SMALL)
    stores = []
    results = [m.dk, m.dv]
    for n, source in enumerate((m.out, m.gx)):
        moves[n].wait()
        tile = results[n].at[pl.ds(0, cells)]
        pick_cells(tile, m.table, 8, source, m.back_arrivals[n], 128)
        stores.append(pltpu.make_async_copy(tile, (m.layer_out, m.grad_tokens)[n], m.local_sems.at[n]))
        stores[n].start()
        line.spend(2.0)
    line.finish()
    m.rel_sum[...] = m.held[doubling.last]
    lane_pick = lane_place(512, 512, -place.col * piece)
    lane_pick2 = lane_place(512, 512, -128 - place.col * wide)
    for target, picked in ((m.g_vec, lane_pick), (m.g_b1, lane_pick2)):
        target[...] = jnp.dot(
            m.g_small[...], picked[:, : target.shape[1]].astype(F32),
            preferred_element_type=F32, precision=lax.Precision.HIGHEST,
        )
    for op in [*scatters.values(), doubling]:
        op.settle()
    for move in moves:
        move.finish()
    for store in stores:
        store.wait()


def fold_matrix():
    row = lax.broadcasted_iota(jnp.int32, (REL, 128), 0)
    lane = lax.broadcasted_iota(jnp.int32, (REL, 128), 1)
    half = REL // 2
    inside = jnp.where(row < half, row, row - half)
    target = inside % WIN + jnp.where(row < half, 0, WIN)
    return jnp.where((lane == target) & (inside < CELLS), 1.0, 0.0).astype(BF16)


def body(
    image_tokens, cotangent, content_mask, norm1_gain, norm1_bias, qkv_weight, query_bias, value_bias,
    rel_rows, rel_cols, proj_weight, proj_bias, norm2_gain, norm2_bias, fc1_weight, fc1_bias, fc2_weight, fc2_bias,
):
    images, rows, cols = axis_sizes()
    _, tile_rows, tile_cols, _ = image_tokens.shape
    cells = tile_rows * tile_cols
    plan = plan_windows(rows, cols, tile_rows, tile_cols)
    total, slots, packed, landed = plan["total"], plan["slots"], plan["packed"], plan["landed"]
    piece, wide, ff = qkv_weight.shape[0], fc2_weight.shape[0], fc1_weight.shape[1]
    blocks = ff // D
    line = Unit(piece, D, ROWS)
    part = Unit(wide, D // 3, ROWS if wide % 16 else PLAIN)
    units = [Unit(16, 512, SUM), line, line, line, line, part, part, part] + [line] * blocks

    height = max(total, packed, landed, cells)
    table = np.full((rows * cols, height, 16), -1, np.int32)
    table[:, :total, :5] = plan["where"][:, :, :5]
    for n, name in enumerate(("slot_from", "pack_from", "back_from", "tile_from")):
        table[:, : plan[name].shape[1], 5 + n] = plan[name]
    index = np.arange(WIN)[:, None] - np.arange(WIN)[None, :] + WIN - 1
    span = rel_rows.shape[0]
    select = np.zeros((span, REL // 2), np.float32)
    select[index.reshape(-1), np.arange(CELLS)] = 1
    vectors = [norm1_gain, norm1_bias, query_bias, value_bias, proj_bias, norm2_gain, norm2_bias, fc2_bias]

    def everywhere(value):
        return Item(value, space=pl.ANY)

    def vmem(*shape, kind=BF16):
        return Item(shape, kind)

    inputs = dict(
        in_tokens=everywhere(image_tokens.reshape(cells, D)), in_cotangent=everywhere(cotangent.reshape(cells, D)),
        in_table=everywhere(jnp.asarray(table)), mask=Item(content_mask[0]), vectors=Item(jnp.stack(vectors)), bias=Item(fc1_bias[None]),
        rel_rows=Item(rel_rows), rel_cols=Item(rel_cols), select=Item(jnp.asarray(select, BF16)),
        w_qkv=everywhere(qkv_weight), w_proj=everywhere(proj_weight), w_fc1=everywhere(fc1_weight), w_fc2=everywhere(fc2_weight),
    )
    outputs = dict(
        layer_out=Item((cells, D), BF16, pl.ANY), grad_tokens=Item((cells, D), BF16, pl.ANY),
        g_qkv=vmem(piece, 3 * D, kind=F32), g_proj=vmem(piece, D, kind=F32),
        g_fc1=vmem(piece, ff, kind=F32), g_fc2=vmem(wide, D, kind=F32),
        g_vec=vmem(16, 128, kind=F32), g_b1=vmem(16, round_up(wide, 128), kind=F32), rel_sum=vmem(2, span, HEAD_DIM, kind=F32),
    )
    swaps = (images * rows * cols).bit_length() - 1
    count = sum(u.copies() for u in units) + swaps + 4 * len(plan["pairs"])
    sems = pltpu.SemaphoreType.DMA
    scratch = dict(
        table=vmem(height, 16, kind=jnp.int32), small=vmem(16, 512), thirds=[vmem(piece, D)] * 3, third_sems=Item(pltpu.SemaphoreType.DMA((9,))), rel=vmem(2 * HEAD_DIM, REL), fold=vmem(REL, 128),
        xs=vmem(total, D), gs=vmem(total, D), n1=vmem(total, D), q=vmem(total, D), k=vmem(total, D), v=vmem(total, D),
        key=vmem(total, 128), soft=vmem(slots * PAIRS, 2 * SLOT, SLOT), o=vmem(total, D), n2=vmem(total, D),
        r=vmem(total, D, kind=F32), dr=vmem(total, D, kind=F32), dn2=vmem(total, D, kind=F32), own=vmem(total, REL),
        vec=vmem(16, D, kind=F32), b1=vmem(8, ff, kind=F32), db1=vmem(8, ff, kind=F32), sums=vmem(8, D, kind=F32),
        drel=vmem(2 * HEAD_DIM, REL, kind=F32), held=vmem(swaps + 1, 2, span, HEAD_DIM, kind=F32),
        arriving=vmem(swaps, 2, span, HEAD_DIM, kind=F32), g_small=vmem(16, 512, kind=F32),
        grad_small=vmem(*units[SMALL].full_shape()), back_arrivals=[vmem(packed, D)] * 2,
        full=[vmem(*(u.full_shape() if u is not part else (8, 128))) for u in units],
        half=[vmem(*(u.half_shape() if u is not part else (8, 128))) for u in units],
        fc2=vmem(ff, D), half_fc2=vmem(ff // 2, D),
        stage=[vmem(*(u.stage_shape() if u.mode != PLAIN else (8, 128))) for u in units],
        buffers=[[vmem(*shape) for shape in u.buffer_shapes()] for u in units],
        dw_fc1=[vmem(*line.full_shape())] * blocks, dw_fc2=vmem(ff, D),
        send_sems=Item(sems((count,))), recv_sems=Item(sems((count,))), local_sems=Item(sems((len(units) + 3,))),
    )
    done = run(functools.partial(layer_kernel, plan, units), inputs, outputs, scratch)
    g_vec, g_b1 = done.g_vec[:8, :piece], done.g_b1[0, :wide]
    return (
        done.layer_out.reshape(image_tokens.shape), done.grad_tokens.reshape(image_tokens.shape),
        g_vec[0], g_vec[1], done.g_qkv, g_vec[2], g_vec[3], done.rel_sum[0], done.rel_sum[1],
        done.g_proj, g_vec[4], g_vec[5], g_vec[6], done.g_fc1, g_b1, done.g_fc2, g_vec[7],
    )


def solution(mesh):
    everywhere = ("img", "row", "col")
    tile, vector, matrix = P("img", "row", "col", None), P(everywhere), P(everywhere, None)
    in_specs = (
        tile, tile, P("img", None, None), vector, vector, matrix, vector, vector, P(), P(),
        matrix, vector, vector, vector, matrix, vector, matrix, vector,
    )
    out_specs = (
        tile, tile, vector, vector, matrix, vector, vector, P(), P(),
        matrix, vector, vector, vector, matrix, vector, matrix, vector,
    )
    return jax.shard_map(body, mesh=mesh, in_specs=in_specs, out_specs=out_specs, check_vma=False)
```

```python
import functools
import types

import jax
import jax.numpy as jnp
import numpy as np
from jax import lax
from jax.experimental import pallas as pl
from jax.experimental.pallas import tpu as pltpu
from jax.sharding import PartitionSpec as P

D = 768
HEADS = 12
HEAD_DIM = 64
PAIRS = HEADS // 2
WIN = 14
CELLS = WIN * WIN
SLOT = 208
MESH = pl.DeviceIdType.MESH
F32 = jnp.float32
BF16 = jnp.bfloat16
VMEM_LIMIT = 62 * 2**20


def round_up(value, unit):
    return -(-value // unit) * unit


def plan_windows(rows, cols, tile_rows, tile_cols):
    devices = rows * cols
    height, width = rows * tile_rows, cols * tile_cols
    windows = []
    for top in range(0, height, WIN):
        for left in range(0, width, WIN):
            windows.append(
                [
                    (r, c, r - top, c - left)
                    for r in range(top, min(top + WIN, height))
                    for c in range(left, min(left + WIN, width))
                ]
            )
    bins = []
    for window in sorted(windows, key=len, reverse=True):
        for held in bins:
            if len(held) < 2 and sum(map(len, held)) + len(window) <= CELLS:
                held.append(window)
                break
        else:
            bins.append([window])
    slots = -(-len(bins) // devices)
    while len(bins) < slots * devices:
        bins.append([])

    def home(cell):
        return cell[0] // tile_rows * cols + cell[1] // tile_cols

    weights = np.zeros((len(bins), devices), np.int64)
    for number, held in enumerate(bins):
        for window in held:
            for cell in window:
                weights[number, home(cell)] += 1
    hops = np.zeros((devices, devices, rows * rows * cols + cols * cols * rows))
    for source in range(devices):
        for target in range(devices):
            r0, c0, r1, c1 = source // cols, source % cols, target // cols, target % cols
            step = 1 if r1 > r0 else -1
            for r in range(r0, r1, step):
                hops[source, target, (r * rows + r + step) * cols + c0] = 1
            step = 1 if c1 > c0 else -1
            for c in range(c0, c1, step):
                hops[source, target, rows * rows * cols + (c * cols + c + step) * rows + r1] = 1
    loads = np.einsum("bs,sdl->bdl", weights, hops)

    def cost(order):
        load = loads[np.arange(len(bins)), np.array(order) // slots].sum(axis=0)
        return load.max() * 100 + load.sum()

    order = [0] * len(bins)
    free = [slots] * devices
    for number in range(len(bins)):
        options = [d for d in range(devices) if free[d]]
        best = min(options, key=lambda d: (loads[number, d].sum(), d))
        order[number] = best * slots + slots - free[best]
        free[best] -= 1
    current = cost(order)
    while True:
        found = None
        for a in range(len(bins)):
            for b in range(a):
                if order[a] // slots != order[b] // slots:
                    order[a], order[b] = order[b], order[a]
                    trial = cost(order)
                    if trial < current:
                        current, found = trial, (a, b)
                    order[a], order[b] = order[b], order[a]
        if found is None:
            break
        a, b = found
        order[a], order[b] = order[b], order[a]
    total = slots * SLOT
    place = [[] for _ in range(devices)]
    for number in sorted(range(len(bins)), key=lambda n: order[n]):
        device, slot = order[number] // slots, order[number] % slots
        position = slot * SLOT
        for group, window in enumerate(bins[number]):
            for cell in window:
                place[device].append((position, cell, group))
                position += 1
    cells = tile_rows * tile_cols
    pairs = []
    sent, got = [0] * devices, [0] * devices
    moved = {}
    for source in range(devices):
        for target in range(devices):
            if source != target:
                listed = [e for e in place[target] if home(e[1]) == source]
                if listed:
                    count = round_up(len(listed), 16)
                    pairs.append((source, target, sent[source], got[target], count))
                    moved[source, target] = (listed, sent[source], got[target])
                    sent[source] += count
                    got[target] += count
    packed, landed = round_up(max(sent), 128), round_up(max(got), 128)
    pack_from = np.full((devices, packed), -1, np.int32)
    slot_from = np.full((devices, total), -1, np.int32)
    back_from = np.full((devices, landed), -1, np.int32)
    tile_from = np.full((devices, cells), -1, np.int32)
    where = np.full((devices, total, 8), -1, np.int32)
    for device in range(devices):
        for position, cell, group in place[device]:
            where[device, position, :5] = (cell[2], cell[3], group, cell[0], cell[1])
            if home(cell) == device:
                local = cell[0] % tile_rows * tile_cols + cell[1] % tile_cols
                slot_from[device, position] = local
                tile_from[device, local] = position
    for (source, target), (listed, out, into) in moved.items():
        for k, (position, cell, group) in enumerate(listed):
            local = cell[0] % tile_rows * tile_cols + cell[1] % tile_cols
            pack_from[source, out + k] = local
            slot_from[target, position] = cells + into + k
            back_from[target, into + k] = position
            tile_from[source, local] = total + out + k
    return dict(
        slots=slots, total=total, pairs=pairs, packed=packed, landed=landed, where=where,
        pack_from=pack_from, slot_from=slot_from, back_from=back_from, tile_from=tile_from,
    )


def matmul(a, b):
    return jnp.dot(a, b, preferred_element_type=F32)


def matmul_nt(a, b):
    return lax.dot_general(a, b, (((1,), (1,)), ((), ())), preferred_element_type=F32)


def matmul_tn(a, b):
    return lax.dot_general(a, b, (((0,), (0,)), ((), ())), preferred_element_type=F32)


def one_hot(index, width):
    return (index == lax.broadcasted_iota(jnp.int32, (index.shape[0], width), 1)).astype(BF16)


def normalized(values):
    offset = values - jnp.mean(values, axis=-1, keepdims=True)
    rate = lax.rsqrt(jnp.mean(offset * offset, axis=-1, keepdims=True) + 1e-06)
    return offset * rate, rate


def norm_back(cotangent, gain, hat, rate):
    e = cotangent * gain
    mean_e = jnp.mean(e, axis=-1, keepdims=True)
    mean_eh = jnp.mean(e * hat, axis=-1, keepdims=True)
    return rate * (e - mean_e - hat * mean_eh)


def column_sum(values):
    return jnp.sum(values, axis=0, keepdims=True)


def params(**more):
    return pltpu.CompilerParams(vmem_limit_bytes=VMEM_LIMIT, **more)


def head_halves(pair):
    low = lax.broadcasted_iota(jnp.int32, pair.shape, 1) < HEAD_DIM
    zero = jnp.zeros_like(pair)
    return jnp.concatenate([jnp.where(low, pair, zero), jnp.where(low, zero, pair)], axis=0)


def join_halves(stacked):
    low = lax.broadcasted_iota(jnp.int32, (SLOT, 2 * HEAD_DIM), 1) < HEAD_DIM
    return jnp.where(low, stacked[:SLOT], stacked[SLOT:])


REL = 512


def axis_sizes():
    return lax.axis_size("img"), lax.axis_size("row"), lax.axis_size("col")


class Place:
    def __init__(self):
        images, self.rows, self.cols = axis_sizes()
        self.chips = images // 2
        img = lax.axis_index("img")
        self.chip, self.core = img // 2, img % 2
        self.row, self.col = lax.axis_index("row"), lax.axis_index("col")

    def other(self, axis, k):
        if axis == "row":
            index = (self.row + k) % self.rows
            return index, {"row": index}
        if axis == "col":
            index = (self.col + k) % self.cols
            return index, {"col": index}
        index = (self.chip + k) % self.chips
        return index, {"img": index * 2 + self.core}

    def sibling(self):
        return {"img": self.chip * 2 + 1 - self.core}

    def count(self, axis):
        return {"row": self.rows, "col": self.cols, "chip": self.chips}[axis]


def greet(place):
    barrier = pltpu.get_barrier_semaphore()
    heard = 1
    pl.semaphore_signal(barrier, inc=1, device_id=place.sibling(), device_id_type=MESH)
    for k in range(1, place.chips):
        pl.semaphore_signal(barrier, inc=1, device_id=place.other("img", k)[1], device_id_type=MESH)
        heard += 1
    for r in range(place.rows):
        for c in range(place.cols):
            if (r, c) == (0, 0):
                continue
            target = {"row": (place.row + r) % place.rows, "col": (place.col + c) % place.cols}
            pl.semaphore_signal(barrier, inc=1, device_id=target, device_id_type=MESH)
            heard += 1
    return heard


class Copies:
    def __init__(self, send_sems, recv_sems):
        self.send_sems, self.recv_sems = send_sems, recv_sems
        self.used = 0

    def start(self, source, target, device):
        copy = pltpu.make_async_remote_copy(
            src_ref=source,
            dst_ref=target,
            send_sem=self.send_sems.at[self.used],
            recv_sem=self.recv_sems.at[self.used],
            device_id=device,
            device_id_type=MESH,
        )
        self.used += 1
        copy.start()
        return copy


def swap_steps(place):
    steps = [place.sibling()]
    bit = 1
    while bit < place.chips:
        flip = place.chip + bit - 2 * bit * (place.chip // bit % 2)
        steps.append({"img": flip * 2 + place.core})
        bit *= 2
    bit = 1
    while bit < place.rows:
        steps.append({"row": place.row + bit - 2 * bit * (place.row // bit % 2)})
        bit *= 2
    bit = 1
    while bit < place.cols:
        steps.append({"col": place.col + bit - 2 * bit * (place.col // bit % 2)})
        bit *= 2
    return steps


SMALL, QKV, _, _, PROJ, FC2, _, _, FC1 = range(9)
ROWS, PLAIN, SUM = range(3)
ALONG, ACROSS, CORES = range(3)


class Unit:
    def __init__(self, rows, width, mode):
        self.rows, self.width, self.mode = rows, width, mode
        images, self.row_count, self.col_count = axis_sizes()
        self.chips = images // 2
        self.block = rows if mode == SUM else rows * self.col_count
        self.line = self.block * self.row_count
        self.half = width // 2
        self.low, self.high = pl.ds(0, self.half), pl.ds(self.half, width - self.half)
        self.size = 2 * self.chips * self.line * width / (D * D)

    def full_shape(self):
        return (2 * self.chips * self.line, self.width)

    def half_shape(self):
        return (self.chips * self.line, self.width)

    def stage_shape(self):
        return (self.col_count, self.rows, self.width)

    def buffer_shapes(self):
        c, r, n = self.chips, self.row_count, self.col_count
        return [
            (c - 1, self.line, self.half),
            (r - 1, c, self.block, self.half),
            (r - 1, self.block, self.half),
            (c - 1, self.block, self.half),
            (n - 1, self.rows, self.width),
        ]

    def rows_at(self, index, count=1):
        return pl.ds(pl.multiple_of(index * self.block, 8), count * self.block)

    def copies(self):
        c, r, n = self.chips, self.row_count, self.col_count
        return 2 * ((n - 1) + (r - 1) + (c - 1) + (c - 1) + (r - 1) * c + c)

    def spread(self, k):
        row = lax.broadcasted_iota(jnp.int32, (self.block, self.rows), 0)
        col = lax.broadcasted_iota(jnp.int32, (self.block, self.rows), 1)
        return jnp.where(row == col + k * self.rows, 1.0, 0.0).astype(BF16)


class Phased:
    last = 4

    def __init__(self, place, copies):
        self.place, self.copies = place, copies
        self.phase, self.waiting, self.sent = 0, [], []

    @property
    def done(self):
        return self.phase > self.last

    def send(self, source, target, device):
        copy = self.copies.start(source, target, device)
        self.waiting.append(copy)
        self.sent.append(copy)

    def advance(self):
        for copy in self.waiting:
            copy.wait_recv()
        self.waiting = []
        self.step()
        self.phase += 1

    def settle(self):
        for copy in self.sent:
            copy.wait_send()
        self.sent = []


class Gather(Phased):
    def __init__(self, place, copies, unit, shard, full, stage, local):
        super().__init__(place, copies)
        self.unit, self.shard, self.full, self.stage, self.local = unit, shard, full, stage, local

    def cost(self):
        size = self.unit.size
        return [(ALONG, 3.3 * size), (ACROSS, 1.7 * size), (ACROSS, 3.3 * size), (CORES, 0.95 * size), None][self.phase - 1]

    def step(self):
        place, unit, full = self.place, self.unit, self.full
        y, c, x, z = place.chip, place.core, place.row, place.col
        own = unit.rows_at((y * 2 + c) * place.rows + x)
        if self.phase == 0:
            if unit.mode == PLAIN:
                first = ((y * 2 + c) * place.rows + x) * unit.block + z * unit.rows
                target = full.at[pl.ds(pl.multiple_of(first, 8), unit.rows)]
            else:
                target = self.stage.at[z]
            self.keep = pltpu.make_async_copy(self.shard, target, self.local)
            self.keep.start()
            for k in range(1, place.cols):
                self.send(self.shard, target, place.other("col", k)[1])
        if self.phase == 1:
            self.keep.wait()
            if unit.mode != PLAIN:
                total = None
                for k in range(place.cols):
                    slab = self.stage[k]
                    term = slab.astype(F32) if unit.mode == SUM else matmul(unit.spread(k), slab)
                    total = term if total is None else total + term
                full[own, :] = total.astype(BF16)
            for k in range(1, place.rows):
                part = full.at[own, unit.low]
                self.send(part, part, place.other("row", k)[1])
            for k in range(1, place.chips):
                part = full.at[own, unit.high]
                self.send(part, part, place.other("img", k)[1])
        if self.phase == 2:
            for k in range(1, place.chips):
                part = full.at[unit.rows_at((y * 2 + c) * place.rows, place.rows), unit.low]
                self.send(part, part, place.other("img", k)[1])
            for k in range(1, place.rows):
                for chip in range(place.chips):
                    part = full.at[unit.rows_at((chip * 2 + c) * place.rows + x), unit.high]
                    self.send(part, part, place.other("row", k)[1])
        if self.phase == 3:
            for chip in range(place.chips):
                part = full.at[unit.rows_at((chip * 2 + c) * place.rows, place.rows)]
                self.send(part, part, place.sibling())


def add_rows(ref, start, count, lanes, terms):
    step = 32 if count % 32 == 0 else count

    def add(first):
        rows = pl.ds(pl.multiple_of(start + first, 8), step)
        total = ref[rows, lanes].astype(F32)
        for term in terms:
            total = total + term(pl.ds(pl.multiple_of(first, 8), step)).astype(F32)
        ref[rows, lanes] = total.astype(BF16)

    if step == count:
        add(0)
    else:
        pl.loop(0, count // step)(lambda n: add(n * step))


class Scatter(Phased):
    def __init__(self, place, copies, unit, full, half, buffers, cut, out):
        super().__init__(place, copies)
        self.unit, self.full, self.half, self.buffers, self.cut, self.out = unit, full, half, buffers, cut, out

    def cost(self):
        size = self.unit.size
        return [(CORES, 0.95 * size), (ACROSS, 3.3 * size), (ACROSS, 1.7 * size), (ALONG, 3.3 * size), None][self.phase - 1]

    def step(self):
        place, unit, half = self.place, self.unit, self.half
        y, c, x, z = place.chip, place.core, place.row, place.col
        low_chip, high_row, low_row, high_chip, along = self.buffers
        own = unit.rows_at(y * place.rows + x)

        def slab(index):
            if unit.mode == ROWS:
                return self.cut, index
            if unit.mode == SUM:
                return half, own
            first = (y * place.rows + x) * unit.block + index * unit.rows
            return half, pl.ds(pl.multiple_of(first, 8), unit.rows)

        if self.phase == 0:
            for chip in range(place.chips):
                part = self.full.at[unit.rows_at((chip * 2 + 1 - c) * place.rows, place.rows)]
                self.send(part, half.at[unit.rows_at(chip * place.rows, place.rows)], place.sibling())
        if self.phase == 1:
            for chip in range(place.chips):
                first = (chip * 2 + c) * unit.line
                term = lambda rows, first=first: self.full[pl.ds(pl.multiple_of(first + rows.start, 8), rows.size), :]
                add_rows(half, chip * unit.line, unit.line, slice(None), [term])
            for k in range(1, place.chips):
                to, device = place.other("img", k)
                part = half.at[unit.rows_at(to * place.rows, place.rows), unit.low]
                self.send(part, low_chip.at[k - 1], device)
            for k in range(1, place.rows):
                to, device = place.other("row", k)
                for chip in range(place.chips):
                    part = half.at[unit.rows_at(chip * place.rows + to), unit.high]
                    self.send(part, high_row.at[k - 1, chip], device)
        if self.phase == 2:
            terms = [lambda rows, k=k: low_chip[k, rows, :] for k in range(place.chips - 1)]
            add_rows(half, y * unit.line, unit.line, unit.low, terms)
            for chip in range(place.chips):
                terms = [lambda rows, k=k, chip=chip: high_row[k, chip, rows, :] for k in range(place.rows - 1)]
                add_rows(half, chip * unit.line + x * unit.block, unit.block, unit.high, terms)
            for k in range(1, place.rows):
                to, device = place.other("row", k)
                self.send(half.at[unit.rows_at(y * place.rows + to), unit.low], low_row.at[k - 1], device)
            for k in range(1, place.chips):
                to, device = place.other("img", k)
                self.send(half.at[unit.rows_at(to * place.rows + x), unit.high], high_chip.at[k - 1], device)
        if self.phase == 3:
            first = (y * place.rows + x) * unit.block
            terms = [lambda rows, k=k: low_row[k, rows, :] for k in range(place.rows - 1)]
            add_rows(half, first, unit.block, unit.low, terms)
            terms = [lambda rows, k=k: high_chip[k, rows, :] for k in range(place.chips - 1)]
            add_rows(half, first, unit.block, unit.high, terms)
            if unit.mode == ROWS:
                block = half[own, :]
                for k in range(place.cols):
                    self.cut[k] = matmul_tn(unit.spread(k), block).astype(BF16)
            for k in range(1, place.cols):
                to, device = place.other("col", k)
                ref, at = slab(to)
                self.send(ref.at[at], along.at[k - 1], device)
        if self.phase == 4:
            ref, at = slab(z)
            total = ref[at].astype(F32)
            for k in range(place.cols - 1):
                total = total + along[k].astype(F32)
            first = 0
            for out in self.out:
                out[...] = total[:, first : first + out.shape[1]]
                first += out.shape[1]


class Doubling(Phased):
    def __init__(self, place, copies, held, arriving):
        super().__init__(place, copies)
        self.held, self.arriving = held, arriving
        self.partners = swap_steps(place)
        self.last = len(self.partners)

    def cost(self):
        return None if self.done else (CORES, 0.5)

    def step(self):
        n = self.phase
        if n > 0:
            self.held[n] = self.held[n - 1] + self.arriving[n - 1]
        if n < len(self.partners):
            self.send(self.held.at[n], self.arriving.at[n], self.partners[n])


class Exchange:
    def __init__(self, place, copies, plan, source, target, back):
        self.me = place.row * place.cols + place.col
        self.first, self.copies, self.cols = copies.used, copies, place.cols
        copies.used += len(plan["pairs"])
        self.pairs, self.source, self.target, self.back = plan["pairs"], source, target, back

    def listed(self):
        for number, (giver, taker, out, into, count) in enumerate(self.pairs):
            if self.back:
                giver, taker, out, into = taker, giver, into, out
            copy = pltpu.make_async_remote_copy(
                src_ref=self.source.at[pl.ds(out, count)],
                dst_ref=self.target.at[pl.ds(into, count)],
                send_sem=self.copies.send_sems.at[self.first + number],
                recv_sem=self.copies.recv_sems.at[self.first + number],
                device_id={"row": taker // self.cols, "col": taker % self.cols},
                device_id_type=MESH,
            )
            yield giver, taker, copy

    def start(self):
        for giver, taker, copy in self.listed():
            pl.when(self.me == giver)(copy.start)

    def wait(self):
        for giver, taker, copy in self.listed():
            pl.when(self.me == taker)(copy.wait_recv)

    def finish(self):
        for giver, taker, copy in self.listed():
            pl.when(self.me == giver)(copy.wait_send)


class Timeline:
    def __init__(self):
        self.now, self.free, self.flying, self.queue = 0.0, [0.0, 0.0, 0.0], [], []

    def load(self, server, time):
        self.free[server] = max(self.free[server], self.now) + time

    def need_time(self, time):
        if self.now < time:
            self.spend(time - self.now)

    def launch(self, op):
        op.advance()
        if not op.done:
            server, time = op.cost()
            early = isinstance(op, Gather)
            self.free[server] = max(self.free[server], self.now) + time * (0.8 if early else 0.8)
            self.flying.append((self.free[server] + (2.0 if early else 2.0), len(self.flying), op))

    def next_up(self):
        entry = min(self.flying, key=lambda e: e[:2])
        self.flying.remove(entry)
        return entry

    def poll(self):
        while True:
            while self.queue and self.free[ALONG] < self.now:
                self.launch(self.queue.pop(0))
            if not self.flying or min(e[0] for e in self.flying) > self.now:
                return
            self.launch(self.next_up()[2])

    def spend(self, time):
        self.now += time
        self.poll()

    def need(self, *ops):
        while not all(op.done for op in ops):
            if not self.flying:
                self.launch(self.queue.pop(0))
                continue
            entry = self.next_up()
            self.now = max(self.now, entry[0])
            self.launch(entry[2])
            self.poll()

    def finish(self):
        while self.flying:
            entry = self.next_up()
            self.now = max(self.now, entry[0])
            self.launch(entry[2])


class Item:
    def __init__(self, value, kind=None, space=pltpu.VMEM):
        self.value, self.kind, self.space = value, kind, space


def run(kernel, inputs, outputs, scratch):
    leaves, tree = jax.tree.flatten((inputs, outputs, scratch))
    ins, outs = jax.tree.leaves(inputs), jax.tree.leaves(outputs)

    def wrapped(*refs):
        named = jax.tree.unflatten(tree, refs)
        kernel(types.SimpleNamespace(**named[0], **named[1], **named[2]))

    results = pl.pallas_call(
        wrapped,
        out_shape=[jax.ShapeDtypeStruct(item.value, item.kind) for item in outs],
        in_specs=[pl.BlockSpec(memory_space=item.space) for item in ins],
        out_specs=[pl.BlockSpec(memory_space=item.space) for item in outs],
        scratch_shapes=[
            item.value if item.kind is None else item.space(item.value, item.kind) for item in leaves[len(ins) + len(outs) :]
        ],
        compiler_params=params(collective_id=0, has_side_effects=True),
    )(*[item.value for item in ins])
    return types.SimpleNamespace(**jax.tree.unflatten(jax.tree.structure(outputs), results))


def lane_place(rows, width, first):
    lane = lax.broadcasted_iota(jnp.int32, (rows, width), 1)
    row = lax.broadcasted_iota(jnp.int32, (rows, width), 0)
    return jnp.where(lane == row + first, 1.0, 0.0).astype(BF16)


def slot_rows(s):
    return pl.ds(pl.multiple_of(s * SLOT, SLOT), SLOT)


def pair_lanes(p):
    return pl.ds(pl.multiple_of(p * 128, 128), 128)


def attend(m, s, p):
    rows, at = slot_rows(s), pair_lanes(p)
    own2 = jnp.concatenate([m.own[rows, :], m.own[rows, :]], axis=0)
    qs = head_halves(m.q[rows, at])
    spread = matmul(qs, m.rel[...]).astype(BF16) * own2
    group = lax.broadcasted_iota(jnp.int32, (SLOT, 128), 1) - 2 * WIN
    second = m.table[rows, 2:3] == 1
    mark = jnp.where(((group == 0) & ~second) | ((group == 1) & second), 1.0, 0.0)
    near = matmul(spread, m.fold[...]) + jnp.concatenate([mark, mark], axis=0)
    left = jnp.concatenate([qs * BF16(0.125), near.astype(BF16)], axis=1)
    right = jnp.concatenate([m.k[rows, at], m.key[rows, :]], axis=1)
    scores = matmul_nt(left, right)
    weight = jnp.exp(scores - jnp.max(scores, axis=-1, keepdims=True))
    soft = (weight / jnp.sum(weight, axis=-1, keepdims=True)).astype(BF16)
    m.soft[s * PAIRS + p] = soft
    m.o[rows, at] = join_halves(matmul(soft, m.v[rows, at])).astype(BF16)


def attend_back(m, s, p):
    rows, at = slot_rows(s), pair_lanes(p)
    own2 = jnp.concatenate([m.own[rows, :], m.own[rows, :]], axis=0)
    qs, dos = head_halves(m.q[rows, at]), head_halves(m.do[rows, at])
    o = m.o[rows, at].astype(F32)
    soft = m.soft[s * PAIRS + p]
    inner = jnp.sum(dos.astype(F32) * jnp.concatenate([o, o], axis=0), axis=-1, keepdims=True)
    ds = (soft.astype(F32) * (matmul_nt(dos, m.v[rows, at]) - inner)).astype(BF16)
    right = jnp.concatenate([m.k[rows, at], m.key[rows, :]], axis=1)
    back = matmul(ds, right)
    spread = matmul_nt(back[:, 128:].astype(BF16), m.fold[...]).astype(BF16) * own2
    dq = back[:, :128] * 0.125 + matmul_nt(spread, m.rel[...])
    m.dq[rows, at] = join_halves(dq).astype(BF16)
    m.drel[...] += matmul_tn(qs, spread)
    m.dk[rows, at] = (matmul_tn(ds, qs) * 0.125).astype(BF16)
    m.dv[rows, at] = matmul_tn(soft, dos).astype(BF16)


def own_place(table):
    lane = lax.broadcasted_iota(jnp.int32, (SLOT, REL), 1)
    row, col = table[:, 0:1], table[:, 1:2]
    first, second = row * WIN, REL // 2 + col * WIN
    hot = (lane >= first) & (lane < first + WIN) & (row >= 0)
    hot = hot | ((lane >= second) & (lane < second + WIN) & (col >= 0))
    return jnp.where(hot, 1.0, 0.0).astype(BF16)


def key_columns(m, total):
    place = m.table[0:total, :]
    mask = m.mask[...].astype(F32).astype(BF16)
    rows = matmul(one_hot(place[:, 3:4], mask.shape[0]), mask)
    lane = lax.broadcasted_iota(jnp.int32, rows.shape, 1)
    valid = jnp.sum(jnp.where(lane == place[:, 4:5], rows, 0.0), axis=1, keepdims=True)
    lane = lax.broadcasted_iota(jnp.int32, m.key.shape, 1)
    hot = (lane == place[:, 0:1]) | ((lane == place[:, 1:2] + WIN) & (place[:, 1:2] >= 0))
    group = lane - 2 * WIN
    shut = ((group == 0) | (group == 1)) & ((valid < 0.5) | (place[:, 2:3] != group))
    m.key[...] = jnp.where(shut, -1e30, jnp.where(hot, 1.0, 0.0)).astype(BF16)


def pack_small(m, place, piece, wide):
    first, second = lane_place(piece, 128, place.col * piece), lane_place(wide, 384, place.col * wide)
    m.small[...] = jnp.zeros_like(m.small)
    m.small[0:8, 0:128] = matmul(m.vectors[...], first).astype(BF16)
    m.small[0:1, 128:512] = matmul(m.bias[...], second).astype(BF16)


def unpack_small(m, blocks, piece, wide):
    full = m.full[SMALL]
    vec = None
    for n in range(blocks):
        term = matmul(full[pl.ds(n * 16, 16), 0:piece], lane_place(piece, D, n * piece))
        vec = term if vec is None else vec + term
    m.vec[...] = vec
    per = 1 if wide % 128 == 0 else 4
    for n in range(0, blocks, per):
        row = None
        for j in range(per):
            block = full[pl.ds((n + j) * 16, 16), 128 : 128 + wide]
            term = block.astype(F32) if per == 1 else matmul(block, lane_place(wide, per * wide, j * wide))
            row = term if row is None else row + term
        m.b1[:, pl.ds(n * wide, per * wide)] = row[:8]


def split_small(m, blocks, piece, wide, ff):
    full = m.grad_small
    sums, db1 = m.sums[...].astype(BF16), m.db1[...].astype(BF16)
    full[...] = jnp.zeros_like(full)
    for n in range(blocks):
        rows = pl.ds(n * 16, 8)
        full[rows, 0:128] = matmul_nt(sums, lane_place(128, D, n * piece)).astype(BF16)
        if wide % 128 == 0:
            full[rows, 128 : 128 + wide] = db1[:, n * wide : (n + 1) * wide]
        else:
            first = n * wide // 128 * 128
            last = min(round_up(n * wide + wide, 128), ff)
            place = lane_place(128, last - first, n * wide - first)
            full[rows, 128:256] = matmul_nt(db1[:, first:last], place).astype(BF16)


def pick_cells(target, table, column, near, far, step):
    @pl.loop(0, target.shape[0] // step)
    def _(n):
        rows = pl.ds(pl.multiple_of(n * step, 16), step)
        index = table[rows, column : column + 1]
        here, there = one_hot(index, near.shape[0]), one_hot(index - near.shape[0], far.shape[0])
        target[rows, :] = (matmul(here, near[...]) + matmul(there, far[...])).astype(BF16)


def layer_kernel(plan, units, m):
    total, slots = plan["total"], plan["slots"]
    packed, landed = plan["packed"], plan["landed"]
    blocks = len(units) - FC1
    cells = m.in_tokens.shape[0]
    first = 0
    early = []
    for size in (cells, cells, packed, packed, landed, landed):
        early.append(m.dw_fc2.at[pl.ds(first, size)])
        first += size
    tiles, packets, arrivals = early[:2], early[2:4], early[4:]
    m.acc, m.do, m.gx = m.dr, m.n2, m.xs
    late = [m.fc2.at[pl.ds(n * total, total)] for n in range(4)]
    m.dq, m.dk, m.dv, m.out = late
    back_packets = [m.fc2.at[pl.ds(4 * total, landed)], m.fc2.at[pl.ds(0, landed)]]
    width = D // 3
    thirds_of = [pl.ds(third * width, width) for third in range(3)]
    full, halves = list(m.full), list(m.half)
    for third in range(3):
        full[FC2 + third], halves[FC2 + third] = m.fc2.at[:, thirds_of[third]], m.half_fc2.at[:, thirds_of[third]]
    grads = {PROJ: full[FC1 + 3], SMALL: m.grad_small}
    for third in range(3):
        grads[QKV + third] = full[FC1 + third]
        grads[FC2 + third] = m.dw_fc2.at[:, thirds_of[third]]
    for b in range(blocks):
        grads[FC1 + b] = m.dw_fc1[b]

    place = Place()
    me = place.row * place.cols + place.col
    table = pltpu.make_async_copy(m.in_table.at[me], m.table, m.local_sems.at[len(units)])
    table.start()
    loads = []
    for n, source in enumerate((m.in_tokens, m.in_cotangent)):
        loads.append(pltpu.make_async_copy(source, tiles[n], m.local_sems.at[len(units) + 1 + n]))
        loads[n].start()
    thirds = []
    for third in range(3):
        for n in range(3):
            source = m.w_qkv.at[:, pl.ds(n * D + third * width, width)]
            target = m.thirds[third].at[:, pl.ds(n * width, width)]
            thirds.append(pltpu.make_async_copy(source, target, m.third_sems.at[third * 3 + n]))
            thirds[-1].start()
    for n in range(2):
        arrivals[n][...] = jnp.zeros((landed, D), BF16)
        m.back_arrivals[n][...] = jnp.zeros((packed, D), BF16)
    heard = greet(place)
    copies = Copies(m.send_sems, m.recv_sems)
    line = Timeline()
    piece, wide = units[PROJ].rows, units[FC2].rows
    pack_small(m, place, piece, wide)
    moves = [Exchange(place, copies, plan, packets[n], arrivals[n], False) for n in range(2)]

    def post(n):
        packets[n][...] = matmul(one_hot(m.table[0:packed, 6:7], cells), tiles[n][...]).astype(BF16)
        moves[n].start()
        line.load(ALONG, 8.0)
        line.load(ACROSS, 5.0)
        line.spend(1.5)

    def receive(n):
        moves[n].wait()
        pick_cells((m.xs, m.gs)[n], m.table, 5, tiles[n], arrivals[n], SLOT)
        line.spend(2.0)

    shards = {SMALL: m.small, PROJ: m.w_proj}
    for third in range(3):
        shards[FC2 + third] = m.w_fc2.at[:, thirds_of[third]]
        shards[QKV + third] = m.thirds[third]
    for b in range(blocks):
        shards[FC1 + b] = m.w_fc1.at[:, pl.ds(b * D, D)]
    gathers = [
        Gather(place, copies, units[n], shards[n], full[n], m.stage[n], m.local_sems.at[n]) for n in range(len(units))
    ]
    outs = {PROJ: [m.g_proj], SMALL: [m.g_small]}
    for third in range(3):
        outs[FC2 + third] = [m.g_fc2.at[:, thirds_of[third]]]
        outs[QKV + third] = [m.g_qkv.at[:, pl.ds(n * D + third * width, width)] for n in range(3)]
    for b in range(blocks):
        outs[FC1 + b] = [m.g_fc1.at[:, pl.ds(b * D, D)]]
    scatters = {}

    def scatter(n):
        scatters[n] = Scatter(place, copies, units[n], grads[n], halves[n], m.buffers[n], m.stage[n], outs[n])
        line.launch(scatters[n])

    line.queue = list(gathers)
    for copy in thirds:
        copy.wait()
    pl.semaphore_wait(pltpu.get_barrier_semaphore(), heard)
    for n in range(2):
        line.launch(line.queue.pop(0))
    table.wait()
    loads[0].wait()
    post(0)
    m.fold[...] = fold_matrix()
    rel = jnp.concatenate([matmul_tn(r[...], m.select[...]).astype(BF16) for r in (m.rel_rows, m.rel_cols)], axis=1)
    m.rel[...] = jnp.concatenate([rel, rel], axis=0)
    key_columns(m, total)

    @pl.loop(0, slots)
    def _(s):
        m.own[slot_rows(s), :] = own_place(m.table[slot_rows(s), :])

    line.spend(4.0)
    line.need_time(12.0)
    receive(0)
    line.need(gathers[SMALL])
    small = units[SMALL]
    line_count = 2 * small.chips * small.row_count
    unpack_small(m, line_count, place.cols * piece, place.cols * wide)
    vec = m.vec

    @pl.loop(0, slots)
    def _(s):
        rows = slot_rows(s)
        hat, _ = normalized(m.xs[rows, :].astype(F32))
        m.n1[rows, :] = (hat * vec[0:1, :] + vec[1:2, :]).astype(BF16)

    line.spend(3.0)
    def pairs_of(s, pairs, function):
        @pl.loop(pairs.start, pairs.stop)
        def _(p):
            function(m, s, p)

    for third in range(3):
        line.need(gathers[QKV + third])
        lanes = pl.ds(third * width, width)
        for n, (target, bias) in enumerate(((m.q, vec[2:3, :]), (m.k, None), (m.v, vec[3:4, :]))):
            out = matmul(m.n1[...], m.full[QKV + third][:, pl.ds(n * width, width)])
            if bias is not None:
                out = out + bias[:, third * width : (third + 1) * width]
            target[:, lanes] = out.astype(BF16)
        line.spend(1.5)
        if third == 0:
            loads[1].wait()
            post(1)
        for s in range(slots):
            pairs_of(s, range(third * PAIRS // 3, (third + 1) * PAIRS // 3), attend)
            line.spend(2.1)
        if third == 1:
            receive(1)
    line.need(gathers[PROJ])

    @pl.loop(0, slots)
    def _(s):
        rows = slot_rows(s)
        r = m.xs[rows, :].astype(F32) + matmul(m.o[rows, :], m.full[PROJ][...]) + vec[4:5, :]
        m.r[rows, :] = r
        hat, _ = normalized(r)
        m.n2[rows, :] = (hat * vec[5:6, :] + vec[6:7, :]).astype(BF16)
        m.acc[rows, :] = r + vec[7:8, :]

    line.spend(4.5)
    for move in moves:
        move.finish()
    line.need(*gathers[FC2 : FC2 + 3])
    size = width
    for b in range(blocks):
        line.need(gathers[FC1 + b])
        for h in range(3):
            lanes, rows = pl.ds(h * size, size), pl.ds(b * D + h * size, size)
            w1, w2 = m.full[FC1 + b][:, lanes], m.fc2[rows, :]
            u = matmul(m.n2[...], w1) + m.b1[0:1, rows]
            half = 0.5 + 0.5 * lax.erf(u * 0.7071067811865476)
            a = (u * half).astype(BF16)
            m.acc[...] += matmul(a, w2)
            m.dw_fc2[rows, :] = matmul_tn(a, m.gs[...]).astype(BF16)
            slope = half + u * jnp.exp(u * u * -0.5) * 0.3989422804014327
            du = (matmul_nt(m.gs[...], w2) * slope).astype(BF16)
            m.db1[:, rows] = jnp.broadcast_to(column_sum(du.astype(F32)), (8, size))
            m.dw_fc1[b][:, lanes] = matmul_tn(m.n2[...], du).astype(BF16)
            term = matmul_nt(du, w1)
            if b == 0 and h == 0:
                m.dn2[...] = term
            else:
                m.dn2[...] += term
        line.spend(5.0)
        scatter(FC1 + b)
    for gather in gathers:
        gather.settle()
    for third in range(3):
        scatter(FC2 + third)

    m.sums[...] = jnp.zeros_like(m.sums)

    @pl.loop(0, slots)
    def _(s):
        rows = slot_rows(s)
        m.out[rows, :] = m.acc[rows, :].astype(BF16)
        hat, rate = normalized(m.r[rows, :])
        dn2, g = m.dn2[rows, :], m.gs[rows, :].astype(F32)
        m.sums[5:6, :] += column_sum(dn2 * hat)
        m.sums[6:7, :] += column_sum(dn2)
        m.sums[7:8, :] += column_sum(g)
        dr = g + norm_back(dn2, vec[5:6, :], hat, rate)
        m.dr[rows, :] = dr
        m.sums[4:5, :] += column_sum(dr.astype(BF16).astype(F32))

    line.spend(3.5)
    db = m.dr[...].astype(BF16)
    grads[PROJ][...] = matmul_tn(m.o[...], db).astype(BF16)
    scatter(PROJ)
    m.do[...] = matmul_nt(db, m.full[PROJ][...]).astype(BF16)
    line.spend(4.0)
    back_packets[0][...] = matmul(one_hot(m.table[0:landed, 7:8], total), m.out[...]).astype(BF16)
    moves = [Exchange(place, copies, plan, back_packets[n], m.back_arrivals[n], True) for n in range(2)]
    moves[0].start()
    line.spend(1.5)

    m.drel[...] = jnp.zeros_like(m.drel)
    dn1 = m.dn2
    for third in range(3):
        for s in range(slots):
            pairs_of(s, range(third * PAIRS // 3, (third + 1) * PAIRS // 3), attend_back)
            line.spend(2.3)
        own = pl.ds(third * width, width)
        for n, d in enumerate((m.dq, m.dk, m.dv)):
            lanes = pl.ds(n * width, width)
            grads[QKV + third][:, lanes] = matmul_tn(m.n1[...], d[:, own]).astype(BF16)
        line.spend(2.2)
        scatter(QKV + third)
        for n, d in enumerate((m.dq, m.dk, m.dv)):
            term = matmul_nt(d[:, own], m.full[QKV + third][:, pl.ds(n * width, width)])
            if third == 0 and n == 0:
                dn1[...] = term
            else:
                dn1[...] += term
            line.spend(0.7)
    drel = m.drel[:HEAD_DIM, :] + m.drel[HEAD_DIM:, :]
    for n in range(2):
        part = drel[:, n * (REL // 2) : (n + 1) * (REL // 2)]
        m.held[0, n] = lax.dot_general(
            m.select[...].astype(F32), part, (((1,), (1,)), ((), ())), preferred_element_type=F32,
            precision=lax.Precision.HIGHEST,
        )
    doubling = Doubling(place, copies, m.held, m.arriving)
    line.launch(doubling)

    for s in range(slots):
        rows = pl.ds(s * SLOT, SLOT)
        hat, rate = normalized(m.xs[rows, :].astype(F32))
        d = dn1[rows, :]
        m.sums[0:1, :] += column_sum(d * hat)
        m.sums[1:2, :] += column_sum(d)
        m.sums[2:3, :] += column_sum(m.dq[rows, :].astype(F32))
        m.sums[3:4, :] += column_sum(m.dv[rows, :].astype(F32))
        m.gx[rows, :] = (m.dr[rows, :] + norm_back(d, vec[0:1, :], hat, rate)).astype(BF16)
        line.spend(1.3)
    split_small(m, line_count, place.cols * piece, place.cols * wide, blocks * D)
    scatter(SMALL)
    back_packets[1][...] = matmul(one_hot(m.table[0:landed, 7:8], total), m.gx[...]).astype(BF16)
    moves[1].start()
    line.spend(2.0)
    stores = []
    results = [m.dk, m.dv]
    for n, source in enumerate((m.out, m.gx)):
        moves[n].wait()
        tile = results[n].at[pl.ds(0, cells)]
        pick_cells(tile, m.table, 8, source, m.back_arrivals[n], 128)
        stores.append(pltpu.make_async_copy(tile, (m.layer_out, m.grad_tokens)[n], m.local_sems.at[n]))
        stores[n].start()
        line.spend(2.0)
    line.finish()
    m.rel_sum[...] = m.held[doubling.last]
    lane_pick = lane_place(512, 512, -place.col * piece)
    lane_pick2 = lane_place(512, 512, -128 - place.col * wide)
    for target, picked in ((m.g_vec, lane_pick), (m.g_b1, lane_pick2)):
        target[...] = jnp.dot(
            m.g_small[...], picked[:, : target.shape[1]].astype(F32),
            preferred_element_type=F32, precision=lax.Precision.HIGHEST,
        )
    for op in [*scatters.values(), doubling]:
        op.settle()
    for move in moves:
        move.finish()
    for store in stores:
        store.wait()


def fold_matrix():
    row = lax.broadcasted_iota(jnp.int32, (REL, 128), 0)
    lane = lax.broadcasted_iota(jnp.int32, (REL, 128), 1)
    half = REL // 2
    inside = jnp.where(row < half, row, row - half)
    target = inside % WIN + jnp.where(row < half, 0, WIN)
    return jnp.where((lane == target) & (inside < CELLS), 1.0, 0.0).astype(BF16)


def body(
    image_tokens, cotangent, content_mask, norm1_gain, norm1_bias, qkv_weight, query_bias, value_bias,
    rel_rows, rel_cols, proj_weight, proj_bias, norm2_gain, norm2_bias, fc1_weight, fc1_bias, fc2_weight, fc2_bias,
):
    images, rows, cols = axis_sizes()
    _, tile_rows, tile_cols, _ = image_tokens.shape
    cells = tile_rows * tile_cols
    plan = plan_windows(rows, cols, tile_rows, tile_cols)
    total, slots, packed, landed = plan["total"], plan["slots"], plan["packed"], plan["landed"]
    piece, wide, ff = qkv_weight.shape[0], fc2_weight.shape[0], fc1_weight.shape[1]
    blocks = ff // D
    line = Unit(piece, D, ROWS)
    part = Unit(wide, D // 3, ROWS if wide % 16 else PLAIN)
    units = [Unit(16, 512, SUM), line, line, line, line, part, part, part] + [line] * blocks

    height = max(total, packed, landed, cells)
    table = np.full((rows * cols, height, 16), -1, np.int32)
    table[:, :total, :5] = plan["where"][:, :, :5]
    for n, name in enumerate(("slot_from", "pack_from", "back_from", "tile_from")):
        table[:, : plan[name].shape[1], 5 + n] = plan[name]
    index = np.arange(WIN)[:, None] - np.arange(WIN)[None, :] + WIN - 1
    span = rel_rows.shape[0]
    select = np.zeros((span, REL // 2), np.float32)
    select[index.reshape(-1), np.arange(CELLS)] = 1
    vectors = [norm1_gain, norm1_bias, query_bias, value_bias, proj_bias, norm2_gain, norm2_bias, fc2_bias]

    def everywhere(value):
        return Item(value, space=pl.ANY)

    def vmem(*shape, kind=BF16):
        return Item(shape, kind)

    inputs = dict(
        in_tokens=everywhere(image_tokens.reshape(cells, D)), in_cotangent=everywhere(cotangent.reshape(cells, D)),
        in_table=everywhere(jnp.asarray(table)), mask=Item(content_mask[0]), vectors=Item(jnp.stack(vectors)), bias=Item(fc1_bias[None]),
        rel_rows=Item(rel_rows), rel_cols=Item(rel_cols), select=Item(jnp.asarray(select, BF16)),
        w_qkv=everywhere(qkv_weight), w_proj=everywhere(proj_weight), w_fc1=everywhere(fc1_weight), w_fc2=everywhere(fc2_weight),
    )
    outputs = dict(
        layer_out=Item((cells, D), BF16, pl.ANY), grad_tokens=Item((cells, D), BF16, pl.ANY),
        g_qkv=vmem(piece, 3 * D, kind=F32), g_proj=vmem(piece, D, kind=F32),
        g_fc1=vmem(piece, ff, kind=F32), g_fc2=vmem(wide, D, kind=F32),
        g_vec=vmem(16, 128, kind=F32), g_b1=vmem(16, round_up(wide, 128), kind=F32), rel_sum=vmem(2, span, HEAD_DIM, kind=F32),
    )
    swaps = (images * rows * cols).bit_length() - 1
    count = sum(u.copies() for u in units) + swaps + 4 * len(plan["pairs"])
    sems = pltpu.SemaphoreType.DMA
    scratch = dict(
        table=vmem(height, 16, kind=jnp.int32), small=vmem(16, 512), thirds=[vmem(piece, D)] * 3, third_sems=Item(pltpu.SemaphoreType.DMA((9,))), rel=vmem(2 * HEAD_DIM, REL), fold=vmem(REL, 128),
        xs=vmem(total, D), gs=vmem(total, D), n1=vmem(total, D), q=vmem(total, D), k=vmem(total, D), v=vmem(total, D),
        key=vmem(total, 128), soft=vmem(slots * PAIRS, 2 * SLOT, SLOT), o=vmem(total, D), n2=vmem(total, D),
        r=vmem(total, D, kind=F32), dr=vmem(total, D, kind=F32), dn2=vmem(total, D, kind=F32), own=vmem(total, REL),
        vec=vmem(16, D, kind=F32), b1=vmem(8, ff, kind=F32), db1=vmem(8, ff, kind=F32), sums=vmem(8, D, kind=F32),
        drel=vmem(2 * HEAD_DIM, REL, kind=F32), held=vmem(swaps + 1, 2, span, HEAD_DIM, kind=F32),
        arriving=vmem(swaps, 2, span, HEAD_DIM, kind=F32), g_small=vmem(16, 512, kind=F32),
        grad_small=vmem(*units[SMALL].full_shape()), back_arrivals=[vmem(packed, D)] * 2,
        full=[vmem(*(u.full_shape() if u is not part else (8, 128))) for u in units],
        half=[vmem(*(u.half_shape() if u is not part else (8, 128))) for u in units],
        fc2=vmem(ff, D), half_fc2=vmem(ff // 2, D),
        stage=[vmem(*(u.stage_shape() if u.mode != PLAIN else (8, 128))) for u in units],
        buffers=[[vmem(*shape) for shape in u.buffer_shapes()] for u in units],
        dw_fc1=[vmem(*line.full_shape())] * blocks, dw_fc2=vmem(ff, D),
        send_sems=Item(sems((count,))), recv_sems=Item(sems((count,))), local_sems=Item(sems((len(units) + 3,))),
    )
    done = run(functools.partial(layer_kernel, plan, units), inputs, outputs, scratch)
    g_vec, g_b1 = done.g_vec[:8, :piece], done.g_b1[0, :wide]
    return (
        done.layer_out.reshape(image_tokens.shape), done.grad_tokens.reshape(image_tokens.shape),
        g_vec[0], g_vec[1], done.g_qkv, g_vec[2], g_vec[3], done.rel_sum[0], done.rel_sum[1],
        done.g_proj, g_vec[4], g_vec[5], g_vec[6], done.g_fc1, g_b1, done.g_fc2, g_vec[7],
    )


def solution(mesh):
    everywhere = ("img", "row", "col")
    tile, vector, matrix = P("img", "row", "col", None), P(everywhere), P(everywhere, None)
    in_specs = (
        tile, tile, P("img", None, None), vector, vector, matrix, vector, vector, P(), P(),
        matrix, vector, vector, vector, matrix, vector, matrix, vector,
    )
    out_specs = (
        tile, tile, vector, vector, matrix, vector, vector, P(), P(),
        matrix, vector, vector, vector, matrix, vector, matrix, vector,
    )
    return jax.shard_map(body, mesh=mesh, in_specs=in_specs, out_specs=out_specs, check_vma=False)
```
